32 devices in a mesh: dp: 8 (over z, x), seq: 4 (over y, core).
Axes of the slice: x: 2, y: 2, z: 4, core: 2. Of those that a mesh axis runs over, the one named last changes fastest.
Arguments:
- tokens: bfloat16 [24, 324, 512], P('dp', 'seq'), may hold values from -6 to 6
- res_class: int32 [24], P('dp'), may hold values from 0 to 2, as said below
- skip_mask: int32 [24], P('dp'), may hold values 0 or 1
- w_in: bfloat16 [512, 3072], replicated, may hold values from -0.25 to 0.25
- w_out: bfloat16 [1536, 512], replicated, may hold values from -0.15625 to 0.15625
- spatial: bfloat16 [324, 324], P('seq'), may hold values from -0.3125 to 0.3125
- spatial_bias: float32 [324], P('seq'), may hold values from 0.1 to 1.9
- gain_one: float32 [512], replicated, may hold values from 0.5 to 1.5
- shift_one: float32 [512], replicated, may hold values from -1.75 to 1.75
- gain_two: float32 [1536], replicated, may hold values from 0.5 to 1.5
- shift_two: float32 [1536], replicated, may hold values from -1.75 to 1.75
- cotangent: bfloat16 [24, 324, 512], P('dp', 'seq'), may hold values from -6 to 6
Outputs:
- output: bfloat16 [24, 324, 512], P('dp', 'seq')
- grad_tokens: bfloat16 [24, 324, 512], P('dp', 'seq')
- grad_w_in: float32 [512, 3072], replicated
- grad_w_out: float32 [1536, 512], replicated
- grad_spatial: float32 [324, 324], P('seq')
- grad_bias: float32 [324], P('seq')
- grad_gain_one: float32 [512], replicated
- grad_shift_one: float32 [512], replicated
- grad_gain_two: float32 [1536], replicated
- grad_shift_two: float32 [1536], replicated
The draws below stay inside these ranges and needn't reach their ends.
Inputs may be any that keep to these rules, and one draw needn't show every extreme that they name: `res_class`: 0, 1, 2 stand for 100, 196 and 324 patches; the images of every index of dp include at least one of class 2.
All inputs are finite; a program needn't handle non-finite values. No bound on the sum of `skip_mask` on one device may be relied on, other than what follows from the above.
Results may differ from the reference program's by a relative error of at most 0.011.
Values may be sent and summed in bfloat16 or wider, within the bound.
No kernel may reach another device: no remote copies, remote signals or barrier semaphores. Data moves between devices by JAX's collectives and lax.ppermute only.
A program may use at most 128 MiB of HBM per device.

```python
import jax
import jax.numpy as jnp
from jax import lax

D = 512
HID = 3072
GATE = 1536
PATCHES = 324
SMALL_P = 100
MID_P = 196
SAMP_DEV = 3
SAMPLES = 24
N_DP = 8


def draw_res_class(key, part):
    key = jax.random.fold_in(key, 11)
    key_classes, key_chosen = jax.random.split(key)
    classes = jax.random.randint(key_classes, (N_DP, SAMP_DEV), 0, 3)
    chosen = jax.random.randint(key_chosen, (N_DP, 1), 0, SAMP_DEV)
    slots = jnp.arange(SAMP_DEV)[None, :]
    return jnp.where(slots == chosen, 2, classes).reshape(-1).astype(jnp.int32)


def with_ends(values, own_key, low, top_value):
    index_at = [jax.random.randint(jax.random.fold_in(own_key, axis), (), 0, length) for axis, length in enumerate(values.shape)]
    main_axis = values.shape.index(max(values.shape))
    beside = index_at[:main_axis] + [(index_at[main_axis] + 1) % values.shape[main_axis]] + index_at[main_axis + 1:]
    return values.at[tuple(index_at)].set(low).at[tuple(beside)].set(top_value)


def steps_of(stream_key, extent, pieces, least, top_value):
    loudness, own = 1.0, jax.random.fold_in(stream_key, 6)
    for axis_at, shards_of in pieces:
        steps = jnp.exp(jax.random.uniform(jax.random.fold_in(own, axis_at), (shards_of,), jnp.float32, least / len(pieces), top_value / len(pieces)))
        loudness = loudness * jnp.repeat(steps, extent[axis_at] // shards_of).reshape([-1 if axis == axis_at else 1 for axis in range(len(extent))])
    return loudness


def noise(own_key, shape, deviation, reach, cuts=(), kind=jnp.bfloat16):
    values = deviation * jax.random.normal(own_key, shape, jnp.float32)
    if cuts:
        values = values * steps_of(own_key, shape, cuts, -0.22, 0.18)
    return jnp.clip(values, -reach, reach).astype(kind)


def setup_inputs(seed: int = 0) -> dict:
    splits = jax.random.split(jax.random.key(seed), 13)
    return {
        "tokens": noise(splits[0], (SAMPLES, PATCHES, D), 1.0, 6.0, ((0, 8), (1, 4))),
        "res_class": draw_res_class(jax.random.fold_in(splits[12], 71), 0),
        "skip_mask": with_ends((jax.random.randint(splits[2], (SAMPLES,), 0, 10) < 9).astype(jnp.int32), jax.random.fold_in(splits[2], 1), 0, 1),
        "w_in": noise(splits[3], (D, HID), D ** -0.5, 0.25),
        "w_out": noise(splits[4], (GATE, D), GATE ** -0.5, 0.15625),
        "spatial": noise(splits[5], (PATCHES, PATCHES), PATCHES ** -0.5, 0.3125, ((0, 4),)),
        "spatial_bias": jnp.clip(1.0 + 0.18 * jax.random.normal(splits[6], (PATCHES,), jnp.float32), 0.1, 1.9),
        "gain_one": jnp.clip(1.0 + 0.1 * jax.random.normal(splits[7], (D,), jnp.float32), 0.5, 1.5),
        "shift_one": noise(splits[8], (D,), 0.3, 1.75, (), jnp.float32),
        "gain_two": jnp.clip(1.0 + 0.1 * jax.random.normal(splits[9], (GATE,), jnp.float32), 0.5, 1.5),
        "shift_two": noise(splits[10], (GATE,), 0.3, 1.75, (), jnp.float32),
        "cotangent": noise(splits[11], (SAMPLES, PATCHES, D), 1.0, 6.0, ((0, 8), (1, 4))),
    }


EPSILON = 1e-05
SURVIVAL = 0.9
HIGHEST = lax.Precision.HIGHEST

@jax.custom_vjp
def low(v):
    return lax.optimization_barrier(v.astype(jnp.bfloat16)).astype(jnp.float32)

@jax.custom_vjp
def low_back(v):
    return v

def low_keep(v):
    return (low(v), None)

def low_pass(kept, grad):
    return (grad,)

def back_keep(v):
    return (v, None)

def back_low(kept, grad):
    return (low(grad),)
low.defvjp(low_keep, low_pass)
low_back.defvjp(back_keep, back_low)

def layer_norm(values, gain_vector, shift_vector):
    center = values - lax.optimization_barrier(jnp.mean(values, axis=-1, keepdims=True))
    spread = lax.optimization_barrier(jnp.mean(center * center, axis=-1, keepdims=True))
    return center * lax.rsqrt(spread + EPSILON) * gain_vector + shift_vector

def forward(inputs, params, valid_rows, branch_scale):
    w_in, w_out, spatial, spatial_bias, gain_one, shift_one, gain_two, shift_two = params
    half_width = w_out.shape[0]
    normed = low(layer_norm(inputs, gain_one, shift_one))
    hidden = low_back(jnp.einsum('spd,dh->sph', normed, w_in, precision=HIGHEST))
    active = jax.nn.gelu(hidden)
    gate_u = active[..., :half_width]
    gate_v = active[..., half_width:]
    mixed = low(layer_norm(gate_v, gain_two, shift_two)) * valid_rows[..., None]
    spatial_out = low_back(jnp.einsum('pq,sqc->spc', spatial, mixed, precision=HIGHEST) + spatial_bias[None, :, None])
    product = low(gate_u * spatial_out)
    branch = low_back(jnp.einsum('spc,cd->spd', product, w_out, precision=HIGHEST))
    return inputs + branch_scale[..., None] * branch

def reference(tokens, res_class, skip_mask, w_in, w_out, spatial, spatial_bias, gain_one, shift_one, gain_two, shift_two, cotangent):
    parameters = tuple((a.astype(jnp.float32) for a in (w_in, w_out, spatial, spatial_bias, gain_one, shift_one, gain_two, shift_two)))
    patch_counts = jnp.where(res_class == 0, SMALL_P, jnp.where(res_class == 1, MID_P, PATCHES))
    valid_rows = (jnp.arange(PATCHES)[None, :] < patch_counts[:, None]).astype(jnp.float32)
    branch_scale = valid_rows * skip_mask[:, None].astype(jnp.float32) / SURVIVAL
    group_count = tokens.shape[0] // 8

    def grouped(array):
        return array.reshape((group_count, 8) + array.shape[1:])

    def advance(totals, item):
        token_group, grad_group, valid_group, scale_group = item

        def run(inputs, params):
            return forward(inputs, params, valid_group, scale_group)
        result, pullback = jax.vjp(run, token_group.astype(jnp.float32), parameters)
        grad_inputs, grad_params = pullback(grad_group.astype(jnp.float32))
        totals = jax.tree.map(lambda a, b: a + b, totals, grad_params)
        return (totals, (result.astype(jnp.bfloat16), grad_inputs.astype(jnp.bfloat16)))
    initial = jax.tree.map(jnp.zeros_like, parameters)
    totals, (results, grads) = lax.scan(advance, initial, (grouped(tokens), grouped(cotangent), grouped(valid_rows), grouped(branch_scale)))
    return (results.reshape(tokens.shape), grads.reshape(tokens.shape), totals[0], totals[1], totals[2], totals[3], totals[4], totals[5], totals[6], totals[7])
```

```python
import functools

import jax
import jax.numpy as jnp
from jax import lax
from jax.experimental import pallas as pl
from jax.experimental.pallas import tpu as pltpu
from jax.sharding import PartitionSpec as P

PATCHES = 324
SMALL_P = 100
MID_P = 196

EPSILON = 1e-05
SURVIVAL = 0.9

BF = jnp.bfloat16
F32 = jnp.float32
CHUNK = 16
VM = pl.BlockSpec(memory_space=pltpu.VMEM)
SM = pl.BlockSpec(memory_space=pltpu.SMEM)
HB = pl.BlockSpec(memory_space=pl.ANY)


def round_up(size, multiple):
    return -(-size // multiple) * multiple


def dot(a, b, ca, cb):
    return lax.dot_general(a, b, (((ca,), (cb,)), ((), ())), preferred_element_type=F32)


def iota(shape, axis):
    return lax.broadcasted_iota(jnp.int32, shape, axis)


def rows_at(start, size, multiple):
    return pl.ds(pl.multiple_of(start, multiple), size)


def call(body, outs, ins, scratch=(), specs=None, out_specs=None, flops=0, nbytes=0, **more):
    return pl.pallas_call(
        body,
        out_shape=outs,
        in_specs=specs if specs is not None else [VM] * len(ins),
        out_specs=out_specs if out_specs is not None else [VM] * len(outs),
        scratch_shapes=list(scratch),
        compiler_params=pltpu.CompilerParams(vmem_limit_bytes=48 * 2**20),
        cost_estimate=pl.CostEstimate(flops=flops, bytes_accessed=nbytes, transcendentals=0),
        **more,
    )(*ins)


def shape_of(shape, dtype):
    return jax.ShapeDtypeStruct(shape, dtype)


def project_body(first, pad, *refs):
    if first:
        tok_a, tok_b, g1, s1, wu, wv, normed, gu, dgu, v, dgv, st, xs, hid, tile = refs
    else:
        tok_a, tok_b, g1, s1, wu, wv, n_in, st_in, normed, gu, dgu, v, dgv, st, xs, hid, tile = refs
    samples, rows, width = tok_a.shape
    half = wu.shape[1]
    base = 0 if first else 2 * pad
    tile[...] = jnp.zeros_like(tile)
    xs[rows // 8 * 8 :, :] = jnp.zeros((pad - rows // 8 * 8, width), F32)
    gain, shift = g1[...], s1[...]
    for i in range(samples):
        for b, tok in enumerate((tok_a, tok_b)):
            xs[0:rows, :] = tok[i].astype(F32)

            def norm_chunk(c, carry, i=i, b=b):
                x = xs[rows_at(c * CHUNK, CHUNK, CHUNK), :]
                center = x - jnp.mean(x, axis=-1, keepdims=True)
                inverse = lax.rsqrt(jnp.mean(center * center, axis=-1, keepdims=True) + EPSILON)
                out = center * inverse * gain + shift
                normed[i, rows_at(base + b * pad + c * CHUNK, CHUNK, CHUNK), :] = out.astype(BF)
                return carry

            lax.fori_loop(0, pad // CHUNK, norm_chunk, 0, unroll=3)
        both = normed[i, base : base + 2 * pad, :]
        hid[i, :, 0:half] = dot(both, wu[...], 1, 0)
        hid[i, :, half:] = dot(both, wv[...], 1, 0)
        if not first:
            normed[i, 0:base, :] = n_in[i]
    c0 = 0.7978845608028654
    c1 = 0.7978845608028654 * 0.044715

    def gelu_pair(h):
        a = (c1 * h) * h
        s = 0.5 + 0.5 * jnp.tanh(h * (c0 + a))
        g = h * s
        return g, s + (2.0 * g) * (1.0 - s) * (c0 + 3.0 * a)

    lane = iota((CHUNK, 128), 1)
    for i in range(samples):
        for b in range(2):
            blk = i * 4 + b + (0 if first else 2)

            def gelu_chunk(c, carry, i=i, b=b, blk=blk):
                at = rows_at(b * pad + c * CHUNK, CHUNK, CHUNK)
                g, d = gelu_pair(hid[i, at, 0:half])
                gu[i, at, :] = g.astype(BF)
                dgu[i, at, :] = d.astype(BF)
                g, d = gelu_pair(hid[i, at, half:])
                v[i, at, :] = g
                dgv[i, at, :] = d.astype(BF)
                mean = jnp.mean(g, axis=-1, keepdims=True)
                center = g - mean
                square = jnp.sum(center * center, axis=-1, keepdims=True)
                here = rows_at(c * CHUNK, CHUNK, CHUNK)
                old = tile[here, :]
                tile[here, :] = jnp.where(
                    lane == 2 * blk, mean, jnp.where(lane == 2 * blk + 1, square, old)
                )
                return carry

            lax.fori_loop(0, pad // CHUNK, gelu_chunk, 0, unroll=2)
    flipped = jnp.transpose(tile[...])[0 : st.shape[0], :]
    st[...] = flipped if first else flipped + st_in[...]


def project(first, pad, tok_a, tok_b, g1, s1, wu, wv, extra):
    samples, rows, width = tok_a.shape
    half = wu.shape[1]
    n_rows = 2 * pad if first else 4 * pad
    st_rows = round_up(samples * 8, 8)
    outs = [
        shape_of((samples, n_rows, width), BF),
        shape_of((samples, 2 * pad, half), BF),
        shape_of((samples, 2 * pad, half), BF),
        shape_of((samples, 2 * pad, half), F32),
        shape_of((samples, 2 * pad, half), BF),
        shape_of((st_rows, 128), F32),
    ]
    scratch = [
        pltpu.VMEM((pad, width), F32),
        pltpu.VMEM((samples, 2 * pad, 2 * half), F32),
        pltpu.VMEM((128, 128), F32),
    ]
    flops = 2 * samples * 2 * pad * width * 2 * half
    return call(
        functools.partial(project_body, first, pad),
        outs,
        [tok_a, tok_b, g1, s1, wu, wv, *extra],
        scratch,
        flops=flops,
        nbytes=6_000_000,
        name="project",
    )


def position_map(seq, rows, pad, n, columns):
    a = iota((columns, n * pad), 0)
    j = iota((columns, n * pad), 1)
    r = jnp.zeros_like(j)
    for k in range(1, n):
        r = r + (j >= k * pad).astype(jnp.int32)
    q = j - r * pad
    hit = (a == (r ^ seq) * rows + q) & (q < rows)
    hit = hit | ((a == n * rows) & (j == pad - 1)) | ((a == n * rows + 1) & (j == pad - 2))
    return jnp.where(hit, 1.0, 0.0).astype(BF)


def spatial_body(
    n, pad, meta, va, vb, gua, gub, dgua, dgub, normed, c0, c1, c2, c3, wo, g2, s2, t0, t1, t2, t3,
    mixed, prod, gs, ghu, gmix, cols, st, o_keep, o_send, u_keep, u_send,
    pm, sp, spt, gb, so, gp, tile, ow, uw,
):
    samples, rows, half = c0.shape[0] - 1, c0.shape[1], wo.shape[0]
    seq, dp = meta[0], meta[1]
    cots = (c0, c1, c2, c3)
    columns = pm.shape[0]
    pm[...] = position_map(seq, rows, pad, n, columns)
    low = rows // 16 * 16
    for r in range(n):
        sp[r * pad + low : (r + 1) * pad, :] = jnp.zeros((pad - low, n * pad), BF)
        sp[r * pad : r * pad + rows, :] = dot(cots[r][samples, :, 0:columns], pm[...], 1, 0).astype(BF)
    spt[...] = jnp.transpose(sp[...].astype(F32)).astype(BF)
    whole = half * n
    stats = (t0, t1, t2, t3)
    tile[...] = jnp.zeros_like(tile)
    for i in range(samples):
        for r in range(n):
            means = [stats[k][pl.ds(2 * (i * n + (r ^ k)), 1), :] for k in range(n)]
            squares = [stats[k][pl.ds(2 * (i * n + (r ^ k)) + 1, 1), :] for k in range(n)]
            mean = ((means[0] + means[1]) + (means[2] + means[3])) / n
            spread = (squares[0] + squares[1]) + (squares[2] + squares[3])
            for k in range(n):
                spread = spread + half * (means[k] - mean) * (means[k] - mean)
            blk = 2 * (i * n + r)
            tile[blk : blk + 1, :] = mean
            tile[blk + 1 : blk + 2, :] = lax.rsqrt(spread / whole + EPSILON)
    cols[...] = jnp.transpose(tile[...])
    row = iota((CHUNK, 1), 0)
    gain, shift = g2[...], s2[...]

    def position(c, r):
        p = c * CHUNK + row
        return p, (seq ^ r) * rows + p

    for i in range(samples):
        count = meta[2 + i]
        for r in range(n):
            v = (va, vb)[r // 2]
            blk = 2 * (i * n + r)

            def mix_chunk(c, carry, i=i, r=r, v=v, blk=blk, count=count):
                p, where = position(c, r)
                valid = jnp.where((p < rows) & (where < count), 1.0, 0.0)
                here = rows_at(c * CHUNK, CHUNK, CHUNK)
                mean, inverse = cols[here, blk : blk + 1], cols[here, blk + 1 : blk + 2]
                x = v[i, rows_at((r % 2) * pad + c * CHUNK, CHUNK, CHUNK), :]
                out = ((x - mean) * inverse * gain + shift) * valid
                if r == 0:
                    out = jnp.where(p >= pad - 2, 1.0, out)
                mixed[i, rows_at(r * pad + c * CHUNK, CHUNK, CHUNK), :] = out.astype(BF)
                return carry

            lax.fori_loop(0, pad // CHUNK, mix_chunk, 0, unroll=3)
            p = iota((rows, 1), 0)
            keep = jnp.where((seq ^ r) * rows + p < count, meta[2 + samples + i], 0).astype(F32)
            scale = keep / SURVIVAL
            gb[i, r * pad + low : (r + 1) * pad, :] = jnp.zeros((pad - low, gb.shape[2]), BF)
            gb[i, r * pad : r * pad + rows, :] = (cots[r][i].astype(F32) * scale).astype(BF)
        so[i] = dot(sp[...], mixed[i], 1, 0)
        gp[i] = dot(gb[i], wo[...], 1, 1)
    for i in range(samples):
        for r in range(n):
            gu, dgu = (gua, gub)[r // 2], (dgua, dgub)[r // 2]

            def gate_chunk(c, carry, i=i, r=r, gu=gu, dgu=dgu):
                src = rows_at((r % 2) * pad + c * CHUNK, CHUNK, CHUNK)
                at = rows_at(r * pad + c * CHUNK, CHUNK, CHUNK)
                g = gu[i, src, :].astype(F32)
                s, q = so[i, at, :], gp[i, at, :]
                prod[i, at, :] = (g * s).astype(BF)
                gs[i, at, :] = (q * g).astype(BF)
                ghu[i, at, :] = (q * s * dgu[i, src, :].astype(F32)).astype(BF)
                return carry

            lax.fori_loop(0, pad // CHUNK, gate_chunk, 0, unroll=3)
        so[i] = dot(spt[...], gs[i], 1, 0)
    total_o = dot(prod[0], gb[0], 0, 0)
    total_u = dot(normed[0], ghu[0], 0, 0)
    for i in range(1, samples):
        total_o = total_o + dot(prod[i], gb[i], 0, 0)
        total_u = total_u + dot(normed[i], ghu[i], 0, 0)
    ow[...] = total_o
    uw[...] = total_u
    store_shards(dp, ow, o_keep, o_send)
    store_shards(dp, uw, u_keep, u_send)
    lane = iota((CHUNK, 128), 1)
    tile[...] = jnp.zeros_like(tile)
    for i in range(samples):
        count = meta[2 + i]
        for r in range(n):
            v = (va, vb)[r // 2]
            blk = 2 * (i * n + r)

            def back_chunk(c, carry, i=i, r=r, v=v, blk=blk, count=count):
                p, where = position(c, r)
                valid = jnp.where((p < rows) & (where < count), 1.0, 0.0)
                here = rows_at(c * CHUNK, CHUNK, CHUNK)
                at = rows_at(r * pad + c * CHUNK, CHUNK, CHUNK)
                mean, inverse = cols[here, blk : blk + 1], cols[here, blk + 1 : blk + 2]
                x = v[i, rows_at((r % 2) * pad + c * CHUNK, CHUNK, CHUNK), :]
                g = so[i, at, :] * valid
                gmix[i, at, :] = g
                t = g * gain
                first = jnp.sum(t, axis=-1, keepdims=True)
                second = jnp.sum(t * ((x - mean) * inverse), axis=-1, keepdims=True)
                tile[here, :] = jnp.where(
                    lane == blk, first, jnp.where(lane == blk + 1, second, tile[here, :])
                )
                return carry

            lax.fori_loop(0, pad // CHUNK, back_chunk, 0, unroll=3)
    st[...] = jnp.transpose(tile[...])[0 : st.shape[0], :]


def store_shards(dp, whole, keep, send):
    size = keep.shape[1]
    for e in range(2):
        here = whole[rows_at(((dp ^ (2 * e)) & 3) * size, size, 16), :]
        keep[e] = here.astype(BF)
        here = whole[rows_at(((dp ^ (2 * e + 1)) & 3) * size, size, 16), :]
        send[e] = here.astype(BF)


def branch_body(n, pad, meta, prod, wo, gs, mixed, keep, send, pm):
    samples = prod.shape[0]
    rows = keep.shape[2]
    pm[...] = position_map(meta[0], rows, pad, n, pm.shape[0])
    total = dot(gs[0], mixed[0], 1, 1)
    for i in range(1, samples):
        total = total + dot(gs[i], mixed[i], 1, 1)
    placed = dot(total.astype(BF), pm[...], 1, 1)
    for r in range(n):
        out = (keep, send)[r % 2]
        out[r // 2, samples, :, 0 : pm.shape[0]] = placed[r * pad : r * pad + rows, :].astype(BF)
        out[r // 2, samples, :, pm.shape[0] :] = jnp.zeros((rows, out.shape[3] - pm.shape[0]), BF)
    for i in range(samples):
        full = dot(prod[i], wo[...], 1, 0)
        for r in range(n):
            out = (keep, send)[r % 2]
            out[r // 2, i] = full[r * pad : r * pad + rows, :].astype(BF)


def back_body(
    n, pad, meta, gmix, va, vb, dgva, dgvb, cols, t0, t1, t2, t3, g2, normed, ghu, wu, wv,
    v_keep, v_send, keep, send, small,
    tile, col, ghv, vw, acc,
):
    samples, rows, half = gmix.shape[0], keep.shape[2], gmix.shape[2]
    dp = meta[1]
    stats = (t0, t1, t2, t3)
    tile[...] = jnp.zeros_like(tile)
    for i in range(samples):
        for r in range(n):
            blk = 2 * (i * n + r)
            for j in range(2):
                part = [stats[k][pl.ds(2 * (i * n + (r ^ k)) + j, 1), :] for k in range(n)]
                tile[blk + j : blk + j + 1, :] = ((part[0] + part[1]) + (part[2] + part[3])) / (
                    half * n
                )
    col[...] = jnp.transpose(tile[...])
    gain = g2[...]
    acc[...] = jnp.zeros_like(acc)
    for i in range(samples):
        for r in range(n):
            v, dgv = (va, vb)[r // 2], (dgva, dgvb)[r // 2]
            blk = 2 * (i * n + r)

            def back_chunk(c, carry, i=i, r=r, v=v, dgv=dgv, blk=blk):
                here = rows_at(c * CHUNK, CHUNK, CHUNK)
                at = rows_at(r * pad + c * CHUNK, CHUNK, CHUNK)
                src = rows_at((r % 2) * pad + c * CHUNK, CHUNK, CHUNK)
                mean, inverse = cols[here, blk : blk + 1], cols[here, blk + 1 : blk + 2]
                first, second = col[here, blk : blk + 1], col[here, blk + 1 : blk + 2]
                standard = (v[i, src, :] - mean) * inverse
                g = gmix[i, at, :]
                grad = inverse * (g * gain - first - standard * second)
                ghv[i, at, :] = (grad * dgv[i, src, :].astype(F32)).astype(BF)
                acc[0] += g * standard
                acc[1] += g
                return carry

            lax.fori_loop(0, pad // CHUNK, back_chunk, 0, unroll=3)
    small[...] = jnp.zeros_like(small)
    small[0:1, :] = jnp.sum(acc[0], axis=0, keepdims=True)
    small[1:2, :] = jnp.sum(acc[1], axis=0, keepdims=True)
    total = dot(normed[0], ghv[0], 0, 0)
    for i in range(1, samples):
        total = total + dot(normed[i], ghv[i], 0, 0)
    vw[...] = total
    store_shards(dp, vw, v_keep, v_send)
    for i in range(samples):
        full = dot(ghu[i], wu[...], 1, 1) + dot(ghv[i], wv[...], 1, 1)
        for r in range(n):
            out = (keep, send)[r % 2]
            out[r // 2, i] = full[r * pad : r * pad + rows, :].astype(BF)


def tokens_body(tok, cot, a, b, ea, eb, g1, small, grad_tokens, extra):
    samples, rows, width = tok.shape
    half = small.shape[1]
    gain = g1[...]
    extra[...] = jnp.zeros_like(extra)
    extra[0:rows, :] = (ea[...].astype(F32) + eb[...].astype(F32)).astype(BF)
    sums = jnp.zeros((1, width), F32)
    shifts = jnp.zeros((1, width), F32)
    for i in range(samples):
        x = tok[i].astype(F32)
        center = x - jnp.mean(x, axis=-1, keepdims=True)
        inverse = lax.rsqrt(jnp.mean(center * center, axis=-1, keepdims=True) + EPSILON)
        standard = center * inverse
        g = a[i].astype(F32) + b[i].astype(F32)
        t = g * gain
        first = jnp.mean(t, axis=-1, keepdims=True)
        second = jnp.mean(t * standard, axis=-1, keepdims=True)
        grad = cot[i].astype(F32) + inverse * (t - first - standard * second)
        grad_tokens[i] = grad.astype(BF)
        sums = sums + jnp.sum(g * standard, axis=0, keepdims=True)
        shifts = shifts + jnp.sum(g, axis=0, keepdims=True)
    row = iota((16, width), 0)
    low = rows // 16 * 16
    tail = jnp.where(row == 8, sums, jnp.where(row == 9, shifts, 0.0))
    two = jnp.concatenate(
        [small[0:2, :], jnp.zeros((2, width - half), F32)], axis=1
    )
    tail = jnp.where(row == 10, two[0:1, :], jnp.where(row == 11, two[1:2, :], tail))
    extra[low : low + 16, :] = (extra[low : low + 16, :].astype(F32) + tail).astype(BF)


def sources(meta):
    seq, shard = meta[0], meta[1] & 3
    out = []
    for flip in (0, 1):
        s = seq ^ flip
        core = s & 1
        out += [
            (shard, s),
            (shard ^ (1 - core), s ^ (2 * core)),
            (shard ^ core, s ^ (2 * (1 - core))),
            (shard ^ 1, s ^ 2),
        ]
    return out


def place_body(by_column, offset, has_base, meta, *refs):
    pieces = refs[:8]
    out, wide, sems = refs[8 + has_base :]
    size, width = pieces[0].shape[1:]
    copies = []
    for k, (shard, seq) in enumerate(sources(meta)):
        for e in range(2):
            slot = 2 * k + e
            wide[slot] = pieces[k][e].astype(F32)
            at = shard ^ (2 * e)
            if by_column:
                dst = out.at[
                    rows_at(at * size, size, 16),
                    rows_at(offset + seq * width, width, 128),
                ]
            else:
                dst = out.at[rows_at((seq * 4 + at) * size, size, 16), :]
            copy = pltpu.make_async_copy(wide.at[slot], dst, sems.at[slot])
            copy.start()
            copies.append(copy)
    for copy in copies:
        copy.wait()


def place(meta, pieces, out_shape, by_column, offset=0, base=None):
    size, width = pieces[0].shape[1:]
    ins = [meta, *pieces] + ([base] if base is not None else [])
    return call(
        functools.partial(place_body, by_column, offset, int(base is not None)),
        [shape_of(out_shape, F32)],
        ins,
        [pltpu.VMEM((16, size, width), F32), pltpu.SemaphoreType.DMA((16,))],
        specs=[SM] + [VM] * 8 + ([HB] if base is not None else []),
        out_specs=[HB],
        input_output_aliases={9: 0} if base is not None else {},
        nbytes=10_000_000,
        name="place",
    )[0]


def solution(mesh):
    n, m = mesh.shape["seq"], mesh.shape["dp"]

    def over_seq(x, flip):
        return lax.ppermute(x, "seq", [(i, i ^ flip) for i in range(n)])

    def over_dp(x, flip):
        return lax.ppermute(x, "dp", [(i, i ^ flip) for i in range(m)])

    def mixed_axes(x, core_of_x):
        pairs = []
        for d in range(m):
            for s in range(n):
                other = (d ^ 1, s) if s & 1 == core_of_x else (d, s ^ 2)
                pairs.append((d * n + s, other[0] * n + other[1]))
        return lax.ppermute(x, ("dp", "seq"), pairs)

    def add(a, b):
        return (a.astype(F32) + b.astype(F32)).astype(BF)

    def reduce_gather(keep, send):
        got = over_dp(send, 1)
        mine = add(keep[0], got[0])
        other = add(keep[1], got[1])
        mine = add(mine, over_dp(other, 2))
        flip = 4
        while flip < m:
            mine = add(mine, over_dp(mine, flip))
            flip *= 2
        pair = jnp.stack([mine, over_dp(mine, 2)])
        first = mixed_axes(pair, 0)
        second = mixed_axes(pair, 1)
        third = mixed_axes(first, 1)
        own = [pair, first, second, third]
        return own + [over_seq(x, 1) for x in own]

    def shards(
        tokens,
        res_class,
        skip_mask,
        w_in,
        w_out,
        spatial,
        spatial_bias,
        gain_one,
        shift_one,
        gain_two,
        shift_two,
        cotangent,
    ):
        samples, rows, width = tokens.shape
        gate = w_out.shape[0]
        half = gate // n
        pad = round_up(rows + 2, 16)
        full = n * pad
        columns = round_up(n * rows + 2, 128)
        seq, dp = lax.axis_index("seq"), lax.axis_index("dp")
        counts = jnp.where(res_class == 0, SMALL_P, jnp.where(res_class == 1, MID_P, PATCHES))
        meta = jnp.concatenate([seq[None], dp[None], counts, skip_mask]).astype(jnp.int32)

        t0 = tokens
        t1 = over_seq(t0, 1)
        t2 = over_seq(t0, 2)
        t3 = over_seq(t2, 1)
        high = lax.reduce_precision(spatial_bias, 8, 7)
        side = jnp.stack([high, spatial_bias - high], axis=1).astype(BF)
        packed = jnp.concatenate([spatial, side], axis=1)
        packed = jnp.pad(packed, ((0, 0), (0, width - packed.shape[1])))
        c0 = jnp.concatenate([cotangent, packed[None]])
        c1 = over_seq(c0, 1)
        c2 = over_seq(c0, 2)
        c3 = over_seq(c2, 1)

        wu = lax.dynamic_slice(w_in, (0, seq * half), (width, half))
        wv = lax.dynamic_slice(w_in, (0, gate + seq * half), (width, half))
        wo = lax.dynamic_slice(w_out, (seq * half, 0), (half, width))
        g2 = lax.dynamic_slice(gain_two, (seq * half,), (half,))[None]
        s2 = lax.dynamic_slice(shift_two, (seq * half,), (half,))[None]
        g1, s1 = gain_one[None], shift_one[None]

        na, gua, dgua, va, dgva, sa = project(True, pad, t0, t1, g1, s1, wu, wv, ())
        normed, gub, dgub, vb, dgvb, st = project(False, pad, t2, t3, g1, s1, wu, wv, (na, sa))
        stats = [st] + [over_seq(st, k) for k in range(1, n)]

        big = shape_of((samples, full, half), BF)
        square = round_up(samples * 2 * n, 8)
        o_shape = shape_of((2, half // 4, width), BF)
        u_shape = shape_of((2, width // 4, half), BF)
        outs = [
            big, big, big, big,
            shape_of((samples, full, half), F32),
            shape_of((128, 128), F32),
            shape_of((square, 128), F32),
            o_shape, o_shape, u_shape, u_shape,
        ]
        scratch = [
            pltpu.VMEM((columns, full), BF),
            pltpu.VMEM((full, full), BF),
            pltpu.VMEM((full, full), BF),
            pltpu.VMEM((samples, full, width), BF),
            pltpu.VMEM((samples, full, half), F32),
            pltpu.VMEM((samples, full, half), F32),
            pltpu.VMEM((128, 128), F32),
            pltpu.VMEM((half, width), F32),
            pltpu.VMEM((width, half), F32),
        ]
        ins = [meta, va, vb, gua, gub, dgua, dgub, normed, c0, c1, c2, c3, wo, g2, s2, *stats]
        mixed, prod, gs, ghu, gmix, cols, st2, o_keep, o_send, u_keep, u_send = call(
            functools.partial(spatial_body, n, pad),
            outs,
            ins,
            scratch,
            specs=[SM] + [VM] * (len(ins) - 1),
            flops=3_000_000_000,
            nbytes=12_000_000,
            name="spatial",
        )
        o_pieces = reduce_gather(o_keep, o_send)
        u_pieces = reduce_gather(u_keep, u_send)
        stats = [st2] + [over_seq(st2, k) for k in range(1, n)]

        branch = shape_of((n // 2, samples + 1, rows, width), BF)
        b_keep, b_send = call(
            functools.partial(branch_body, n, pad),
            [branch, branch],
            [meta, prod, wo, gs, mixed],
            [pltpu.VMEM((columns, full), BF)],
            specs=[SM] + [VM] * 4,
            flops=1_000_000_000,
            nbytes=5_000_000,
            name="branch",
        )
        rest = shape_of((n // 2, samples, rows, width), BF)
        ins = [meta, gmix, va, vb, dgva, dgvb, cols, *stats, g2, normed, ghu, wu, wv]
        v_keep, v_send, n_keep, n_send, small = call(
            functools.partial(back_body, n, pad),
            [u_shape, u_shape, rest, rest, shape_of((8, half), F32)],
            ins,
            [
                pltpu.VMEM((128, 128), F32),
                pltpu.VMEM((128, 128), F32),
                pltpu.VMEM((samples, full, half), BF),
                pltpu.VMEM((width, half), F32),
                pltpu.VMEM((2, CHUNK, half), F32),
            ],
            specs=[SM] + [VM] * (len(ins) - 1),
            flops=2_000_000_000,
            nbytes=10_000_000,
            name="back",
        )
        v_pieces = reduce_gather(v_keep, v_send)

        got = over_seq(b_send, 1)
        b_mine = add(b_keep[0], got[0])
        b_got = over_seq(add(b_keep[1], got[1]), 2)
        got = over_seq(n_send, 1)
        n_mine = add(n_keep[0], got[0])
        n_got = over_seq(add(n_keep[1], got[1]), 2)

        valid = seq * rows + jnp.arange(rows)[None, :] < counts[:, None]
        scale = valid.astype(F32) * skip_mask[:, None].astype(F32) / SURVIVAL
        total = b_mine[:samples].astype(F32) + b_got[:samples].astype(F32)
        output = (tokens.astype(F32) + scale[..., None] * total).astype(BF)

        extra_rows = round_up(rows, 16)
        grad_tokens, extra = call(
            tokens_body,
            [shape_of(tokens.shape, BF), shape_of((extra_rows, width), BF)],
            [tokens, cotangent, n_mine, n_got, b_mine[samples], b_got[samples], g1, small],
            flops=10_000_000,
            nbytes=2_000_000,
            name="tokens_back",
        )
        flip = 1
        while flip < m:
            extra = add(extra, over_dp(extra, flip))
            flip *= 2
        grad_spatial = extra[:rows, : n * rows].astype(F32)
        grad_bias = extra[:rows, n * rows].astype(F32)
        tail = extra[rows // 16 * 16 + 8 :, :]
        tails = [tail] + [over_seq(tail, k) for k in range(1, n)]
        tails = [t.astype(F32) for t in tails]
        norm_one = (tails[0] + tails[1]) + (tails[2] + tails[3])
        order = []
        for j in range(n):
            part = tails[0]
            for k in range(1, n):
                part = jnp.where(seq ^ k == j, tails[k], part)
            order.append(part[2:4, :half])
        norm_two = jnp.concatenate(order, axis=1)

        grad_w_out = place(meta, o_pieces, (gate, width), False)
        grad_w_in = place(meta, u_pieces, (width, 2 * gate), True)
        grad_w_in = place(meta, v_pieces, (width, 2 * gate), True, gate, grad_w_in)
        return (
            output,
            grad_tokens,
            grad_w_in,
            grad_w_out,
            grad_spatial,
            grad_bias,
            norm_one[0],
            norm_one[1],
            norm_two[0],
            norm_two[1],
        )

    placed = (
        P("dp", "seq", None),
        P("dp"),
        P("dp"),
        P(),
        P(),
        P("seq", None),
        P("seq"),
        P(),
        P(),
        P(),
        P(),
        P("dp", "seq", None),
    )
    return jax.shard_map(
        shards,
        mesh=mesh,
        in_specs=placed,
        out_specs=(
            P("dp", "seq", None),
            P("dp", "seq", None),
            P(),
            P(),
            P("seq", None),
            P("seq"),
            P(),
            P(),
            P(),
            P(),
        ),
        check_vma=False,
    )
```

```python
import functools

import jax
import jax.numpy as jnp
from jax import lax
from jax.experimental import pallas as pl
from jax.experimental.pallas import tpu as pltpu
from jax.sharding import PartitionSpec as P

PATCHES = 324
SMALL_P = 100
MID_P = 196

EPSILON = 1e-05
SURVIVAL = 0.9

BF = jnp.bfloat16
F32 = jnp.float32
CHUNK = 16
VM = pl.BlockSpec(memory_space=pltpu.VMEM)
SM = pl.BlockSpec(memory_space=pltpu.SMEM)
HB = pl.BlockSpec(memory_space=pltpu.HBM)


def round_up(size, multiple):
    return -(-size // multiple) * multiple


def dot(a, b, ca, cb):
    return lax.dot_general(a, b, (((ca,), (cb,)), ((), ())), preferred_element_type=F32)


def iota(shape, axis):
    return lax.broadcasted_iota(jnp.int32, shape, axis)


def rows_at(start, size, multiple):
    return pl.ds(pl.multiple_of(start, multiple), size)


def call(body, outs, ins, scratch=(), specs=None, out_specs=None, **more):
    return pl.pallas_call(
        body,
        out_shape=outs,
        in_specs=specs if specs is not None else [VM] * len(ins),
        out_specs=out_specs if out_specs is not None else [VM] * len(outs),
        scratch_shapes=list(scratch),
        compiler_params=pltpu.CompilerParams(vmem_limit_bytes=20 * 2**20),
        cost_estimate=pl.CostEstimate(flops=1, bytes_accessed=1, transcendentals=0),
        **more,
    )(*ins)


def shape_of(shape, dtype):
    return jax.ShapeDtypeStruct(shape, dtype)


def project_body(pad, first_block, *refs):
    refs = list(refs)
    n_tok = len(refs) - 13 - (1 if first_block else 0)
    toks, refs = refs[:n_tok], refs[n_tok:]
    g1, s1, wu, wv = refs[:4]
    refs = refs[4:]
    if first_block:
        st_in, refs = refs[0], refs[1:]
    normed, gu, dgu, v, dgv, st, xs, hid, tile = refs
    samples, rows, width = toks[0].shape
    half = wu.shape[1]
    found = [jnp.zeros((CHUNK, 128), F32)] * (128 // CHUNK)
    low = rows // 8 * 8
    gain, shift = g1[...], s1[...]
    for i in range(samples):
        for b, tok in enumerate(toks):
            xs[i, b, low:, :] = jnp.zeros((pad - low, width), F32)
            xs[i, b, 0:rows, :] = tok[i].astype(F32)
            for c in range(pad // CHUNK):
                x = xs[i, b, c * CHUNK : (c + 1) * CHUNK, :]
                center = x - jnp.mean(x, axis=-1, keepdims=True)
                inverse = lax.rsqrt(jnp.mean(center * center, axis=-1, keepdims=True) + EPSILON)
                out = center * inverse * gain + shift
                normed[i, b * pad + c * CHUNK : b * pad + (c + 1) * CHUNK, :] = out.astype(BF)
        hid[i, :, 0:half] = dot(normed[i], wu[...], 1, 0)
        hid[i, :, half:] = dot(normed[i], wv[...], 1, 0)
    c0 = 0.7978845608028654
    c1 = 0.7978845608028654 * 0.044715

    def gelu_pair(h):
        a = (c1 * h) * h
        s = 0.5 + 0.5 * jnp.tanh(h * (c0 + a))
        g = h * s
        return g, s + (2.0 * g) * (1.0 - s) * (c0 + 3.0 * a)

    lane = iota((CHUNK, 128), 1)
    for i in range(samples):
        for b in range(len(toks)):
            blk = 2 * (i * 4 + first_block + b)
            for c in range(pad // CHUNK):
                at = slice(b * pad + c * CHUNK, b * pad + (c + 1) * CHUNK)
                g, d = gelu_pair(hid[i, at, 0:half])
                gu[i, at, :] = g.astype(BF)
                dgu[i, at, :] = d.astype(BF)
                g, d = gelu_pair(hid[i, at, half:])
                v[i, at, :] = g
                dgv[i, at, :] = d.astype(BF)
                mean = jnp.mean(g, axis=-1, keepdims=True)
                center = g - mean
                square = jnp.sum(center * center, axis=-1, keepdims=True)
                found[c] = jnp.where(
                    lane == blk, mean, jnp.where(lane == blk + 1, square, found[c])
                )
    for c, part_found in enumerate(found):
        tile[c * CHUNK : (c + 1) * CHUNK, :] = part_found
    flipped = jnp.transpose(tile[...])[0 : st.shape[0], :]
    st[...] = flipped + st_in[...] if first_block else flipped


def project(pad, first_block, toks, g1, s1, wu, wv, st_in=None):
    samples, rows, width = toks[0].shape
    half = wu.shape[1]
    n_rows = len(toks) * pad
    outs = [
        shape_of((samples, n_rows, width), BF),
        shape_of((samples, n_rows, half), BF),
        shape_of((samples, n_rows, half), BF),
        shape_of((samples, n_rows, half), F32),
        shape_of((samples, n_rows, half), BF),
        shape_of((round_up(samples * 8, 8), 128), F32),
    ]
    scratch = [
        pltpu.VMEM((samples, len(toks), pad, width), F32),
        pltpu.VMEM((samples, n_rows, 2 * half), F32),
        pltpu.VMEM((128, 128), F32),
    ]
    ins = [*toks, g1, s1, wu, wv] + ([st_in] if first_block else [])
    return call(
        functools.partial(project_body, pad, first_block),
        outs,
        ins,
        scratch,
        name="project",
    )


GROUPS = ((0, 1), (2,), (3,))


def part(r, pad):
    for k, blocks in enumerate(GROUPS):
        if r in blocks:
            return k, (r - blocks[0]) * pad


def position_map(seq, rows, pad, n, columns):
    a = iota((columns, n * pad), 0)
    j = iota((columns, n * pad), 1)
    r = jnp.zeros_like(j)
    for k in range(1, n):
        r = r + (j >= k * pad).astype(jnp.int32)
    q = j - r * pad
    hit = (a == (r ^ seq) * rows + q) & (q < rows)
    hit = hit | ((a == n * rows) & (j == pad - 1)) | ((a == n * rows + 1) & (j == pad - 2))
    return jnp.where(hit, 1.0, 0.0).astype(BF)


def patch_count(meta, i):
    kind = meta[2 + i]
    return jnp.where(kind == 0, SMALL_P, jnp.where(kind == 1, MID_P, PATCHES))


def branch_scale(meta, i, samples, where):
    keep = jnp.where(where < patch_count(meta, i), meta[2 + samples + i], 0)
    return keep.astype(F32) / SURVIVAL


def valid_rows(meta, i, r, c, rows):
    p = c * CHUNK + iota((CHUNK, 1), 0)
    return (p < rows) & ((meta[0] ^ r) * rows + p < patch_count(meta, i))


def prepare_body(
    n, pad, meta, c0, c1, c2, c3, wo, gu0, gu1, gu2,
    sp, gb, gp, gs, gmix, pm,
    spt,
):
    samples, rows = c0.shape[0] - 1, c0.shape[1]
    seq = meta[0]
    cots, gus = (c0, c1, c2, c3), (gu0, gu1, gu2)
    columns = pm.shape[0]
    low = rows // 16 * 16
    pm[...] = position_map(seq, rows, pad, n, columns)
    for r in range(n):
        sp[r * pad + low : (r + 1) * pad, :] = jnp.zeros((pad - low, n * pad), BF)
        sp[r * pad : r * pad + rows, :] = dot(cots[r][samples, :, 0:columns], pm[...], 1, 0).astype(BF)
    spt[...] = jnp.transpose(sp[...].astype(F32)).astype(BF)
    for i in range(samples):
        for r in range(n):
            p = iota((rows, 1), 0)
            scale = branch_scale(meta, i, samples, (seq ^ r) * rows + p)
            gb[i, r * pad + low : (r + 1) * pad, :] = jnp.zeros((pad - low, gb.shape[2]), BF)
            gb[i, r * pad : r * pad + rows, :] = (cots[r][i].astype(F32) * scale).astype(BF)
        gp[i] = dot(gb[i], wo[...], 1, 1)
        for r in range(n):
            k, base = part(r, pad)
            for c in range(pad // CHUNK):
                at = slice(r * pad + c * CHUNK, r * pad + (c + 1) * CHUNK)
                src = slice(base + c * CHUNK, base + (c + 1) * CHUNK)
                gs[i, at, :] = (gp[i, at, :] * gus[k][i, src, :].astype(F32)).astype(BF)
        full = dot(spt[...], gs[i], 1, 0)
        for r in range(n):
            for c in range(pad // CHUNK):
                at = slice(r * pad + c * CHUNK, r * pad + (c + 1) * CHUNK)
                gmix[i, at, :] = jnp.where(valid_rows(meta, i, r, c, rows), full[at], 0.0)


def own_lanes(rows, seq, half):
    count = half // 128
    return jnp.concatenate([rows[pl.ds(seq * count + k, 1), :] for k in range(count)], axis=1)


def lane_sum(x):
    total = x[:, 0:128]
    for k in range(1, x.shape[1] // 128):
        total = total + x[:, k * 128 : (k + 1) * 128]
    return total


def row_sums(parts, st, pad):
    ones = jnp.ones((8, 128), BF)
    blocks = parts.shape[0] // 2
    for b in range(blocks):
        for j in range(2):
            x = parts[j * blocks + b]
            high = x.astype(BF)
            low = (x - high.astype(F32)).astype(BF)
            sums = dot(ones, high, 1, 1) + dot(ones, low, 1, 1)
            st[2 * b + j : 2 * b + j + 1, 0:pad] = sums[0:1, :]


def spatial_body(
    n, pad, meta, v0, v1, v2, gu0, gu1, gu2, dgu0, dgu1, dgu2, sp, gp, gs, pm, gmix, g2, s2, t0, t1, t2, t3,
    prod, ghu, cols, st, keep, send,
    mixed, so, tile, parts,
):
    samples, half, rows = gp.shape[0], gp.shape[2], PATCHES // n
    whole = half * n
    stats, vs, gus, dgus = (t0, t1, t2, t3), (v0, v1, v2), (gu0, gu1, gu2), (dgu0, dgu1, dgu2)
    tile[...] = jnp.zeros_like(tile)
    for i in range(samples):
        for r in range(n):
            at = [2 * (i * n + (r ^ k)) for k in range(n)]
            means = [stats[k][at[k] : at[k] + 1, :] for k in range(n)]
            squares = [stats[k][at[k] + 1 : at[k] + 2, :] for k in range(n)]
            mean = ((means[0] + means[1]) + (means[2] + means[3])) / n
            spread = (squares[0] + squares[1]) + (squares[2] + squares[3])
            for k in range(n):
                spread = spread + half * (means[k] - mean) * (means[k] - mean)
            blk = 2 * (i * n + r)
            tile[blk : blk + 1, :] = mean
            tile[blk + 1 : blk + 2, :] = lax.rsqrt(spread / whole + EPSILON)
    cols[...] = jnp.transpose(tile[...])
    gain, shift = own_lanes(g2, meta[0], half), own_lanes(s2, meta[0], half)
    for i in range(samples):
        for r in range(n):
            k, base = part(r, pad)
            blk = 2 * (i * n + r)
            for c in range(pad // CHUNK):
                here = slice(c * CHUNK, (c + 1) * CHUNK)
                at = slice(r * pad + c * CHUNK, r * pad + (c + 1) * CHUNK)
                mean, inverse = cols[here, blk : blk + 1], cols[here, blk + 1 : blk + 2]
                standard = (vs[k][i, base + c * CHUNK : base + (c + 1) * CHUNK, :] - mean) * inverse
                out = jnp.where(valid_rows(meta, i, r, c, rows), standard * gain + shift, 0.0)
                if r == 0 and (c + 1) * CHUNK == pad:
                    p = c * CHUNK + iota((CHUNK, 1), 0)
                    out = jnp.where(p >= pad - 2, 1.0, out)
                mixed[i, at, :] = out.astype(BF)
                t = gmix[i, at, :] * gain
                parts[i * n + r, here, :] = lane_sum(t)
                parts[samples * n + i * n + r, here, :] = lane_sum(t * standard)
        so[i] = dot(sp[...], mixed[i], 1, 0)
    row_sums(parts, st, pad)
    total = dot(gs[0], mixed[0], 1, 1)
    for i in range(1, samples):
        total = total + dot(gs[i], mixed[i], 1, 1)
    placed = dot(total.astype(BF), pm[...], 1, 1).astype(BF)
    for r in range(n):
        (keep, send)[r % 2][r // 2] = placed[r * pad : (r + 1) * pad, :]
    for i in range(samples):
        for r in range(n):
            k, base = part(r, pad)
            for c in range(pad // CHUNK):
                src = slice(base + c * CHUNK, base + (c + 1) * CHUNK)
                at = slice(r * pad + c * CHUNK, r * pad + (c + 1) * CHUNK)
                s = so[i, at, :]
                prod[i, at, :] = (gus[k][i, src, :].astype(F32) * s).astype(BF)
                ghu[i, at, :] = (gp[i, at, :] * s * dgus[k][i, src, :].astype(F32)).astype(BF)


def weight_sum(normed, grads, pad):
    total = None
    for i in range(grads.shape[0]):
        for k, blocks in enumerate(GROUPS):
            rows = slice(blocks[0] * pad, (blocks[-1] + 1) * pad)
            term = dot(normed[k][i], grads[i, rows, :], 0, 0)
            total = term if total is None else total + term
    return total


def store_shards(dp, whole, outs, base):
    shard = whole.shape[0] // 4
    for rho, out in enumerate(outs):
        here = whole[rows_at(((dp ^ rho) & 3) * shard, shard, 16), :]
        out[base : base + shard, :] = here.astype(BF)


def weights_body(n, pad, meta, prod, gb, ghu, n0, n1, n2, keep_a, keep_b, send, ow, uw):
    total = dot(gb[0], prod[0], 0, 0)
    for i in range(1, prod.shape[0]):
        total = total + dot(gb[i], prod[i], 0, 0)
    ow[...] = total
    uw[...] = weight_sum((n0, n1, n2), ghu, pad)
    shard = ow.shape[0] // 4
    outs = (keep_a, send.at[0], keep_b, send.at[1])
    store_shards(meta[1], ow, outs, 0)
    store_shards(meta[1], uw, outs, shard)


EXTRA = 32


def back_body(
    n, pad, meta, gmix, v0, v1, v2, dgv0, dgv1, dgv2, cols, t0, t1, t2, t3, g1, s1, g2, n0, n1, n2,
    ghu, wu, wv, e0, e1, e2,
    grad, keep_a, keep_b, send,
    tile, col, ghv, vw, acc, sums, extra,
):
    samples, half = gmix.shape[0], gmix.shape[2]
    width = grad.shape[2]
    stats, vs, dgvs = (t0, t1, t2, t3), (v0, v1, v2), (dgv0, dgv1, dgv2)
    tile[...] = jnp.zeros_like(tile)
    for i in range(samples):
        for r in range(n):
            blk = 2 * (i * n + r)
            terms = [
                stats[k][2 * (i * n + (r ^ k)) : 2 * (i * n + (r ^ k)) + 2, :] for k in range(n)
            ]
            tile[blk : blk + 2, :] = ((terms[0] + terms[1]) + (terms[2] + terms[3])) / (half * n)
    col[...] = jnp.transpose(tile[...])
    gain = own_lanes(g2, meta[0], half)
    acc[...] = jnp.zeros_like(acc)
    for i in range(samples):
        for r in range(n):
            k, base = part(r, pad)
            blk = 2 * (i * n + r)
            for c in range(pad // CHUNK):
                here = slice(c * CHUNK, (c + 1) * CHUNK)
                at = slice(r * pad + c * CHUNK, r * pad + (c + 1) * CHUNK)
                src = slice(base + c * CHUNK, base + (c + 1) * CHUNK)
                mean, inverse = cols[here, blk : blk + 1], cols[here, blk + 1 : blk + 2]
                first, second = col[here, blk : blk + 1], col[here, blk + 1 : blk + 2]
                standard = (vs[k][i, src, :] - mean) * inverse
                g = gmix[i, at, :]
                out = inverse * (g * gain - first - standard * second)
                ghv[i, at, :] = (out * dgvs[k][i, src, :].astype(F32)).astype(BF)
                acc[0] += g * standard
                acc[1] += g
    normed = (n0, n1, n2)
    vw[...] = weight_sum(normed, ghv, pad)
    sums[...] = jnp.zeros_like(sums)
    for i in range(samples):
        grad[i] = dot(ghu[i], wu[...], 1, 1) + dot(ghv[i], wv[...], 1, 1)
        for r in range(n):
            k, base = part(r, pad)
            for c in range(pad // CHUNK):
                at = slice(r * pad + c * CHUNK, r * pad + (c + 1) * CHUNK)
                src = slice(base + c * CHUNK, base + (c + 1) * CHUNK)
                g = grad[i, at, :]
                sums[0] += g * normed[k][i, src, :].astype(F32)
                sums[1] += g
    shift_one = jnp.sum(sums[1], axis=0, keepdims=True)
    gain_one = (jnp.sum(sums[0], axis=0, keepdims=True) - s1[...] * shift_one) / g1[...]
    edge = e0[0].astype(F32) + e1[0].astype(F32) + e2[...].astype(F32)
    size = pad // 4
    extra[...] = jnp.zeros_like(extra)
    for k in range(4):
        extra[k, 0:size, :] = edge[k * size : (k + 1) * size, :]
    extra[0, size : size + 1, :] = jnp.sum(acc[0], axis=0, keepdims=True)
    extra[1, size : size + 1, :] = jnp.sum(acc[1], axis=0, keepdims=True)
    for k, row in ((2, gain_one), (3, shift_one)):
        extra[k, size : size + 1, :] = row[:, 0:half]
        extra[k, size + 1 : size + 2, 0 : width - half] = row[:, half:]
    outs = (keep_a, send.at[0], keep_b, send.at[1])
    store_shards(meta[1], vw, outs, 0)
    shard = vw.shape[0] // 4
    for rho, out in enumerate(outs):
        out[shard:, :] = extra[(meta[1] ^ rho) & 3].astype(BF)


def rows_body(n, pad, prod, wo, grad, keep_a, send_a, keep_b, send_b):
    samples, rows = prod.shape[0], keep_a.shape[1]
    outs = (keep_a, send_a, keep_b, send_b)
    for i in range(samples):
        full = dot(prod[i], wo[...], 1, 0)
        for r in range(n):
            outs[r][i] = full[r * pad : r * pad + rows, :].astype(BF)
            outs[r][samples + i] = grad[i, r * pad : r * pad + rows, :].astype(BF)


def finish_rows_body(meta, tok, cot, keep, got_a, got_b, g1, output, grad_tokens):
    samples, rows = tok.shape[0], tok.shape[1]
    gain = g1[...]
    p = meta[0] * rows + iota((rows, 1), 0)
    for i in range(samples):
        x = tok[i].astype(F32)
        total = keep[i].astype(F32) + got_a[i].astype(F32) + got_b[i].astype(F32)
        output[i] = (x + branch_scale(meta, i, samples, p) * total).astype(BF)
        center = x - jnp.mean(x, axis=-1, keepdims=True)
        inverse = lax.rsqrt(jnp.mean(center * center, axis=-1, keepdims=True) + EPSILON)
        standard = center * inverse
        k = samples + i
        t = (keep[k].astype(F32) + got_a[k].astype(F32) + got_b[k].astype(F32)) * gain
        first = jnp.mean(t, axis=-1, keepdims=True)
        second = jnp.mean(t * standard, axis=-1, keepdims=True)
        grad = cot[i].astype(F32) + inverse * (t - first - standard * second)
        grad_tokens[i] = grad.astype(BF)


def sources(meta):
    seq, shard = meta[0], meta[1] & 3
    out = []
    for flip in (0, 1):
        s = seq ^ flip
        core = s & 1
        out += [
            (shard, s),
            (shard ^ (1 - core), s ^ (2 * core)),
            (shard ^ core, s ^ (2 * (1 - core))),
            (shard ^ 1, s ^ 2),
        ]
    return out


def place_first_body(half, meta, *refs):
    pieces = refs[:8]
    w_in, w_out, wide, tall, sems = refs[8:]
    shard = wide.shape[1]
    copies = []
    for k, (group, seq) in enumerate(sources(meta)):
        for e in range(2):
            slot = 2 * k + e
            row = (group ^ (2 * e)) * shard
            columns = rows_at(seq * half, half, 128)
            tall[slot] = jnp.transpose(pieces[k][e, 0:shard, :].astype(F32))
            target = w_out.at[columns, rows_at(row, shard, 128)]
            copies.append(pltpu.make_async_copy(tall.at[slot], target, sems.at[2 * slot]))
            copies[-1].start()
            wide[slot] = pieces[k][e, shard:, :].astype(F32)
            target = w_in.at[rows_at(row, shard, 16), columns]
            copies.append(pltpu.make_async_copy(wide.at[slot], target, sems.at[2 * slot + 1]))
            copies[-1].start()
    for copy in copies:
        copy.wait()


def place_last_body(half, gate, meta, *refs):
    pieces = refs[:8]
    w_in, spatial, bias, gain_one, shift_one, gain_two, shift_two, wide, edge, norms, sems = refs[9:]
    shard = wide.shape[1]
    rows, patches = spatial.shape
    size = edge.shape[0] // 4
    me, core = meta[0], meta[0] & 1
    origins = sources(meta)
    copies = []
    small = []
    for k, (group, seq) in enumerate(origins):
        for e in range(2):
            slot = 2 * k + e
            at = group ^ (2 * e)
            wide[slot] = pieces[k][e, 0:shard, :].astype(F32)
            columns = rows_at(gate + seq * half, half, 128)
            target = w_in.at[rows_at(at * shard, shard, 16), columns]
            copies.append(pltpu.make_async_copy(wide.at[slot], target, sems.at[slot]))
            copies[-1].start()
            rest = pieces[k][e, shard:, :].astype(F32)
            small.append((at, rest[0:size]))
            norms[at, seq] = rest[size:]
    for e in range(2):
        at, own = small[e]
        edge[rows_at(at * size, size, 8), :] = own
        at = (meta[1] & 3) ^ 1 ^ (2 * e)
        edge[rows_at(at * size, size, 8), :] = jnp.where(core == 0, small[2 + e][1], small[4 + e][1])
    spatial[...] = edge[0:rows, 0:patches]
    first = patches // 128 * 128
    tail = edge[0:rows, first:]
    column = jnp.sum(
        jnp.where(iota(tail.shape, 1) == patches - first, tail, 0.0), axis=1, keepdims=True
    )
    diagonal = iota((rows, rows), 0) == iota((rows, rows), 1)
    bias[...] = jnp.sum(jnp.where(diagonal, column, 0.0), axis=0, keepdims=True)
    for at, out in ((2, gain_one), (3, shift_one)):
        total = (norms[at, 0] + norms[at, 1]) + (norms[at, 2] + norms[at, 3])
        out[:, 0:half] = total[0:1, :]
        out[:, half:] = total[1:2, 0 : out.shape[1] - half]
    for at, out in ((0, gain_two), (1, shift_two)):
        for j in range(4):
            out[:, j * half : (j + 1) * half] = norms[at, j, 0:1, :]
    for copy in copies:
        copy.wait()


def solution(mesh):
    n, m = mesh.shape["seq"], mesh.shape["dp"]

    def over_seq(x, flip):
        return lax.ppermute(x, "seq", [(i, i ^ flip) for i in range(n)])

    def over_dp(x, flip):
        return lax.ppermute(x, "dp", [(i, i ^ flip) for i in range(m)])

    def mixed_axes(x, core_of_x):
        pairs = []
        for d in range(m):
            for s in range(n):
                other = (d ^ 1, s) if s & 1 == core_of_x else (d, s ^ 2)
                pairs.append((d * n + s, other[0] * n + other[1]))
        return lax.ppermute(x, ("dp", "seq"), pairs)

    def add(*terms):
        total = terms[0].astype(F32)
        for t in terms[1:]:
            total = total + t.astype(F32)
        return total.astype(BF)

    def ordered():
        last = []

        def step(body, *ins):
            if last:
                ins, _ = lax.optimization_barrier((ins, last[0]))
            out = body(*ins) if body else ins[0]
            last[:] = [jax.tree.leaves(out)[0]]
            return out

        return step

    def shards(
        tokens,
        res_class,
        skip_mask,
        w_in,
        w_out,
        spatial,
        spatial_bias,
        gain_one,
        shift_one,
        gain_two,
        shift_two,
        cotangent,
    ):
        samples, rows, width = tokens.shape
        gate = w_out.shape[0]
        half = gate // n
        pad = round_up(rows + 2, 16)
        full = n * pad
        columns = round_up(n * rows + 2, 128)
        seq, dp = lax.axis_index("seq"), lax.axis_index("dp")
        meta = jnp.concatenate([seq[None], dp[None], res_class, skip_mask]).astype(jnp.int32)
        step = ordered()
        big_bf, big_f32 = (shape_of((samples, full, half), d) for d in (BF, F32))
        shard = width // 4
        square = shape_of((round_up(samples * 2 * n, 8), 128), F32)

        t0 = tokens
        t2 = over_seq(t0, 2)
        t1 = over_seq(t0, 1)
        high = lax.reduce_precision(spatial_bias, 8, 7)
        side = jnp.stack([high, spatial_bias - high], axis=1).astype(BF)
        packed = jnp.concatenate([spatial, side], axis=1)
        packed = jnp.pad(packed, ((0, 0), (0, width - packed.shape[1])))
        c0 = jnp.concatenate([cotangent, packed[None]])
        c2 = over_seq(c0, 2)
        wu = lax.dynamic_slice(w_in, (0, seq * half), (width, half))
        wv = lax.dynamic_slice(w_in, (0, gate + seq * half), (width, half))
        wo = lax.dynamic_slice(w_out, (seq * half, 0), (half, width))
        g1, s1 = gain_one[None], shift_one[None]
        g2, s2 = gain_two.reshape(-1, 128), shift_two.reshape(-1, 128)
        meta, wu, wv, wo, c0, t1 = lax.optimization_barrier((meta, wu, wv, wo, c0, t1))
        c1 = over_seq(c0, 1)

        n0, gu0, dgu0, v0, dgv0, st = step(
            lambda *a: project(pad, 0, a[:2], *a[2:]), t0, t1, g1, s1, wu, wv
        )
        t2 = step(None, t2)
        t3 = over_seq(t2, 1)
        n1, gu1, dgu1, v1, dgv1, st = step(
            lambda *a: project(pad, 2, a[:1], *a[1:]), t2, g1, s1, wu, wv, st
        )
        n2, gu2, dgu2, v2, dgv2, st = step(
            lambda *a: project(pad, 3, a[:1], *a[1:]), t3, g1, s1, wu, wv, st
        )
        normed = [n0, n1, n2]
        stats = step(None, [st] + [over_seq(st, k) for k in range(1, n)])
        c2 = step(None, c2)
        c3 = over_seq(c2, 1)

        def prepare(*ins):
            return call(
                functools.partial(prepare_body, n, pad),
                [
                    shape_of((full, full), BF), shape_of((samples, full, width), BF),
                    big_f32, big_bf, big_f32, shape_of((columns, full), BF),
                ],
                ins,
                [pltpu.VMEM((full, full), BF)],
                specs=[SM] + [VM] * (len(ins) - 1),
                name="prepare",
            )

        sp, gb, gp, gs, gmix, pm = step(
            prepare, meta, c0, c1, c2, c3, wo, gu0, gu1, gu2
        )

        def spatial_unit(*ins):
            edge = shape_of((n // 2, pad, columns), BF)
            return call(
                functools.partial(spatial_body, n, pad),
                [big_bf, big_bf, shape_of((128, 128), F32), square, edge, edge],
                ins,
                [
                    pltpu.VMEM((samples, full, half), BF),
                    pltpu.VMEM((samples, full, half), F32),
                    pltpu.VMEM((128, 128), F32),
                    pltpu.VMEM((2 * samples * n, pad, 128), F32),
                ],
                specs=[SM] + [VM] * (len(ins) - 1),
                name="spatial",
            )

        prod, ghu, cols, st2, e_keep, e_send = step(
            spatial_unit, meta, v0, v1, v2, gu0, gu1, gu2, dgu0, dgu1, dgu2, sp, gp, gs, pm, gmix,
            g2, s2, *stats,
        )
        stats = [st2] + [over_seq(st2, k) for k in range(1, n)]
        e_got = over_seq(e_send, 1)

        def weights(*ins):
            shape = shape_of((2 * shard, half), BF)
            return call(
                functools.partial(weights_body, n, pad),
                [shape, shape, shape_of((2, 2 * shard, half), BF)],
                ins,
                [pltpu.VMEM((width, half), F32), pltpu.VMEM((width, half), F32)],
                specs=[SM] + [VM] * (len(ins) - 1),
                name="weights",
            )

        def add_second(a, b):
            return add(a, b[1])

        def add_first(a, b, c):
            return add(a, b[0], c)

        def pair_up(*a):
            return jnp.stack(a)

        def twin(x):
            return over_seq(x, 1)

        w_a, w_b, w_send = step(weights, meta, prod, gb, ghu, *normed)
        w_got = over_dp(w_send, 1)
        e_last = over_seq(step(lambda a, b: add(a[1], b[1]), e_keep, e_got), 2)

        def back(*ins):
            shape = shape_of((shard + EXTRA, half), BF)
            return call(
                functools.partial(back_body, n, pad),
                [
                    shape_of((samples, full, width), F32), shape, shape,
                    shape_of((2, shard + EXTRA, half), BF),
                ],
                ins,
                [
                    pltpu.VMEM((128, 128), F32),
                    pltpu.VMEM((128, 128), F32),
                    pltpu.VMEM((samples, full, half), BF),
                    pltpu.VMEM((width, half), F32),
                    pltpu.VMEM((2, CHUNK, half), F32),
                    pltpu.VMEM((2, CHUNK, width), F32),
                    pltpu.VMEM((4, EXTRA, half), F32),
                ],
                specs=[SM] + [VM] * (len(ins) - 1),
                name="back",
            )

        grad, v_a, v_b, v_send = step(
            back, meta, gmix, v0, v1, v2, dgv0, dgv1, dgv2, cols, *stats, g1, s1, g2, *normed, ghu,
            wu, wv, e_keep, e_got, e_last,
        )
        v_got = over_dp(v_send, 1)

        def rows_out(*ins):
            shape = shape_of((2 * samples, rows, width), BF)
            return call(functools.partial(rows_body, n, pad), [shape] * 4, ins, name="rows_out")

        r_a, send_a, r_b, send_b = step(rows_out, prod, wo, grad)
        r_got, r_got_b = twin(send_a), twin(send_b)

        w_z = over_dp(step(add_second, w_b, w_got), 2)
        r_got, r_got_b = step(None, (r_got, r_got_b))
        r_last = over_seq(step(add, r_b, r_got_b), 2)
        v_z = over_dp(step(add_second, v_b, v_got), 2)
        w_mine = step(add_first, w_a, w_got, w_z)
        w_z = over_dp(w_mine, 4) if m > 4 else None
        v_mine = step(add_first, v_a, v_got, v_z)
        v_z = over_dp(v_mine, 4) if m > 4 else None
        flip = 8
        while flip < m:
            w_mine, v_mine = step(add, w_mine, w_z), step(add, v_mine, v_z)
            w_z, v_z = over_dp(w_mine, flip), over_dp(v_mine, flip)
            flip *= 2
        if m > 4:
            w_mine = step(add, w_mine, w_z)
        w_z = over_dp(w_mine, 2)

        def finish_rows(*ins):
            shape = shape_of(tokens.shape, BF)
            return call(
                finish_rows_body, [shape, shape], ins, specs=[SM] + [VM] * 6, name="finish_rows"
            )

        output, grad_tokens = step(finish_rows, meta, t0, c0, r_a, r_got, r_last, g1)
        if m > 4:
            v_mine = step(add, v_mine, v_z)
        v_z = over_dp(v_mine, 2)
        w_pair = step(pair_up, w_mine, w_z)
        w_first, w_second, w_pair_b = mixed_axes(w_pair, 0), mixed_axes(w_pair, 1), twin(w_pair)
        v_z, w_pair_b = step(None, (v_z, w_pair_b))
        v_pair = step(pair_up, v_mine, v_z)
        v_first, v_second = mixed_axes(v_pair, 0), mixed_axes(v_pair, 1)
        w_first, w_second = step(None, (w_first, w_second))
        w_third, w_first_b, w_second_b = mixed_axes(w_first, 1), twin(w_first), twin(w_second)
        v_first, v_second, w_first_b, w_second_b = step(
            None, (v_first, v_second, w_first_b, w_second_b)
        )
        v_third, v_pair_b, v_first_b = mixed_axes(v_first, 1), twin(v_pair), twin(v_first)
        w_third, v_pair_b, v_first_b = step(None, (w_third, v_pair_b, v_first_b))
        w_third_b, v_second_b = twin(w_third), twin(v_second)

        def place_first(*ins):
            return call(
                functools.partial(place_first_body, half),
                [shape_of((width, 2 * gate), F32), shape_of((gate, width), F32)],
                ins,
                [
                    pltpu.VMEM((16, shard, half), F32),
                    pltpu.VMEM((16, half, shard), F32),
                    pltpu.SemaphoreType.DMA((32,)),
                ],
                specs=[SM] + [VM] * 8,
                out_specs=[HB] * 2,
                name="place_first",
            )

        def place_last(*ins):
            one, two = shape_of((1, width), F32), shape_of((1, gate), F32)
            small = [shape_of((rows, n * rows), F32), shape_of((1, rows), F32), one, one, two, two]
            return call(
                functools.partial(place_last_body, half, gate),
                [shape_of((width, 2 * gate), F32)] + small,
                ins,
                [
                    pltpu.VMEM((16, shard, half), F32),
                    pltpu.VMEM((pad, columns), F32),
                    pltpu.VMEM((4, n, EXTRA - pad // 4, half), F32),
                    pltpu.SemaphoreType.DMA((16,)),
                ],
                specs=[SM] + [VM] * 8 + [HB],
                out_specs=[HB] + [VM] * 6,
                input_output_aliases={9: 0},
                name="place_last",
            )

        grad_w_in, grad_w_out = step(
            place_first, meta, w_pair, w_first, w_second, w_third, w_pair_b, w_first_b, w_second_b,
            w_third_b,
        )
        v_third = step(None, v_third)
        v_third_b = twin(v_third)
        grad_w_in, grad_spatial, *sums = step(
            place_last, meta, v_pair, v_first, v_second, v_third, v_pair_b, v_first_b, v_second_b,
            v_third_b, grad_w_in,
        )
        sums = [v.reshape(-1) for v in sums]
        return (output, grad_tokens, grad_w_in, grad_w_out, grad_spatial, *sums)

    placed = (
        P("dp", "seq", None),
        P("dp"),
        P("dp"),
        P(),
        P(),
        P("seq", None),
        P("seq"),
        P(),
        P(),
        P(),
        P(),
        P("dp", "seq", None),
    )
    return jax.shard_map(
        shards,
        mesh=mesh,
        in_specs=placed,
        out_specs=(
            P("dp", "seq", None),
            P("dp", "seq", None),
            P(),
            P(),
            P("seq", None),
            P("seq"),
            P(),
            P(),
            P(),
            P(),
        ),
        check_vma=False,
    )
```

```python
import functools

import jax
import jax.numpy as jnp
from jax import lax
from jax.experimental import pallas as pl
from jax.experimental.pallas import tpu as pltpu
from jax.sharding import PartitionSpec as P

PATCHES = 324
SMALL_P = 100
MID_P = 196

EPSILON = 1e-05
SURVIVAL = 0.9

BF = jnp.bfloat16
F32 = jnp.float32
CHUNK = 16
VM = pl.BlockSpec(memory_space=pltpu.VMEM)
SM = pl.BlockSpec(memory_space=pltpu.SMEM)
HB = pl.BlockSpec(memory_space=pltpu.HBM)


ORDER = (
    "weights", "stats", "a_send", "sums", "back", "rows", "a_rs", "tick", "v_send", "rows_core", "v_rs", "a_z2",
    "v_z2", "a_pair", "finish", "v_pair", "a_mark", "v_mark", "a_twin0", "a_twin1", "a_third", "a_twin2", "a_twin3",
    "v_twin0", "v_twin1", "place_first", "v_third", "v_twin2", "v_twin3", "place_most", "place_last",
)


def round_up(size, multiple):
    return -(-size // multiple) * multiple


def dot(a, b, ca, cb):
    return lax.dot_general(a, b, (((ca,), (cb,)), ((), ())), preferred_element_type=F32)


def iota(shape, axis):
    return lax.broadcasted_iota(jnp.int32, shape, axis)


def rows_at(start, size, multiple):
    return pl.ds(pl.multiple_of(start, multiple), size)


def call(body, outs, ins, scratch=(), specs=None, out_specs=None, flops=1, **more):
    return pl.pallas_call(
        body,
        out_shape=outs,
        in_specs=specs if specs is not None else [VM] * len(ins),
        out_specs=out_specs if out_specs is not None else [VM] * len(outs),
        scratch_shapes=list(scratch),
        compiler_params=pltpu.CompilerParams(vmem_limit_bytes=20 * 2**20),
        cost_estimate=pl.CostEstimate(flops=flops, bytes_accessed=1, transcendentals=0),
        **more,
    )(*ins)


def shape_of(shape, dtype):
    return jax.ShapeDtypeStruct(shape, dtype)


def add_body(*refs):
    total = refs[0][...].astype(F32)
    for ref in refs[1:-1]:
        total = total + ref[...].astype(F32)
    refs[-1][...] = total.astype(BF)


def tick_body(clock, out):
    out[...] = clock[...] + 1.0


def pair_body(a, b, out):
    out[0] = a[...]
    out[1] = b[...]


def project_body(pad, first_block, *refs):
    refs = list(refs)
    n_tok = len(refs) - 13 - (1 if first_block else 0)
    toks, refs = refs[:n_tok], refs[n_tok:]
    g1, s1, wu, wv = refs[:4]
    refs = refs[4:]
    if first_block:
        st_in, refs = refs[0], refs[1:]
    normed, gu, dgu, v, dgv, st, xs, hid, tile = refs
    samples, rows, width = toks[0].shape
    half = wu.shape[1]
    size = samples * pad
    found = [jnp.zeros((CHUNK, 128), F32)] * (128 // CHUNK)
    low = rows // 8 * 8
    gain, shift = g1[...], s1[...]
    for b, tok in enumerate(toks):
        for i in range(samples):
            base = (b * samples + i) * pad
            xs[base + low : base + pad, :] = jnp.zeros((pad - low, width), F32)
            xs[base : base + rows, :] = tok[i].astype(F32)
            for c in range(base, base + pad, CHUNK):
                x = xs[c : c + CHUNK, :]
                center = x - jnp.mean(x, axis=-1, keepdims=True)
                inverse = lax.rsqrt(jnp.mean(center * center, axis=-1, keepdims=True) + EPSILON)
                normed[c : c + CHUNK, :] = (center * inverse * gain + shift).astype(BF)
        at = slice(b * size, (b + 1) * size)
        hid[at, 0:half] = dot(normed[at, :], wu[...], 1, 0)
        hid[at, half:] = dot(normed[at, :], wv[...], 1, 0)
    c0 = 0.7978845608028654
    c1 = 0.7978845608028654 * 0.044715

    def gelu_pair(h):
        a = (c1 * h) * h
        s = 0.5 + 0.5 * jnp.tanh(h * (c0 + a))
        g = h * s
        return g, s + (2.0 * g) * (1.0 - s) * (c0 + 3.0 * a)

    lane = iota((CHUNK, 128), 1)
    for b in range(len(toks)):
        for i in range(samples):
            base = (b * samples + i) * pad
            blk = 2 * (i * 4 + first_block + b)
            for c in range(pad // CHUNK):
                at = slice(base + c * CHUNK, base + (c + 1) * CHUNK)
                g, d = gelu_pair(hid[at, 0:half])
                gu[at, :] = g.astype(BF)
                dgu[at, :] = d.astype(BF)
                g, d = gelu_pair(hid[at, half:])
                v[at, :] = g
                dgv[at, :] = d.astype(BF)
                mean = jnp.mean(g, axis=-1, keepdims=True)
                center = g - mean
                square = jnp.sum(center * center, axis=-1, keepdims=True)
                found[c] = jnp.where(
                    lane == blk, mean, jnp.where(lane == blk + 1, square, found[c])
                )
    for c, part_found in enumerate(found):
        tile[c * CHUNK : (c + 1) * CHUNK, :] = part_found
    flipped = jnp.transpose(tile[...])[0 : st.shape[0], :]
    st[...] = flipped + st_in[...] if first_block else flipped


def project(pad, first_block, toks, g1, s1, wu, wv, st_in=None):
    samples, rows, width = toks[0].shape
    half = wu.shape[1]
    n_rows = len(toks) * samples * pad
    outs = [
        shape_of((n_rows, width), BF),
        shape_of((n_rows, half), BF),
        shape_of((n_rows, half), BF),
        shape_of((n_rows, half), F32),
        shape_of((n_rows, half), BF),
        shape_of((round_up(samples * 8, 8), 128), F32),
    ]
    scratch = [
        pltpu.VMEM((n_rows, width), F32),
        pltpu.VMEM((n_rows, 2 * half), F32),
        pltpu.VMEM((128, 128), F32),
    ]
    ins = [*toks, g1, s1, wu, wv] + ([st_in] if first_block else [])
    return call(
        functools.partial(project_body, pad, first_block),
        outs,
        ins,
        scratch,
        name="project",
    )


GROUPS = ((0, 1), (2,), (3,))


def part(r, i, samples, pad):
    for k, blocks in enumerate(GROUPS):
        if r in blocks:
            return k, ((r - blocks[0]) * samples + i) * pad


def group_rows(size):
    return [slice(blocks[0] * size, (blocks[-1] + 1) * size) for blocks in GROUPS]


def position_map(seq, rows, pad, n, columns):
    a = iota((columns, n * pad), 0)
    j = iota((columns, n * pad), 1)
    r = jnp.zeros_like(j)
    for k in range(1, n):
        r = r + (j >= k * pad).astype(jnp.int32)
    q = j - r * pad
    hit = (a == (r ^ seq) * rows + q) & (q < rows)
    hit = hit | ((a == n * rows) & (j == pad - 1)) | ((a == n * rows + 1) & (j == pad - 2))
    return jnp.where(hit, 1.0, 0.0).astype(BF)


def patch_count(meta, i):
    kind = meta[2 + i]
    return jnp.where(kind == 0, SMALL_P, jnp.where(kind == 1, MID_P, PATCHES))


def branch_scale(meta, i, samples, where):
    keep = jnp.where(where < patch_count(meta, i), meta[2 + samples + i], 0)
    return keep.astype(F32) / SURVIVAL


def valid_rows(meta, i, r, c, rows):
    p = c * CHUNK + iota((CHUNK, 1), 0)
    return (p < rows) & ((meta[0] ^ r) * rows + p < patch_count(meta, i))


def front_rows(pad, first_block, meta, cots, wo, gu, gb, gp, put):
    rows, width = cots[0].shape[1], cots[0].shape[2]
    samples = cots[0].shape[0] - 1
    low = rows // 16 * 16
    size = samples * pad
    for b, cot in enumerate(cots):
        where = (meta[0] ^ (first_block + b)) * rows + iota((rows, 1), 0)
        for i in range(samples):
            base = b * size + i * pad
            scale = branch_scale(meta, i, samples, where)
            gb[base + low : base + pad, :] = jnp.zeros((pad - low, width), BF)
            gb[base : base + rows, :] = (cot[i].astype(F32) * scale).astype(BF)
        at = slice(b * size, (b + 1) * size)
        gp[at, :] = dot(gb[at, :], wo[...], 1, 1)
        for i in range(samples):
            for c in range(0, pad, CHUNK):
                at = slice(b * size + i * pad + c, b * size + i * pad + c + CHUNK)
                put(b, i, c, (gp[at, :] * gu[at, :].astype(F32)).astype(BF))


def matrix_rows(pad, block, cot, pm, sp):
    samples, rows = cot.shape[0] - 1, cot.shape[1]
    low = rows // 16 * 16
    sp[block * pad + low : (block + 1) * pad, :] = jnp.zeros((pad - low, sp.shape[1]), BF)
    out = dot(cot[samples, :, 0 : pm.shape[0]], pm[...], 1, 0)
    sp[block * pad : block * pad + rows, :] = out.astype(BF)


def front_body(n, pad, first_block, count, meta, *refs):
    cots, refs = refs[:count], refs[count:]
    if first_block:
        wo, gu, pm, gb, gp, gs, sp = refs
    else:
        wo, gu, gb, gp, gs, sp, pm = refs
        pm[...] = position_map(meta[0], cots[0].shape[1], pad, n, pm.shape[0])
    samples = cots[0].shape[0] - 1

    def put(b, i, c, out):
        base = (b * samples + i) * pad + c
        gs[base : base + CHUNK, :] = out

    front_rows(pad, first_block, meta, cots, wo, gu, gb, gp, put)
    for b, cot in enumerate(cots):
        matrix_rows(pad, b, cot, pm, sp)


def prepare_body(n, pad, meta, c3, wo, gu2, pm, gs0, gs1, sp0, sp1, gb, gp, gs, gmix, sp, spt):
    samples, rows = c3.shape[0] - 1, c3.shape[1]
    most = (n - 1) * pad
    sp[0 : sp0.shape[0], :] = sp0[...]
    sp[sp0.shape[0] : most, :] = sp1[...]
    matrix_rows(pad, n - 1, c3, pm, sp)
    spt[...] = jnp.transpose(sp[...].astype(F32)).astype(BF)

    half = gp.shape[1]

    def put(b, i, c, out):
        gs[most + c : most + c + CHUNK, i * half : (i + 1) * half] = out

    front_rows(pad, n - 1, meta, (c3,), wo, gu2, gb, gp, put)
    for i in range(samples):
        for r in range(n - 1):
            k, base = part(r, i, samples, pad)
            here = slice(i * half, (i + 1) * half)
            gs[r * pad : (r + 1) * pad, here] = (gs0, gs1)[k][base : base + pad, :]
    full = dot(spt[...], gs[...], 1, 0)
    for i in range(samples):
        for r in range(n):
            base = (r * samples + i) * pad
            for c in range(pad // CHUNK):
                at = slice(r * pad + c * CHUNK, r * pad + (c + 1) * CHUNK)
                out = full[at, i * half : (i + 1) * half]
                out = jnp.where(valid_rows(meta, i, r, c, rows), out, 0.0)
                gmix[base + c * CHUNK : base + (c + 1) * CHUNK, :] = out


def own_lanes(rows, seq, half):
    count = half // 128
    return jnp.concatenate([rows[pl.ds(seq * count + k, 1), :] for k in range(count)], axis=1)


def lane_sum(x):
    total = x[:, 0:128]
    for k in range(1, x.shape[1] // 128):
        total = total + x[:, k * 128 : (k + 1) * 128]
    return total


def row_sum(x):
    ones = jnp.ones((8, x.shape[1]), BF)
    high = x.astype(BF)
    low = (x - high.astype(F32)).astype(BF)
    return dot(ones, high, 1, 1) + dot(ones, low, 1, 1)


def row_sums(parts, st, pad):
    blocks = parts.shape[0] // 2
    for b in range(blocks):
        for j in range(2):
            st[2 * b + j : 2 * b + j + 1, 0:pad] = row_sum(parts[j * blocks + b])[0:1, :]


def pack_sums(st):
    x = jnp.concatenate([st[8 * k : 8 * (k + 1), :] for k in range(3)], axis=1)
    terms = []
    for _ in range(3):
        terms.append(x.astype(BF).astype(F32))
        x = x - terms[-1]
    return jnp.concatenate(terms + [jnp.zeros_like(x)], axis=0).astype(BF)


def unpack_sums(packed):
    x = packed.astype(F32)
    x = (x[16:24] + x[8:16]) + x[0:8]
    return jnp.concatenate([x[:, 128 * k : 128 * (k + 1)] for k in range(3)], axis=0)


def spatial_body(
    n, pad, meta, v0, v1, v2, gu0, gu1, gu2, dgu0, dgu1, dgu2, sp, gp0, gp1, gp2, gs, pm, gmix, g2, s2, t0, t1, t2, t3,
    prod, ghu, cols, st, edge, m1, m2, m3,
    mixed, so, tile, parts,
):
    half, rows = gp0.shape[1], PATCHES // n
    samples = gs.shape[1] // half
    gps = (gp0, gp1, gp2)
    whole = half * n
    stats, vs, gus, dgus = (t0, t1, t2, t3), (v0, v1, v2), (gu0, gu1, gu2), (dgu0, dgu1, dgu2)
    tile[...] = jnp.zeros_like(tile)
    for i in range(samples):
        for r in range(n):
            at = [2 * (i * n + (r ^ k)) for k in range(n)]
            means = [stats[k][at[k] : at[k] + 1, :] for k in range(n)]
            squares = [stats[k][at[k] + 1 : at[k] + 2, :] for k in range(n)]
            mean = ((means[0] + means[1]) + (means[2] + means[3])) / n
            spread = (squares[0] + squares[1]) + (squares[2] + squares[3])
            for k in range(n):
                spread = spread + half * (means[k] - mean) * (means[k] - mean)
            blk = 2 * (i * n + r)
            tile[blk : blk + 1, :] = mean
            tile[blk + 1 : blk + 2, :] = lax.rsqrt(spread / whole + EPSILON)
    cols[...] = jnp.transpose(tile[...])
    gain, shift = own_lanes(g2, meta[0], half), own_lanes(s2, meta[0], half)
    for i in range(samples):
        for r in range(n):
            k, base = part(r, i, samples, pad)
            first = (r * samples + i) * pad
            blk = 2 * (i * n + r)
            for c in range(pad // CHUNK):
                here = slice(c * CHUNK, (c + 1) * CHUNK)
                mean, inverse = cols[here, blk : blk + 1], cols[here, blk + 1 : blk + 2]
                standard = (vs[k][base + c * CHUNK : base + (c + 1) * CHUNK, :] - mean) * inverse
                out = jnp.where(valid_rows(meta, i, r, c, rows), standard * gain + shift, 0.0)
                if r == 0 and (c + 1) * CHUNK == pad:
                    p = c * CHUNK + iota((CHUNK, 1), 0)
                    out = jnp.where(p >= pad - 2, 1.0, out)
                at = slice(r * pad + c * CHUNK, r * pad + (c + 1) * CHUNK)
                mixed[at, i * half : (i + 1) * half] = out.astype(BF)
                t = gmix[first + c * CHUNK : first + (c + 1) * CHUNK, :] * gain
                parts[i * n + r, here, :] = lane_sum(t)
                parts[samples * n + i * n + r, here, :] = lane_sum(t * standard)
    so[...] = dot(sp[...], mixed[...], 1, 0)
    row_sums(parts, st, pad)
    total = dot(gs[...], mixed[...], 1, 1)
    placed = dot(total.astype(BF), pm[...], 1, 1).astype(BF)
    packed = pack_sums(st)
    edge[...] = placed[0:pad, :]
    for r, message in enumerate((m1, m2, m3), 1):
        message[0:pad, :] = placed[r * pad : (r + 1) * pad, :]
        message[pad:, :] = packed
    for i in range(samples):
        for r in range(n):
            k, base = part(r, i, samples, pad)
            first = (r * samples + i) * pad
            for c in range(0, pad, CHUNK):
                src = slice(base + c, base + c + CHUNK)
                at = slice(first + c, first + c + CHUNK)
                s = so[r * pad + c : r * pad + c + CHUNK, i * half : (i + 1) * half]
                prod[at, :] = (gus[k][src, :].astype(F32) * s).astype(BF)
                ghu[at, :] = (gps[k][src, :] * s * dgus[k][src, :].astype(F32)).astype(BF)


def weight_sum(lefts, rights):
    total = None
    for left, right in zip(lefts, rights):
        term = dot(left, right, 0, 0)
        total = term if total is None else total + term
    return total


def store_shards(dp, whole, outs, base):
    shard = whole.shape[0] // 4
    for rho, out in enumerate(outs):
        here = whole[rows_at(((dp ^ rho) & 3) * shard, shard, 16), :]
        out[base : base + shard, :] = here.astype(BF)


def norm_sums(w, grad_w, grads):
    columns = None
    for c in range(0, grads.shape[0], CHUNK):
        g = grads[c : c + CHUNK, :].astype(F32)
        columns = g if columns is None else columns + g
    columns = jnp.sum(columns, axis=0, keepdims=True)
    first, second = [], []
    for c in range(w.shape[0] // CHUNK):
        at = slice(c * CHUNK, (c + 1) * CHUNK)
        x = w[at, :].astype(F32)
        first.append(lane_sum(x * grad_w[at, :]))
        second.append(lane_sum(x * columns))
    first = row_sum(jnp.concatenate(first, axis=0))
    second = row_sum(jnp.concatenate(second, axis=0))
    return jnp.where(iota(first.shape, 0) == 0, first, second)


def flip_body(n0, n1, n2, out, whole):
    base = 0
    for ref in (n0, n1, n2):
        whole[base : base + ref.shape[0], :] = ref[...]
        base += ref.shape[0]
    out[...] = jnp.transpose(whole[...])


def weights_body(meta, prod, gb0, gb1, gb2, ghu, flipped, s0, s1, s2, s3, uw, ow):
    groups = group_rows(prod.shape[0] // 4)
    outs = (s0, s1, s2, s3)
    ow[...] = weight_sum([g[...] for g in (gb0, gb1, gb2)], [prod[at, :] for at in groups])
    uw[...] = dot(flipped[...], ghu[...], 1, 0)
    store_shards(meta[1], ow, outs, 0)
    store_shards(meta[1], uw, outs, ow.shape[0] // 4)


def sums_body(w, grad_w, grads, out):
    out[...] = norm_sums(w, grad_w, grads)


EXTRA = 32


def back_body(
    n, pad, meta, gmix, v0, v1, v2, dgv0, dgv1, dgv2, cols, st, edge0, m1, m2, m3, g1, s1, g2, flipped,
    wv, first_sums,
    ghv, w0, w1, w2, w3,
    tile, col, vw, acc, extra,
):
    samples, half = gmix.shape[0] // (n * pad), gmix.shape[1]
    width = wv.shape[0]
    messages, vs, dgvs = (m1, m2, m3), (v0, v1, v2), (dgv0, dgv1, dgv2)
    stats = [st[...]] + [unpack_sums(m[pad:, :]) for m in messages]
    tile[...] = jnp.zeros_like(tile)
    for i in range(samples):
        for r in range(n):
            blk = 2 * (i * n + r)
            terms = [
                stats[k][2 * (i * n + (r ^ k)) : 2 * (i * n + (r ^ k)) + 2, :] for k in range(n)
            ]
            tile[blk : blk + 2, :] = ((terms[0] + terms[1]) + (terms[2] + terms[3])) / (half * n)
    col[...] = jnp.transpose(tile[...])
    gain = own_lanes(g2, meta[0], half)
    acc[...] = jnp.zeros_like(acc)
    for i in range(samples):
        for r in range(n):
            k, base = part(r, i, samples, pad)
            row = (r * samples + i) * pad
            blk = 2 * (i * n + r)
            for c in range(pad // CHUNK):
                here = slice(c * CHUNK, (c + 1) * CHUNK)
                at = slice(row + c * CHUNK, row + (c + 1) * CHUNK)
                src = slice(base + c * CHUNK, base + (c + 1) * CHUNK)
                mean, inverse = cols[here, blk : blk + 1], cols[here, blk + 1 : blk + 2]
                first, second = col[here, blk : blk + 1], col[here, blk + 1 : blk + 2]
                standard = (vs[k][src, :] - mean) * inverse
                g = gmix[at, :]
                out = inverse * (g * gain - first - standard * second)
                ghv[at, :] = (out * dgvs[k][src, :].astype(F32)).astype(BF)
                acc[0] += g * standard
                acc[1] += g
    vw[...] = dot(flipped[...], ghv[...], 1, 0)
    sums = first_sums[...] + norm_sums(wv, vw, ghv)
    shift_one = sums[1:2, :]
    gain_one = (sums[0:1, :] - s1[...] * shift_one) / g1[...]
    edge = edge0[...].astype(F32)
    for m in messages:
        edge = edge + m[0:pad, :].astype(F32)
    size = pad // 4
    extra[...] = jnp.zeros_like(extra)
    for k in range(4):
        extra[k, 0:size, :] = edge[k * size : (k + 1) * size, :]
    extra[0, size : size + 1, :] = jnp.sum(acc[0], axis=0, keepdims=True)
    extra[1, size : size + 1, :] = jnp.sum(acc[1], axis=0, keepdims=True)
    for k, row in ((2, gain_one), (3, shift_one)):
        extra[k, size : size + 1, :] = row[:, 0:half]
        extra[k, size + 1 : size + 2, 0 : width - half] = row[:, half:]
    outs = (w0, w1, w2, w3)
    store_shards(meta[1], vw, outs, 0)
    shard = vw.shape[0] // 4
    for rho, out in enumerate(outs):
        out[shard:, :] = extra[(meta[1] ^ rho) & 3].astype(BF)


def rows_body(n, pad, prod, wo, ghu, ghv, wu, wv, keep_a, send_a, keep_b, send_b):
    samples, rows = keep_a.shape[0] // 2, keep_a.shape[1]
    for r, out in enumerate((keep_a, send_a, keep_b, send_b)):
        at = slice(r * samples * pad, (r + 1) * samples * pad)
        branch = dot(prod[at, :], wo[...], 1, 0)
        grad = dot(ghu[at, :], wu[...], 1, 1) + dot(ghv[at, :], wv[...], 1, 1)
        for i in range(samples):
            out[i] = branch[i * pad : i * pad + rows, :].astype(BF)
            out[samples + i] = grad[i * pad : i * pad + rows, :].astype(BF)


def finish_rows_body(meta, tok, cot, keep, got_a, got_b, g1, output, grad_tokens):
    samples, rows = tok.shape[0], tok.shape[1]
    gain = g1[...]
    p = meta[0] * rows + iota((rows, 1), 0)
    for i in range(samples):
        x = tok[i].astype(F32)
        total = keep[i].astype(F32) + got_a[i].astype(F32) + got_b[i].astype(F32)
        output[i] = (x + branch_scale(meta, i, samples, p) * total).astype(BF)
        center = x - jnp.mean(x, axis=-1, keepdims=True)
        inverse = lax.rsqrt(jnp.mean(center * center, axis=-1, keepdims=True) + EPSILON)
        standard = center * inverse
        k = samples + i
        t = (keep[k].astype(F32) + got_a[k].astype(F32) + got_b[k].astype(F32)) * gain
        first = jnp.mean(t, axis=-1, keepdims=True)
        second = jnp.mean(t * standard, axis=-1, keepdims=True)
        grad = cot[i].astype(F32) + inverse * (t - first - standard * second)
        grad_tokens[i] = grad.astype(BF)


def sources(meta):
    seq, shard = meta[0], meta[1] & 3
    out = []
    for flip in (0, 1):
        s = seq ^ flip
        core = s & 1
        out += [
            (shard, s),
            (shard ^ (1 - core), s ^ (2 * core)),
            (shard ^ core, s ^ (2 * (1 - core))),
            (shard ^ 1, s ^ 2),
        ]
    return out


def place_first_body(half, meta, *refs):
    pieces = refs[:8]
    w_in, w_out, wide, tall, sems = refs[8:]
    shard = wide.shape[1]
    copies = []
    for k, (group, seq) in enumerate(sources(meta)):
        for e in range(2):
            slot = 2 * k + e
            row = (group ^ (2 * e)) * shard
            columns = rows_at(seq * half, half, 128)
            tall[slot] = jnp.transpose(pieces[k][e, 0:shard, :].astype(F32))
            target = w_out.at[columns, rows_at(row, shard, 128)]
            copies.append(pltpu.make_async_copy(tall.at[slot], target, sems.at[2 * slot]))
            copies[-1].start()
            wide[slot] = pieces[k][e, shard:, :].astype(F32)
            target = w_in.at[rows_at(row, shard, 16), columns]
            copies.append(pltpu.make_async_copy(wide.at[slot], target, sems.at[2 * slot + 1]))
            copies[-1].start()
    for copy in copies:
        copy.wait()


def place_v(half, gate, meta, pieces, which, w_in, wide, sems):
    shard = wide.shape[1]
    copies = []
    origins = sources(meta)
    for piece, k in zip(pieces, which):
        group, seq = origins[k]
        for e in range(2):
            slot = len(copies)
            wide[slot] = piece[e, 0:shard, :].astype(F32)
            columns = rows_at(gate + seq * half, half, 128)
            target = w_in.at[rows_at((group ^ (2 * e)) * shard, shard, 16), columns]
            copies.append(pltpu.make_async_copy(wide.at[slot], target, sems.at[slot]))
            copies[-1].start()
    return copies


def place_most_body(half, gate, which, meta, *refs):
    *pieces, _, w_in, wide, sems = refs
    for copy in place_v(half, gate, meta, pieces, which, w_in, wide, sems):
        copy.wait()


def place_last_body(half, gate, which, meta, *refs):
    pieces = refs[:8]
    w_in, spatial, bias, gain_one, shift_one, gain_two, shift_two, wide, edge, norms, sems = refs[10:]
    shard = wide.shape[1]
    rows, patches = spatial.shape
    size = edge.shape[0] // 4
    core = meta[0] & 1
    copies = place_v(half, gate, meta, [pieces[k] for k in which], which, w_in, wide, sems)
    small = []
    for k, (group, seq) in enumerate(sources(meta)):
        for e in range(2):
            at = group ^ (2 * e)
            rest = pieces[k][e, shard:, :].astype(F32)
            small.append((at, rest[0:size]))
            norms[at, seq] = rest[size:]
    for e in range(2):
        at, own = small[e]
        edge[rows_at(at * size, size, 8), :] = own
        at = (meta[1] & 3) ^ 1 ^ (2 * e)
        edge[rows_at(at * size, size, 8), :] = jnp.where(core == 0, small[2 + e][1], small[4 + e][1])
    spatial[...] = edge[0:rows, 0:patches]
    first = patches // 128 * 128
    tail = edge[0:rows, first:]
    column = jnp.sum(
        jnp.where(iota(tail.shape, 1) == patches - first, tail, 0.0), axis=1, keepdims=True
    )
    diagonal = iota((rows, rows), 0) == iota((rows, rows), 1)
    bias[...] = jnp.sum(jnp.where(diagonal, column, 0.0), axis=0)
    for at, out in ((2, gain_one), (3, shift_one)):
        total = (norms[at, 0] + norms[at, 1]) + (norms[at, 2] + norms[at, 3])
        out[0:half] = total[0, :]
        out[half:] = total[1, 0 : out.shape[0] - half]
    for at, out in ((0, gain_two), (1, shift_two)):
        for j in range(4):
            out[j * half : (j + 1) * half] = norms[at, j, 0, :]
    for copy in copies:
        copy.wait()


def solution(mesh):
    n, m = mesh.shape["seq"], mesh.shape["dp"]

    def over_seq(x, flip):
        return lax.ppermute(x, "seq", [(i, i ^ flip) for i in range(n)])

    def over_dp(x, flip):
        return lax.ppermute(x, "dp", [(i, i ^ flip) for i in range(m)])

    def mixed_axes(x, core_of_x):
        pairs = []
        for d in range(m):
            for s in range(n):
                other = (d ^ 1, s) if s & 1 == core_of_x else (d, s ^ 2)
                pairs.append((d * n + s, other[0] * n + other[1]))
        return lax.ppermute(x, ("dp", "seq"), pairs)

    def add(*terms):
        total = terms[0].astype(F32)
        for t in terms[1:]:
            total = total + t.astype(F32)
        return total.astype(BF)

    def pair_up(*terms):
        return jnp.stack(terms)

    def ordered():
        last = []

        def step(body, *ins):
            if last:
                ins, _ = lax.optimization_barrier((ins, last[0]))
            out = body(*ins) if body else ins[0]
            last[:] = [jax.tree.leaves(out)[0]]
            return out

        return step

    def shards(
        tokens,
        res_class,
        skip_mask,
        w_in,
        w_out,
        spatial,
        spatial_bias,
        gain_one,
        shift_one,
        gain_two,
        shift_two,
        cotangent,
    ):
        samples, rows, width = tokens.shape
        gate = w_out.shape[0]
        half = gate // n
        pad = round_up(rows + 2, 16)
        full = n * pad
        columns = round_up(n * rows + 2, 128)
        seq, dp = lax.axis_index("seq"), lax.axis_index("dp")
        meta = jnp.concatenate([seq[None], dp[None], res_class, skip_mask]).astype(jnp.int32)
        step = ordered()

        def tick(clock):
            return call(tick_body, [shape_of(clock.shape, F32)], [clock], flops=4 * 10**9, name="tick")[0]

        big_bf, big_f32 = (shape_of((samples * full, half), d) for d in (BF, F32))
        images = shape_of((full, samples * half), BF)
        shard = width // 4
        square = shape_of((round_up(samples * 2 * n, 8), 128), F32)

        t0 = tokens
        t2 = over_seq(t0, 2)
        t1 = over_seq(t0, 1)
        high = lax.reduce_precision(spatial_bias, 8, 7)
        side = jnp.stack([high, spatial_bias - high], axis=1).astype(BF)
        packed = jnp.concatenate([spatial, side], axis=1)
        packed = jnp.pad(packed, ((0, 0), (0, width - packed.shape[1])))
        c0 = jnp.concatenate([cotangent, packed[None]])
        c2 = over_seq(c0, 2)
        wu = lax.dynamic_slice(w_in, (0, seq * half), (width, half))
        wv = lax.dynamic_slice(w_in, (0, gate + seq * half), (width, half))
        wo = lax.dynamic_slice(w_out, (seq * half, 0), (half, width))
        g1, s1 = gain_one[None], shift_one[None]
        g2, s2 = gain_two.reshape(-1, 128), shift_two.reshape(-1, 128)
        meta, wu, wv, wo, c0, t1 = lax.optimization_barrier((meta, wu, wv, wo, c0, t1))
        c1 = over_seq(c0, 1)

        n0, gu0, dgu0, v0, dgv0, st = step(
            lambda *a: project(pad, 0, a[:2], *a[2:]), t0, t1, g1, s1, wu, wv
        )
        t2 = step(None, t2)
        t3 = over_seq(t2, 1)
        n1, gu1, dgu1, v1, dgv1, st = step(
            lambda *a: project(pad, 2, a[:1], *a[1:]), t2, g1, s1, wu, wv, st
        )
        n2, gu2, dgu2, v2, dgv2, st = step(
            lambda *a: project(pad, 3, a[:1], *a[1:]), t3, g1, s1, wu, wv, st
        )
        normed = [n0, n1, n2]
        stats = [st] + [over_seq(st, k) for k in range(1, n)]

        def front(first_block, count, *ins):
            def shape(columns, dtype):
                return shape_of((count * samples * pad, columns), dtype)

            outs = [shape(width, BF), shape(half, F32), shape(half, BF)]
            outs.append(shape_of((count * pad, full), BF))
            return call(
                functools.partial(front_body, n, pad, first_block, count),
                outs + ([] if first_block else [shape_of((columns, full), BF)]),
                ins,
                specs=[SM] + [VM] * (len(ins) - 1),
                name="front",
            )

        gb0, gp0, gs0, sp0, pm = step(functools.partial(front, 0, 2), meta, c0, c1, wo, gu0)

        def flip(*ins):
            return call(
                flip_body,
                [shape_of((width, samples * full), BF)],
                ins,
                [pltpu.VMEM((samples * full, width), BF)],
                name="flip",
            )

        (flipped,) = step(flip, *normed)
        stats = step(None, stats)
        c2 = step(None, c2)
        c3 = over_seq(c2, 1)
        gb1, gp1, gs1, sp1 = step(functools.partial(front, 2, 1), meta, c2, wo, gu1, pm)

        def prepare(*ins):
            square_bf = shape_of((full, full), BF)
            last = [shape_of((samples * pad, c), d) for c, d in ((width, BF), (half, F32))]
            return call(
                functools.partial(prepare_body, n, pad),
                [*last, images, big_f32, square_bf],
                ins,
                [pltpu.VMEM((full, full), BF)],
                specs=[SM] + [VM] * (len(ins) - 1),
                name="prepare",
            )

        gb2, gp2, gs, gmix, sp = step(prepare, meta, c3, wo, gu2, pm, gs0, gs1, sp0, sp1)

        def spatial_unit(*ins):
            message = shape_of((pad + 32, columns), BF)
            return call(
                functools.partial(spatial_body, n, pad),
                [big_bf, big_bf, shape_of((128, 128), F32), square, shape_of((pad, columns), BF)]
                + [message] * (n - 1),
                ins,
                [
                    pltpu.VMEM((full, samples * half), BF),
                    pltpu.VMEM((full, samples * half), F32),
                    pltpu.VMEM((128, 128), F32),
                    pltpu.VMEM((2 * samples * n, pad, 128), F32),
                ],
                specs=[SM] + [VM] * (len(ins) - 1),
                name="spatial",
            )

        clock = jnp.zeros((8, 128), F32)
        prod, ghu, cols, st2, edge, *messages = step(
            spatial_unit, meta, v0, v1, v2, gu0, gu1, gu2, dgu0, dgu1, dgu2, sp, gp0, gp1, gp2, gs, pm,
            gmix, g2, s2, *stats,
        )
        messages = [over_seq(x, k) for k, x in enumerate(messages, 1)]

        def weights(*ins):
            return call(
                weights_body,
                [shape_of((2 * shard, half), BF)] * 4 + [shape_of((width, half), F32)],
                ins,
                [pltpu.VMEM((width, half), F32)],
                specs=[SM] + [VM] * (len(ins) - 1),
                name="weights",
            )

        def norm_shares(*ins):
            return call(sums_body, [shape_of((8, width), F32)], ins, name="norm_shares")

        def back(*ins):
            return call(
                functools.partial(back_body, n, pad),
                [big_bf] + [shape_of((shard + EXTRA, half), BF)] * 4,
                ins,
                [
                    pltpu.VMEM((128, 128), F32),
                    pltpu.VMEM((128, 128), F32),
                    pltpu.VMEM((width, half), F32),
                    pltpu.VMEM((2, CHUNK, half), F32),
                    pltpu.VMEM((4, EXTRA, half), F32),
                ],
                specs=[SM] + [VM] * (len(ins) - 1),
                name="back",
            )

        def rows_out(*ins):
            shape = shape_of((2 * samples, rows, width), BF)
            return call(functools.partial(rows_body, n, pad), [shape] * 4, ins, name="rows_out")

        def finish_rows(*ins):
            shape = shape_of(tokens.shape, BF)
            return call(
                finish_rows_body, [shape, shape], ins, specs=[SM] + [VM] * 6, name="finish_rows"
            )

        def place_first(*ins):
            return call(
                functools.partial(place_first_body, half),
                [shape_of((width, 2 * gate), F32), shape_of((gate, width), F32)],
                ins,
                [
                    pltpu.VMEM((16, shard, half), F32),
                    pltpu.VMEM((16, half, shard), F32),
                    pltpu.SemaphoreType.DMA((32,)),
                ],
                specs=[SM] + [VM] * 8,
                out_specs=[HB] * 2,
                name="place_first",
            )

        def place_most(which, *ins):
            return call(
                functools.partial(place_most_body, half, gate, which),
                [shape_of((width, 2 * gate), F32)],
                ins,
                [
                    pltpu.VMEM((2 * len(which), shard, half), F32),
                    pltpu.SemaphoreType.DMA((2 * len(which),)),
                ],
                specs=[SM] + [VM] * len(which) + [HB],
                out_specs=[HB],
                input_output_aliases={1 + len(which): 0},
                name="place_most",
            )

        def place_last(which, *ins):
            one, two = shape_of((width,), F32), shape_of((gate,), F32)
            small = [shape_of((rows, n * rows), F32), shape_of((rows,), F32), one, one, two, two]
            return call(
                functools.partial(place_last_body, half, gate, which),
                [shape_of((width, 2 * gate), F32)] + small,
                ins,
                [
                    pltpu.VMEM((2 * len(which), shard, half), F32),
                    pltpu.VMEM((pad, columns), F32),
                    pltpu.VMEM((4, n, EXTRA - pad // 4, half), F32),
                    pltpu.SemaphoreType.DMA((2 * len(which),)),
                ],
                specs=[SM] + [VM] * 8 + [HB, VM],
                out_specs=[HB] + [VM] * 6,
                input_output_aliases={9: 0},
                name="place_last",
            )

        def twin(x):
            return over_seq(x, 1)

        x = dict(messages=messages, clock=clock)

        def ev_tick():
            x["clock"] = step(tick, x["clock"])

        def reduce_start(key, shards):
            x[key] = shards[0]
            for rho in range(1, 4):
                x[f"{key}{rho}"] = over_dp(shards[rho], rho)

        def ev_weights():
            *x["a_shards"], x["uw"] = step(weights, meta, prod, gb0, gb1, gb2, ghu, flipped)

        def ev_a_send():
            reduce_start("a", step(None, x["a_shards"]))

        def ev_sums():
            (x["sums"],) = step(norm_shares, wu, x["uw"], ghu)

        def ev_stats():
            x["messages"] = step(None, x["messages"])

        def ev_back():
            x["ghv"], *x["v_shards"] = step(
                back, meta, gmix, v0, v1, v2, dgv0, dgv1, dgv2, cols, st2, edge, *x["messages"], g1, s1,
                g2, flipped, wv, x["sums"],
            )

        def ev_v_send():
            reduce_start("v", step(None, x["v_shards"]))

        def ev_rows():
            x["r_a"], send_a, x["r_b"], send_b = step(rows_out, prod, wo, ghu, x["ghv"], wu, wv)
            x["r_got"], x["r_got_b"] = twin(send_a), twin(send_b)

        def ev_rows_core():
            x["r_got"], x["r_got_b"] = step(None, (x["r_got"], x["r_got_b"]))
            x["r_last"] = over_seq(step(add, x["r_b"], x["r_got_b"]), 2)

        def ev_finish():
            x["output"], x["grad_tokens"] = step(
                finish_rows, meta, t0, c0, x["r_a"], x["r_got"], x["r_last"], g1
            )

        def ev_rs(k):
            x[k] = step(add, x[k], x[k + "1"], x[k + "2"], x[k + "3"])
            x[k + "z"] = over_dp(x[k], 4) if m > 4 else None

        def ev_z2(k):
            flip = 8
            while flip <= m:
                x[k] = step(add, x[k], x[k + "z"])
                if flip < m:
                    x[k + "z"] = over_dp(x[k], flip)
                flip *= 2
            x[k + "z"] = over_dp(x[k], 2)

        def ev_pair(k):
            x[k + "p0"] = step(pair_up, x[k], x[k + "z"])
            x[k + "p1"], x[k + "p2"] = mixed_axes(x[k + "p0"], 0), mixed_axes(x[k + "p0"], 1)

        def ev_mark(k):
            x[k + "p1"], x[k + "p2"] = step(None, (x[k + "p1"], x[k + "p2"]))
            x[k + "p3"] = mixed_axes(x[k + "p1"], 1)

        def ev_third(k):
            x[k + "p3"] = step(None, x[k + "p3"])

        def ev_twin(k, j):
            x[f"{k}q{j}"] = twin(x[f"{k}p{j}"])

        def ev_got(k, j):
            x[f"{k}q{j}"] = step(None, x[f"{k}q{j}"])

        def ev_place_first():
            ins = [x[f"ap{j}"] for j in range(4)] + [x[f"aq{j}"] for j in range(4)]
            x["w_in"], x["w_out"] = step(place_first, meta, *ins)

        def ev_place_most():
            which = (0, 1, 2, 4, 5, 6)
            ins = [x[f"v{'pq'[k // 4]}{k % 4}"] for k in which]
            (x["w_in"],) = step(functools.partial(place_most, which), meta, *ins, x["w_in"])

        def ev_place_last():
            ins = [x[f"vp{j}"] for j in range(4)] + [x[f"vq{j}"] for j in range(4)]
            x["w_in"], x["spatial"], *x["small"] = step(
                functools.partial(place_last, (3, 7)), meta, *ins, x["w_in"], x["clock"]
            )

        events = dict(
            weights=ev_weights, sums=ev_sums, stats=ev_stats, back=ev_back,
            rows=ev_rows, rows_core=ev_rows_core, finish=ev_finish,
            place_first=ev_place_first, place_last=ev_place_last, place_most=ev_place_most,
            a_send=ev_a_send, v_send=ev_v_send, tick=ev_tick,
        )
        for k in ("a", "v"):
            for name, f in (("rs", ev_rs), ("z2", ev_z2), ("pair", ev_pair), ("mark", ev_mark), ("third", ev_third)):
                events[f"{k}_{name}"] = functools.partial(f, k)
            for j in range(4):
                events[f"{k}_twin{j}"] = functools.partial(ev_twin, k, j)
                events[f"{k}_got{j}"] = functools.partial(ev_got, k, j)
        for name in ORDER:
            events[name]()
        output, grad_tokens, grad_w_in, grad_w_out = (
            x[k] for k in ("output", "grad_tokens", "w_in", "w_out")
        )
        grad_spatial, sums = x["spatial"], x["small"]
        return (output, grad_tokens, grad_w_in, grad_w_out, grad_spatial, *sums)

    placed = (
        P("dp", "seq", None),
        P("dp"),
        P("dp"),
        P(),
        P(),
        P("seq", None),
        P("seq"),
        P(),
        P(),
        P(),
        P(),
        P("dp", "seq", None),
    )
    return jax.shard_map(
        shards,
        mesh=mesh,
        in_specs=placed,
        out_specs=(
            P("dp", "seq", None),
            P("dp", "seq", None),
            P(),
            P(),
            P("seq", None),
            P("seq"),
            P(),
            P(),
            P(),
            P(),
        ),
        check_vma=False,
    )
```

```python
import functools

import jax
import jax.numpy as jnp
from jax import lax
from jax.experimental import pallas as pl
from jax.experimental.pallas import tpu as pltpu
from jax.sharding import PartitionSpec as P

PATCHES = 324
SMALL_P = 100
MID_P = 196

EPSILON = 1e-05
SURVIVAL = 0.9

BF = jnp.bfloat16
F32 = jnp.float32
CHUNK = 16
VM = pl.BlockSpec(memory_space=pltpu.VMEM)
SM = pl.BlockSpec(memory_space=pltpu.SMEM)
HB = pl.BlockSpec(memory_space=pltpu.HBM)


ORDER = (
    "weights", "a_send", "tick", "stats", "sums", "back", "v_send", "rows", "a_rs", "tick", "rows_core", "v_rs",
    "a_z2", "v_z2", "a_pair", "tick", "v_pair", "finish", "a_mark", "tick", "v_mark", "tick", "a_twin0", "a_twin1",
    "a_twin2", "place_head", "a_third", "a_twin3", "v_third", "v_twin3", "v_twin0", "v_twin1", "v_twin2", "tick",
    "place_most", "place_last",
)


def round_up(size, multiple):
    return -(-size // multiple) * multiple


def dot(a, b, ca, cb):
    return lax.dot_general(a, b, (((ca,), (cb,)), ((), ())), preferred_element_type=F32)


def iota(shape, axis):
    return lax.broadcasted_iota(jnp.int32, shape, axis)


def rows_at(start, size, multiple):
    return pl.ds(pl.multiple_of(start, multiple), size)


def call(body, outs, ins, scratch=(), specs=None, out_specs=None, flops=1, **more):
    return pl.pallas_call(
        body,
        out_shape=outs,
        in_specs=specs if specs is not None else [VM] * len(ins),
        out_specs=out_specs if out_specs is not None else [VM] * len(outs),
        scratch_shapes=list(scratch),
        compiler_params=pltpu.CompilerParams(vmem_limit_bytes=20 * 2**20),
        cost_estimate=pl.CostEstimate(flops=flops, bytes_accessed=1, transcendentals=0),
        **more,
    )(*ins)


def shape_of(shape, dtype):
    return jax.ShapeDtypeStruct(shape, dtype)


def add_body(*refs):
    total = refs[0][...].astype(F32)
    for ref in refs[1:-1]:
        total = total + ref[...].astype(F32)
    refs[-1][...] = total.astype(BF)


def tick_body(clock, out):
    out[...] = clock[...] + 1.0


def pair_body(a, b, out):
    out[0] = a[...]
    out[1] = b[...]


def project_body(pad, first_block, *refs):
    refs = list(refs)
    n_tok = len(refs) - 13 - (1 if first_block else 0)
    toks, refs = refs[:n_tok], refs[n_tok:]
    g1, s1, wu, wv = refs[:4]
    refs = refs[4:]
    if first_block:
        st_in, refs = refs[0], refs[1:]
    normed, gu, dgu, v, dgv, st, xs, hid, tile = refs
    samples, rows, width = toks[0].shape
    half = wu.shape[1]
    size = samples * pad
    found = [jnp.zeros((CHUNK, 128), F32)] * (128 // CHUNK)
    low = rows // 8 * 8
    gain, shift = g1[...], s1[...]
    for b, tok in enumerate(toks):
        for i in range(samples):
            base = (b * samples + i) * pad
            xs[base + low : base + pad, :] = jnp.zeros((pad - low, width), F32)
            xs[base : base + rows, :] = tok[i].astype(F32)
            for c in range(base, base + pad, CHUNK):
                x = xs[c : c + CHUNK, :]
                center = x - jnp.mean(x, axis=-1, keepdims=True)
                inverse = lax.rsqrt(jnp.mean(center * center, axis=-1, keepdims=True) + EPSILON)
                normed[c : c + CHUNK, :] = (center * inverse * gain + shift).astype(BF)
        at = slice(b * size, (b + 1) * size)
        hid[at, 0:half] = dot(normed[at, :], wu[...], 1, 0)
        hid[at, half:] = dot(normed[at, :], wv[...], 1, 0)
    c0 = 0.7978845608028654
    c1 = 0.7978845608028654 * 0.044715

    def gelu_pair(h):
        a = (c1 * h) * h
        s = 0.5 + 0.5 * jnp.tanh(h * (c0 + a))
        g = h * s
        return g, s + (2.0 * g) * (1.0 - s) * (c0 + 3.0 * a)

    lane = iota((CHUNK, 128), 1)
    for b in range(len(toks)):
        for i in range(samples):
            base = (b * samples + i) * pad
            blk = 2 * (i * 4 + first_block + b)
            for c in range(pad // CHUNK):
                at = slice(base + c * CHUNK, base + (c + 1) * CHUNK)
                g, d = gelu_pair(hid[at, 0:half])
                gu[at, :] = g.astype(BF)
                dgu[at, :] = d.astype(BF)
                g, d = gelu_pair(hid[at, half:])
                v[at, :] = g
                dgv[at, :] = d.astype(BF)
                mean = jnp.mean(g, axis=-1, keepdims=True)
                center = g - mean
                square = jnp.sum(center * center, axis=-1, keepdims=True)
                found[c] = jnp.where(
                    lane == blk, mean, jnp.where(lane == blk + 1, square, found[c])
                )
    for c, part_found in enumerate(found):
        tile[c * CHUNK : (c + 1) * CHUNK, :] = part_found
    flipped = jnp.transpose(tile[...])[0 : st.shape[0], :]
    st[...] = flipped + st_in[...] if first_block else flipped


def project(pad, first_block, toks, g1, s1, wu, wv, st_in=None):
    samples, rows, width = toks[0].shape
    half = wu.shape[1]
    n_rows = len(toks) * samples * pad
    outs = [
        shape_of((n_rows, width), BF),
        shape_of((n_rows, half), BF),
        shape_of((n_rows, half), BF),
        shape_of((n_rows, half), F32),
        shape_of((n_rows, half), BF),
        shape_of((round_up(samples * 8, 8), 128), F32),
    ]
    scratch = [
        pltpu.VMEM((n_rows, width), F32),
        pltpu.VMEM((n_rows, 2 * half), F32),
        pltpu.VMEM((128, 128), F32),
    ]
    ins = [*toks, g1, s1, wu, wv] + ([st_in] if first_block else [])
    return call(
        functools.partial(project_body, pad, first_block),
        outs,
        ins,
        scratch,
        name="project",
    )


GROUPS = ((0, 1), (2,), (3,))


def part(r, i, samples, pad):
    for k, blocks in enumerate(GROUPS):
        if r in blocks:
            return k, ((r - blocks[0]) * samples + i) * pad


def group_rows(size):
    return [slice(blocks[0] * size, (blocks[-1] + 1) * size) for blocks in GROUPS]


def position_map(seq, rows, pad, n, columns):
    a = iota((columns, n * pad), 0)
    j = iota((columns, n * pad), 1)
    r = jnp.zeros_like(j)
    for k in range(1, n):
        r = r + (j >= k * pad).astype(jnp.int32)
    q = j - r * pad
    hit = (a == (r ^ seq) * rows + q) & (q < rows)
    hit = hit | ((a == n * rows) & (j == pad - 1)) | ((a == n * rows + 1) & (j == pad - 2))
    return jnp.where(hit, 1.0, 0.0).astype(BF)


def patch_count(meta, i):
    kind = meta[2 + i]
    return jnp.where(kind == 0, SMALL_P, jnp.where(kind == 1, MID_P, PATCHES))


def branch_scale(meta, i, samples, where):
    keep = jnp.where(where < patch_count(meta, i), meta[2 + samples + i], 0)
    return keep.astype(F32) / SURVIVAL


def valid_rows(meta, i, r, c, rows):
    p = c * CHUNK + iota((CHUNK, 1), 0)
    return (p < rows) & ((meta[0] ^ r) * rows + p < patch_count(meta, i))


def front_rows(pad, first_block, meta, cots, wo, gu, gb, gp, put):
    rows, width = cots[0].shape[1], cots[0].shape[2]
    samples = cots[0].shape[0] - 1
    low = rows // 16 * 16
    size = samples * pad
    for b, cot in enumerate(cots):
        where = (meta[0] ^ (first_block + b)) * rows + iota((rows, 1), 0)
        for i in range(samples):
            base = b * size + i * pad
            scale = branch_scale(meta, i, samples, where)
            gb[base + low : base + pad, :] = jnp.zeros((pad - low, width), BF)
            gb[base : base + rows, :] = (cot[i].astype(F32) * scale).astype(BF)
        at = slice(b * size, (b + 1) * size)
        gp[at, :] = dot(gb[at, :], wo[...], 1, 1)
        for i in range(samples):
            for c in range(0, pad, CHUNK):
                at = slice(b * size + i * pad + c, b * size + i * pad + c + CHUNK)
                put(b, i, c, (gp[at, :] * gu[at, :].astype(F32)).astype(BF))


def matrix_rows(pad, block, cot, pm, sp):
    samples, rows = cot.shape[0] - 1, cot.shape[1]
    low = rows // 16 * 16
    sp[block * pad + low : (block + 1) * pad, :] = jnp.zeros((pad - low, sp.shape[1]), BF)
    out = dot(cot[samples, :, 0 : pm.shape[0]], pm[...], 1, 0)
    sp[block * pad : block * pad + rows, :] = out.astype(BF)


def front_body(n, pad, first_block, count, meta, *refs):
    cots, refs = refs[:count], refs[count:]
    if first_block:
        wo, gu, pm, gb, gp, gs, sp = refs
    else:
        wo, gu, gb, gp, gs, sp, pm = refs
        pm[...] = position_map(meta[0], cots[0].shape[1], pad, n, pm.shape[0])
    samples = cots[0].shape[0] - 1

    def put(b, i, c, out):
        base = (b * samples + i) * pad + c
        gs[base : base + CHUNK, :] = out

    front_rows(pad, first_block, meta, cots, wo, gu, gb, gp, put)
    for b, cot in enumerate(cots):
        matrix_rows(pad, b, cot, pm, sp)


def prepare_body(n, pad, meta, c3, wo, gu2, pm, gs0, gs1, sp0, sp1, gb, gp, gs, gmix, sp, spt):
    samples, rows = c3.shape[0] - 1, c3.shape[1]
    most = (n - 1) * pad
    sp[0 : sp0.shape[0], :] = sp0[...]
    sp[sp0.shape[0] : most, :] = sp1[...]
    matrix_rows(pad, n - 1, c3, pm, sp)
    spt[...] = jnp.transpose(sp[...].astype(F32)).astype(BF)

    half = gp.shape[1]

    def put(b, i, c, out):
        gs[most + c : most + c + CHUNK, i * half : (i + 1) * half] = out

    front_rows(pad, n - 1, meta, (c3,), wo, gu2, gb, gp, put)
    for i in range(samples):
        for r in range(n - 1):
            k, base = part(r, i, samples, pad)
            here = slice(i * half, (i + 1) * half)
            gs[r * pad : (r + 1) * pad, here] = (gs0, gs1)[k][base : base + pad, :]
    full = dot(spt[...], gs[...], 1, 0)
    for i in range(samples):
        for r in range(n):
            base = (r * samples + i) * pad
            for c in range(pad // CHUNK):
                at = slice(r * pad + c * CHUNK, r * pad + (c + 1) * CHUNK)
                out = full[at, i * half : (i + 1) * half]
                out = jnp.where(valid_rows(meta, i, r, c, rows), out, 0.0)
                gmix[base + c * CHUNK : base + (c + 1) * CHUNK, :] = out


def own_lanes(rows, seq, half):
    count = half // 128
    return jnp.concatenate([rows[pl.ds(seq * count + k, 1), :] for k in range(count)], axis=1)


def lane_sum(x):
    total = x[:, 0:128]
    for k in range(1, x.shape[1] // 128):
        total = total + x[:, k * 128 : (k + 1) * 128]
    return total


def row_sum(x):
    ones = jnp.ones((8, x.shape[1]), BF)
    high = x.astype(BF)
    low = (x - high.astype(F32)).astype(BF)
    return dot(ones, high, 1, 1) + dot(ones, low, 1, 1)


def row_sums(parts, st, pad):
    blocks = parts.shape[0] // 2
    for b in range(blocks):
        for j in range(2):
            st[2 * b + j : 2 * b + j + 1, 0:pad] = row_sum(parts[j * blocks + b])[0:1, :]


def pack_sums(st):
    x = jnp.concatenate([st[8 * k : 8 * (k + 1), :] for k in range(3)], axis=1)
    terms = []
    for _ in range(3):
        terms.append(x.astype(BF).astype(F32))
        x = x - terms[-1]
    return jnp.concatenate(terms + [jnp.zeros_like(x)], axis=0).astype(BF)


def unpack_sums(packed):
    x = packed.astype(F32)
    x = (x[16:24] + x[8:16]) + x[0:8]
    return jnp.concatenate([x[:, 128 * k : 128 * (k + 1)] for k in range(3)], axis=0)


def spatial_body(
    n, pad, meta, v0, v1, v2, gu0, gu1, gu2, dgu0, dgu1, dgu2, sp, gp0, gp1, gp2, gs, pm, gmix, g2, s2, t0, t1, t2, t3,
    prod, ghu, cols, st, edge, m1, m2, m3,
    mixed, so, tile, parts,
):
    half, rows = gp0.shape[1], PATCHES // n
    samples = gs.shape[1] // half
    gps = (gp0, gp1, gp2)
    whole = half * n
    stats, vs, gus, dgus = (t0, t1, t2, t3), (v0, v1, v2), (gu0, gu1, gu2), (dgu0, dgu1, dgu2)
    tile[...] = jnp.zeros_like(tile)
    for i in range(samples):
        for r in range(n):
            at = [2 * (i * n + (r ^ k)) for k in range(n)]
            means = [stats[k][at[k] : at[k] + 1, :] for k in range(n)]
            squares = [stats[k][at[k] + 1 : at[k] + 2, :] for k in range(n)]
            mean = ((means[0] + means[1]) + (means[2] + means[3])) / n
            spread = (squares[0] + squares[1]) + (squares[2] + squares[3])
            for k in range(n):
                spread = spread + half * (means[k] - mean) * (means[k] - mean)
            blk = 2 * (i * n + r)
            tile[blk : blk + 1, :] = mean
            tile[blk + 1 : blk + 2, :] = lax.rsqrt(spread / whole + EPSILON)
    cols[...] = jnp.transpose(tile[...])
    gain, shift = own_lanes(g2, meta[0], half), own_lanes(s2, meta[0], half)
    for i in range(samples):
        for r in range(n):
            k, base = part(r, i, samples, pad)
            first = (r * samples + i) * pad
            blk = 2 * (i * n + r)
            for c in range(pad // CHUNK):
                here = slice(c * CHUNK, (c + 1) * CHUNK)
                mean, inverse = cols[here, blk : blk + 1], cols[here, blk + 1 : blk + 2]
                standard = (vs[k][base + c * CHUNK : base + (c + 1) * CHUNK, :] - mean) * inverse
                out = jnp.where(valid_rows(meta, i, r, c, rows), standard * gain + shift, 0.0)
                if r == 0 and (c + 1) * CHUNK == pad:
                    p = c * CHUNK + iota((CHUNK, 1), 0)
                    out = jnp.where(p >= pad - 2, 1.0, out)
                at = slice(r * pad + c * CHUNK, r * pad + (c + 1) * CHUNK)
                mixed[at, i * half : (i + 1) * half] = out.astype(BF)
                t = gmix[first + c * CHUNK : first + (c + 1) * CHUNK, :] * gain
                parts[i * n + r, here, :] = lane_sum(t)
                parts[samples * n + i * n + r, here, :] = lane_sum(t * standard)
    so[...] = dot(sp[...], mixed[...], 1, 0)
    row_sums(parts, st, pad)
    total = dot(gs[...], mixed[...], 1, 1)
    placed = dot(total.astype(BF), pm[...], 1, 1).astype(BF)
    packed = pack_sums(st)
    edge[...] = placed[0:pad, :]
    for r, message in enumerate((m1, m2, m3), 1):
        message[0:pad, :] = placed[r * pad : (r + 1) * pad, :]
        message[pad:, :] = packed
    for i in range(samples):
        for r in range(n):
            k, base = part(r, i, samples, pad)
            first = (r * samples + i) * pad
            for c in range(0, pad, CHUNK):
                src = slice(base + c, base + c + CHUNK)
                at = slice(first + c, first + c + CHUNK)
                s = so[r * pad + c : r * pad + c + CHUNK, i * half : (i + 1) * half]
                prod[at, :] = (gus[k][src, :].astype(F32) * s).astype(BF)
                ghu[at, :] = (gps[k][src, :] * s * dgus[k][src, :].astype(F32)).astype(BF)


def weight_sum(lefts, rights):
    total = None
    for left, right in zip(lefts, rights):
        term = dot(left, right, 0, 0)
        total = term if total is None else total + term
    return total


def store_shards(dp, whole, outs, base):
    shard = whole.shape[0] // 4
    for rho, out in enumerate(outs):
        here = whole[rows_at(((dp ^ rho) & 3) * shard, shard, 16), :]
        out[base : base + shard, :] = here.astype(BF)


def norm_sums(w, grad_w, grads):
    columns = None
    for c in range(0, grads.shape[0], CHUNK):
        g = grads[c : c + CHUNK, :].astype(F32)
        columns = g if columns is None else columns + g
    columns = jnp.sum(columns, axis=0, keepdims=True)
    first, second = [], []
    for c in range(w.shape[0] // CHUNK):
        at = slice(c * CHUNK, (c + 1) * CHUNK)
        x = w[at, :].astype(F32)
        first.append(lane_sum(x * grad_w[at, :]))
        second.append(lane_sum(x * columns))
    first = row_sum(jnp.concatenate(first, axis=0))
    second = row_sum(jnp.concatenate(second, axis=0))
    return jnp.where(iota(first.shape, 0) == 0, first, second)


def flip_body(n0, n1, n2, out, whole):
    base = 0
    for ref in (n0, n1, n2):
        whole[base : base + ref.shape[0], :] = ref[...]
        base += ref.shape[0]
    out[...] = jnp.transpose(whole[...])


def weights_body(meta, prod, gb0, gb1, gb2, ghu, flipped, s0, s1, s2, s3, uw, ow):
    groups = group_rows(prod.shape[0] // 4)
    outs = (s0, s1, s2, s3)
    ow[...] = weight_sum([g[...] for g in (gb0, gb1, gb2)], [prod[at, :] for at in groups])
    uw[...] = dot(flipped[...], ghu[...], 1, 0)
    store_shards(meta[1], ow, outs, 0)
    store_shards(meta[1], uw, outs, ow.shape[0] // 4)


def sums_body(w, grad_w, grads, out):
    out[...] = norm_sums(w, grad_w, grads)


EXTRA = 32


def back_body(
    n, pad, meta, gmix, v0, v1, v2, dgv0, dgv1, dgv2, cols, st, edge0, m1, m2, m3, g1, s1, g2, flipped,
    wv, first_sums,
    ghv, w0, w1, w2, w3,
    tile, col, vw, acc, extra,
):
    samples, half = gmix.shape[0] // (n * pad), gmix.shape[1]
    width = wv.shape[0]
    messages, vs, dgvs = (m1, m2, m3), (v0, v1, v2), (dgv0, dgv1, dgv2)
    stats = [st[...]] + [unpack_sums(m[pad:, :]) for m in messages]
    tile[...] = jnp.zeros_like(tile)
    for i in range(samples):
        for r in range(n):
            blk = 2 * (i * n + r)
            terms = [
                stats[k][2 * (i * n + (r ^ k)) : 2 * (i * n + (r ^ k)) + 2, :] for k in range(n)
            ]
            tile[blk : blk + 2, :] = ((terms[0] + terms[1]) + (terms[2] + terms[3])) / (half * n)
    col[...] = jnp.transpose(tile[...])
    gain = own_lanes(g2, meta[0], half)
    acc[...] = jnp.zeros_like(acc)
    for i in range(samples):
        for r in range(n):
            k, base = part(r, i, samples, pad)
            row = (r * samples + i) * pad
            blk = 2 * (i * n + r)
            for c in range(pad // CHUNK):
                here = slice(c * CHUNK, (c + 1) * CHUNK)
                at = slice(row + c * CHUNK, row + (c + 1) * CHUNK)
                src = slice(base + c * CHUNK, base + (c + 1) * CHUNK)
                mean, inverse = cols[here, blk : blk + 1], cols[here, blk + 1 : blk + 2]
                first, second = col[here, blk : blk + 1], col[here, blk + 1 : blk + 2]
                standard = (vs[k][src, :] - mean) * inverse
                g = gmix[at, :]
                out = inverse * (g * gain - first - standard * second)
                ghv[at, :] = (out * dgvs[k][src, :].astype(F32)).astype(BF)
                acc[0] += g * standard
                acc[1] += g
    vw[...] = dot(flipped[...], ghv[...], 1, 0)
    sums = first_sums[...] + norm_sums(wv, vw, ghv)
    shift_one = sums[1:2, :]
    gain_one = (sums[0:1, :] - s1[...] * shift_one) / g1[...]
    edge = edge0[...].astype(F32)
    for m in messages:
        edge = edge + m[0:pad, :].astype(F32)
    size = pad // 4
    extra[...] = jnp.zeros_like(extra)
    for k in range(4):
        extra[k, 0:size, :] = edge[k * size : (k + 1) * size, :]
    extra[0, size : size + 1, :] = jnp.sum(acc[0], axis=0, keepdims=True)
    extra[1, size : size + 1, :] = jnp.sum(acc[1], axis=0, keepdims=True)
    for k, row in ((2, gain_one), (3, shift_one)):
        extra[k, size : size + 1, :] = row[:, 0:half]
        extra[k, size + 1 : size + 2, 0 : width - half] = row[:, half:]
    outs = (w0, w1, w2, w3)
    store_shards(meta[1], vw, outs, 0)
    shard = vw.shape[0] // 4
    for rho, out in enumerate(outs):
        out[shard:, :] = extra[(meta[1] ^ rho) & 3].astype(BF)


def rows_body(n, pad, prod, wo, ghu, ghv, wu, wv, keep_a, send_a, keep_b, send_b):
    samples, rows = keep_a.shape[0] // 2, keep_a.shape[1]
    for r, out in enumerate((keep_a, send_a, keep_b, send_b)):
        at = slice(r * samples * pad, (r + 1) * samples * pad)
        branch = dot(prod[at, :], wo[...], 1, 0)
        grad = dot(ghu[at, :], wu[...], 1, 1) + dot(ghv[at, :], wv[...], 1, 1)
        for i in range(samples):
            out[i] = branch[i * pad : i * pad + rows, :].astype(BF)
            out[samples + i] = grad[i * pad : i * pad + rows, :].astype(BF)


def finish_rows_body(meta, tok, cot, keep, got_a, got_b, g1, output, grad_tokens):
    samples, rows = tok.shape[0], tok.shape[1]
    gain = g1[...]
    p = meta[0] * rows + iota((rows, 1), 0)
    for i in range(samples):
        x = tok[i].astype(F32)
        total = keep[i].astype(F32) + got_a[i].astype(F32) + got_b[i].astype(F32)
        output[i] = (x + branch_scale(meta, i, samples, p) * total).astype(BF)
        center = x - jnp.mean(x, axis=-1, keepdims=True)
        inverse = lax.rsqrt(jnp.mean(center * center, axis=-1, keepdims=True) + EPSILON)
        standard = center * inverse
        k = samples + i
        t = (keep[k].astype(F32) + got_a[k].astype(F32) + got_b[k].astype(F32)) * gain
        first = jnp.mean(t, axis=-1, keepdims=True)
        second = jnp.mean(t * standard, axis=-1, keepdims=True)
        grad = cot[i].astype(F32) + inverse * (t - first - standard * second)
        grad_tokens[i] = grad.astype(BF)


def sources(meta):
    seq, shard = meta[0], meta[1] & 3
    out = []
    for flip in (0, 1):
        s = seq ^ flip
        core = s & 1
        out += [
            (shard, s),
            (shard ^ (1 - core), s ^ (2 * core)),
            (shard ^ core, s ^ (2 * (1 - core))),
            (shard ^ 1, s ^ 2),
        ]
    return out


def place_wu(half, meta, pieces, which, w_in, w_out, wide, tall, sems):
    shard = wide.shape[1]
    copies = []
    origins = sources(meta)
    for piece, k in zip(pieces, which):
        group, seq = origins[k]
        for e in range(2):
            slot = len(copies) // 2
            row = (group ^ (2 * e)) * shard
            columns = rows_at(seq * half, half, 128)
            tall[slot] = jnp.transpose(piece[e, 0:shard, :].astype(F32))
            target = w_out.at[columns, rows_at(row, shard, 128)]
            copies.append(pltpu.make_async_copy(tall.at[slot], target, sems.at[2 * slot]))
            copies[-1].start()
            wide[slot] = piece[e, shard:, :].astype(F32)
            target = w_in.at[rows_at(row, shard, 16), columns]
            copies.append(pltpu.make_async_copy(wide.at[slot], target, sems.at[2 * slot + 1]))
            copies[-1].start()
    return copies


def place_v(half, gate, meta, pieces, which, w_in, wide, sems):
    shard = wide.shape[1]
    copies = []
    origins = sources(meta)
    for piece, k in zip(pieces, which):
        group, seq = origins[k]
        for e in range(2):
            slot = len(copies)
            wide[slot] = piece[e, 0:shard, :].astype(F32)
            columns = rows_at(gate + seq * half, half, 128)
            target = w_in.at[rows_at((group ^ (2 * e)) * shard, shard, 16), columns]
            copies.append(pltpu.make_async_copy(wide.at[slot], target, sems.at[slot]))
            copies[-1].start()
    return copies


def place_body(half, gate, fresh, which_wu, which_v, meta, *refs):
    *pieces, w_in, w_out, wide, tall, sems, more, more_sems = refs
    if not fresh:
        pieces = pieces[:-2]
    count = len(which_wu)
    copies = place_wu(half, meta, pieces[:count], which_wu, w_in, w_out, wide, tall, sems)
    copies += place_v(half, gate, meta, pieces[count:], which_v, w_in, more, more_sems)
    for copy in copies:
        copy.wait()


def place_last_body(half, gate, which, meta, *refs):
    pieces = refs[:8]
    w_in, *targets, wide, edge, norms = refs[10:20]
    spatial, bias, gain_one, shift_one, gain_two, shift_two, sems, small_sems = refs[20:]
    shard = wide.shape[1]
    rows, patches = spatial.shape
    size = edge.shape[0] // 4
    core = meta[0] & 1
    copies = place_v(half, gate, meta, [pieces[k] for k in which], which, w_in, wide, sems)
    small = []
    for k, (group, seq) in enumerate(sources(meta)):
        for e in range(2):
            at = group ^ (2 * e)
            rest = pieces[k][e, shard:, :].astype(F32)
            small.append((at, rest[0:size]))
            norms[at, seq] = rest[size:]
    for e in range(2):
        at, own = small[e]
        edge[rows_at(at * size, size, 8), :] = own
        at = (meta[1] & 3) ^ 1 ^ (2 * e)
        edge[rows_at(at * size, size, 8), :] = jnp.where(core == 0, small[2 + e][1], small[4 + e][1])
    spatial[...] = edge[0:rows, 0:patches]
    first = patches // 128 * 128
    tail = edge[0:rows, first:]
    column = jnp.sum(
        jnp.where(iota(tail.shape, 1) == patches - first, tail, 0.0), axis=1, keepdims=True
    )
    diagonal = iota((rows, rows), 0) == iota((rows, rows), 1)
    bias[...] = jnp.sum(jnp.where(diagonal, column, 0.0), axis=0)
    for at, out in ((2, gain_one), (3, shift_one)):
        total = (norms[at, 0] + norms[at, 1]) + (norms[at, 2] + norms[at, 3])
        out[0:half] = total[0, :]
        out[half:] = total[1, 0 : out.shape[0] - half]
    for at, out in ((0, gain_two), (1, shift_two)):
        for j in range(4):
            out[j * half : (j + 1) * half] = norms[at, j, 0, :]
    smalls = (spatial, bias, gain_one, shift_one, gain_two, shift_two)
    for k, (source, target) in enumerate(zip(smalls, targets)):
        copies.append(pltpu.make_async_copy(source, target, small_sems.at[k]))
        copies[-1].start()
    for copy in copies:
        copy.wait()


def solution(mesh):
    n, m = mesh.shape["seq"], mesh.shape["dp"]

    def over_seq(x, flip):
        return lax.ppermute(x, "seq", [(i, i ^ flip) for i in range(n)])

    def over_dp(x, flip):
        return lax.ppermute(x, "dp", [(i, i ^ flip) for i in range(m)])

    def mixed_axes(x, core_of_x):
        pairs = []
        for d in range(m):
            for s in range(n):
                other = (d ^ 1, s) if s & 1 == core_of_x else (d, s ^ 2)
                pairs.append((d * n + s, other[0] * n + other[1]))
        return lax.ppermute(x, ("dp", "seq"), pairs)

    def add(*terms):
        total = terms[0].astype(F32)
        for t in terms[1:]:
            total = total + t.astype(F32)
        return total.astype(BF)

    def pair_up(*terms):
        return jnp.stack(terms)

    def ordered():
        last = []

        def step(body, *ins):
            if last:
                ins, _ = lax.optimization_barrier((ins, last[0]))
            out = body(*ins) if body else ins[0]
            last[:] = [jax.tree.leaves(out)[0]]
            return out

        return step

    def shards(
        tokens,
        res_class,
        skip_mask,
        w_in,
        w_out,
        spatial,
        spatial_bias,
        gain_one,
        shift_one,
        gain_two,
        shift_two,
        cotangent,
    ):
        samples, rows, width = tokens.shape
        gate = w_out.shape[0]
        half = gate // n
        pad = round_up(rows + 2, 16)
        full = n * pad
        columns = round_up(n * rows + 2, 128)
        seq, dp = lax.axis_index("seq"), lax.axis_index("dp")
        meta = jnp.concatenate([seq[None], dp[None], res_class, skip_mask]).astype(jnp.int32)
        step = ordered()

        def tick(clock):
            return call(tick_body, [shape_of(clock.shape, F32)], [clock], flops=4 * 10**9, name="tick")[0]

        big_bf, big_f32 = (shape_of((samples * full, half), d) for d in (BF, F32))
        images = shape_of((full, samples * half), BF)
        shard = width // 4
        square = shape_of((round_up(samples * 2 * n, 8), 128), F32)

        t0 = tokens
        t2 = over_seq(t0, 2)
        t1 = over_seq(t0, 1)
        high = lax.reduce_precision(spatial_bias, 8, 7)
        side = jnp.stack([high, spatial_bias - high], axis=1).astype(BF)
        packed = jnp.concatenate([spatial, side], axis=1)
        packed = jnp.pad(packed, ((0, 0), (0, width - packed.shape[1])))
        c0 = jnp.concatenate([cotangent, packed[None]])
        c2 = over_seq(c0, 2)
        wu = lax.dynamic_slice(w_in, (0, seq * half), (width, half))
        wv = lax.dynamic_slice(w_in, (0, gate + seq * half), (width, half))
        wo = lax.dynamic_slice(w_out, (seq * half, 0), (half, width))
        g1, s1 = gain_one[None], shift_one[None]
        g2, s2 = gain_two.reshape(-1, 128), shift_two.reshape(-1, 128)
        meta, wu, wv, wo, c0, t1 = lax.optimization_barrier((meta, wu, wv, wo, c0, t1))
        c1 = over_seq(c0, 1)

        n0, gu0, dgu0, v0, dgv0, st = step(
            lambda *a: project(pad, 0, a[:2], *a[2:]), t0, t1, g1, s1, wu, wv
        )
        t2 = step(None, t2)
        t3 = over_seq(t2, 1)
        n1, gu1, dgu1, v1, dgv1, st = step(
            lambda *a: project(pad, 2, a[:1], *a[1:]), t2, g1, s1, wu, wv, st
        )
        n2, gu2, dgu2, v2, dgv2, st = step(
            lambda *a: project(pad, 3, a[:1], *a[1:]), t3, g1, s1, wu, wv, st
        )
        normed = [n0, n1, n2]
        stats = [st] + [over_seq(st, k) for k in range(1, n)]

        def front(first_block, count, *ins):
            def shape(columns, dtype):
                return shape_of((count * samples * pad, columns), dtype)

            outs = [shape(width, BF), shape(half, F32), shape(half, BF)]
            outs.append(shape_of((count * pad, full), BF))
            return call(
                functools.partial(front_body, n, pad, first_block, count),
                outs + ([] if first_block else [shape_of((columns, full), BF)]),
                ins,
                specs=[SM] + [VM] * (len(ins) - 1),
                name="front",
            )

        gb0, gp0, gs0, sp0, pm = step(functools.partial(front, 0, 2), meta, c0, c1, wo, gu0)

        def flip(*ins):
            return call(
                flip_body,
                [shape_of((width, samples * full), BF)],
                ins,
                [pltpu.VMEM((samples * full, width), BF)],
                name="flip",
            )

        (flipped,) = step(flip, *normed)
        stats = step(None, stats)
        c2 = step(None, c2)
        c3 = over_seq(c2, 1)
        gb1, gp1, gs1, sp1 = step(functools.partial(front, 2, 1), meta, c2, wo, gu1, pm)

        def prepare(*ins):
            square_bf = shape_of((full, full), BF)
            last = [shape_of((samples * pad, c), d) for c, d in ((width, BF), (half, F32))]
            return call(
                functools.partial(prepare_body, n, pad),
                [*last, images, big_f32, square_bf],
                ins,
                [pltpu.VMEM((full, full), BF)],
                specs=[SM] + [VM] * (len(ins) - 1),
                name="prepare",
            )

        gb2, gp2, gs, gmix, sp = step(prepare, meta, c3, wo, gu2, pm, gs0, gs1, sp0, sp1)

        def spatial_unit(*ins):
            message = shape_of((pad + 32, columns), BF)
            return call(
                functools.partial(spatial_body, n, pad),
                [big_bf, big_bf, shape_of((128, 128), F32), square, shape_of((pad, columns), BF)]
                + [message] * (n - 1),
                ins,
                [
                    pltpu.VMEM((full, samples * half), BF),
                    pltpu.VMEM((full, samples * half), F32),
                    pltpu.VMEM((128, 128), F32),
                    pltpu.VMEM((2 * samples * n, pad, 128), F32),
                ],
                specs=[SM] + [VM] * (len(ins) - 1),
                name="spatial",
            )

        clock = jnp.zeros((8, 128), F32)
        prod, ghu, cols, st2, edge, *messages = step(
            spatial_unit, meta, v0, v1, v2, gu0, gu1, gu2, dgu0, dgu1, dgu2, sp, gp0, gp1, gp2, gs, pm,
            gmix, g2, s2, *stats,
        )
        messages = [over_seq(x, k) for k, x in enumerate(messages, 1)]

        def weights(*ins):
            return call(
                weights_body,
                [shape_of((2 * shard, half), BF)] * 4 + [shape_of((width, half), F32)],
                ins,
                [pltpu.VMEM((width, half), F32)],
                specs=[SM] + [VM] * (len(ins) - 1),
                name="weights",
            )

        def norm_shares(*ins):
            return call(sums_body, [shape_of((8, width), F32)], ins, name="norm_shares")

        def back(*ins):
            return call(
                functools.partial(back_body, n, pad),
                [big_bf] + [shape_of((shard + EXTRA, half), BF)] * 4,
                ins,
                [
                    pltpu.VMEM((128, 128), F32),
                    pltpu.VMEM((128, 128), F32),
                    pltpu.VMEM((width, half), F32),
                    pltpu.VMEM((2, CHUNK, half), F32),
                    pltpu.VMEM((4, EXTRA, half), F32),
                ],
                specs=[SM] + [VM] * (len(ins) - 1),
                name="back",
            )

        def rows_out(*ins):
            shape = shape_of((2 * samples, rows, width), BF)
            return call(functools.partial(rows_body, n, pad), [shape] * 4, ins, name="rows_out")

        def finish_rows(*ins):
            shape = shape_of(tokens.shape, BF)
            return call(
                finish_rows_body, [shape, shape], ins, specs=[SM] + [VM] * 6, name="finish_rows"
            )

        wide_shapes = shape_of((width, 2 * gate), F32), shape_of((gate, width), F32)

        def place(fresh, which_wu, which_v, *ins):
            count = len(which_wu) + len(which_v)
            return call(
                functools.partial(place_body, half, gate, fresh, which_wu, which_v),
                wide_shapes,
                ins,
                [
                    pltpu.VMEM((2 * len(which_wu), shard, half), F32),
                    pltpu.VMEM((2 * len(which_wu), half, shard), F32),
                    pltpu.SemaphoreType.DMA((4 * len(which_wu),)),
                    pltpu.VMEM((max(2 * len(which_v), 1), shard, half), F32),
                    pltpu.SemaphoreType.DMA((max(2 * len(which_v), 1),)),
                ],
                specs=[SM] + [VM] * count + ([] if fresh else [HB] * 2),
                out_specs=[HB] * 2,
                input_output_aliases={} if fresh else {1 + count: 0, 2 + count: 1},
                name="place",
            )

        def place_last(which, *ins):
            one, two = shape_of((width,), F32), shape_of((gate,), F32)
            small = [shape_of((rows, n * rows), F32), shape_of((rows,), F32), one, one, two, two]
            return call(
                functools.partial(place_last_body, half, gate, which),
                [shape_of((width, 2 * gate), F32)] + small,
                ins,
                [
                    pltpu.VMEM((2 * len(which), shard, half), F32),
                    pltpu.VMEM((pad, columns), F32),
                    pltpu.VMEM((4, n, EXTRA - pad // 4, half), F32),
                    *(pltpu.VMEM(s.shape, F32) for s in small),
                    pltpu.SemaphoreType.DMA((2 * len(which),)),
                    pltpu.SemaphoreType.DMA((len(small),)),
                ],
                specs=[SM] + [VM] * 8 + [HB, VM],
                out_specs=[HB] * 7,
                input_output_aliases={9: 0},
                name="place_last",
            )

        def twin(x):
            return over_seq(x, 1)

        x = dict(messages=messages, clock=clock)

        def ev_tick():
            x["clock"] = step(tick, x["clock"])

        def reduce_start(key, shards):
            x[key] = shards[0]
            for rho in range(1, 4):
                x[f"{key}{rho}"] = over_dp(shards[rho], rho)

        def ev_weights():
            *x["a_shards"], x["uw"] = step(weights, meta, prod, gb0, gb1, gb2, ghu, flipped)

        def ev_a_send():
            reduce_start("a", step(None, x["a_shards"]))

        def ev_sums():
            (x["sums"],) = step(norm_shares, wu, x["uw"], ghu)

        def ev_stats():
            x["messages"] = step(None, x["messages"])

        def ev_back():
            x["ghv"], *x["v_shards"] = step(
                back, meta, gmix, v0, v1, v2, dgv0, dgv1, dgv2, cols, st2, edge, *x["messages"], g1, s1,
                g2, flipped, wv, x["sums"],
            )

        def ev_v_send():
            reduce_start("v", step(None, x["v_shards"]))

        def ev_rows():
            x["r_a"], send_a, x["r_b"], send_b = step(rows_out, prod, wo, ghu, x["ghv"], wu, wv)
            x["r_got"], x["r_got_b"] = twin(send_a), twin(send_b)

        def ev_rows_core():
            x["r_got"], x["r_got_b"] = step(None, (x["r_got"], x["r_got_b"]))
            x["r_last"] = over_seq(step(add, x["r_b"], x["r_got_b"]), 2)

        def ev_finish():
            x["output"], x["grad_tokens"] = step(
                finish_rows, meta, t0, c0, x["r_a"], x["r_got"], x["r_last"], g1
            )

        def ev_rs(k):
            x[k] = step(add, x[k], x[k + "1"], x[k + "2"], x[k + "3"])
            x[k + "z"] = over_dp(x[k], 4) if m > 4 else None

        def ev_z2(k):
            flip = 8
            while flip <= m:
                x[k] = step(add, x[k], x[k + "z"])
                if flip < m:
                    x[k + "z"] = over_dp(x[k], flip)
                flip *= 2
            x[k + "z"] = over_dp(x[k], 2)

        def ev_pair(k):
            x[k + "p0"] = step(pair_up, x[k], x[k + "z"])
            x[k + "p1"], x[k + "p2"] = mixed_axes(x[k + "p0"], 0), mixed_axes(x[k + "p0"], 1)

        def ev_mark(k):
            x[k + "p1"], x[k + "p2"] = step(None, (x[k + "p1"], x[k + "p2"]))
            x[k + "p3"] = mixed_axes(x[k + "p1"], 1)

        def ev_third(k):
            x[k + "p3"] = step(None, x[k + "p3"])

        def ev_twin(k, j):
            x[f"{k}q{j}"] = twin(x[f"{k}p{j}"])

        def ev_got(k, j):
            x[f"{k}q{j}"] = step(None, x[f"{k}q{j}"])

        def pieces(k, which):
            return [x[f"{k}{'pq'[j // 4]}{j % 4}"] for j in which]

        def ev_place(fresh, which_wu, which_v):
            ins = [*pieces("a", which_wu), *pieces("v", which_v)]
            ins += [] if fresh else [x["w_in"], x["w_out"]]
            x["w_in"], x["w_out"] = step(
                functools.partial(place, fresh, which_wu, which_v), meta, *ins
            )

        def ev_place_last():
            ins = [x[f"vp{j}"] for j in range(4)] + [x[f"vq{j}"] for j in range(4)]
            x["w_in"], x["spatial"], *x["small"] = step(
                functools.partial(place_last, (3, 7)), meta, *ins, x["w_in"], x["clock"]
            )

        events = dict(
            weights=ev_weights, sums=ev_sums, stats=ev_stats, back=ev_back,
            rows=ev_rows, rows_core=ev_rows_core, finish=ev_finish,
            place_last=ev_place_last,
            place_own=functools.partial(ev_place, True, (0, 4), (0, 4)),
            place_near=functools.partial(ev_place, False, (1, 2, 5, 6), ()),
            place_far=functools.partial(ev_place, False, (3, 7), (1, 2, 5, 6)),
            place_head=functools.partial(ev_place, True, (0, 1, 2, 4, 5, 6), ()),
            place_most=functools.partial(ev_place, False, (3, 7), (0, 1, 2, 4, 5, 6)),
            a_send=ev_a_send, v_send=ev_v_send, tick=ev_tick,
        )
        for k in ("a", "v"):
            for name, f in (("rs", ev_rs), ("z2", ev_z2), ("pair", ev_pair), ("mark", ev_mark), ("third", ev_third)):
                events[f"{k}_{name}"] = functools.partial(f, k)
            for j in range(4):
                events[f"{k}_twin{j}"] = functools.partial(ev_twin, k, j)
                events[f"{k}_got{j}"] = functools.partial(ev_got, k, j)
        for name in ORDER:
            events[name]()
        output, grad_tokens, grad_w_in, grad_w_out = (
            x[k] for k in ("output", "grad_tokens", "w_in", "w_out")
        )
        grad_spatial, sums = x["spatial"], x["small"]
        return (output, grad_tokens, grad_w_in, grad_w_out, grad_spatial, *sums)

    placed = (
        P("dp", "seq", None),
        P("dp"),
        P("dp"),
        P(),
        P(),
        P("seq", None),
        P("seq"),
        P(),
        P(),
        P(),
        P(),
        P("dp", "seq", None),
    )
    return jax.shard_map(
        shards,
        mesh=mesh,
        in_specs=placed,
        out_specs=(
            P("dp", "seq", None),
            P("dp", "seq", None),
            P(),
            P(),
            P("seq", None),
            P("seq"),
            P(),
            P(),
            P(),
            P(),
        ),
        check_vma=False,
    )
```

```python
import functools

import jax
import jax.numpy as jnp
from jax import lax
from jax.experimental import pallas as pl
from jax.experimental.pallas import tpu as pltpu
from jax.sharding import PartitionSpec as P

PATCHES = 324
SMALL_P = 100
MID_P = 196

EPSILON = 1e-05
SURVIVAL = 0.9

BF = jnp.bfloat16
F32 = jnp.float32
CHUNK = 16
VM = pl.BlockSpec(memory_space=pltpu.VMEM)
SM = pl.BlockSpec(memory_space=pltpu.SMEM)
HB = pl.BlockSpec(memory_space=pltpu.HBM)


ORDER = (
    "weights", "a_send", "tick", "stats", "sums", "back", "v_send", "rows", "a_rs", "tick", "tick", "tick",
    "rows_core", "v_rs", "a_z2", "v_z2", "a_pair", "tick", "v_pair", "finish", "a_mark", "tick", "v_mark", "tick",
    "a_twin0", "a_twin1", "a_twin2", "place_head", "a_third", "a_twin3", "v_third", "v_twin3", "v_twin0", "v_twin1",
    "v_twin2", "tick", "place_most", "place_last",
)


def round_up(size, multiple):
    return -(-size // multiple) * multiple


def dot(a, b, ca, cb):
    return lax.dot_general(a, b, (((ca,), (cb,)), ((), ())), preferred_element_type=F32)


def iota(shape, axis):
    return lax.broadcasted_iota(jnp.int32, shape, axis)


def rows_at(start, size, multiple):
    return pl.ds(pl.multiple_of(start, multiple), size)


def call(body, outs, ins, scratch=(), specs=None, out_specs=None, flops=1, **more):
    return pl.pallas_call(
        body,
        out_shape=outs,
        in_specs=specs if specs is not None else [VM] * len(ins),
        out_specs=out_specs if out_specs is not None else [VM] * len(outs),
        scratch_shapes=list(scratch),
        compiler_params=pltpu.CompilerParams(vmem_limit_bytes=20 * 2**20),
        cost_estimate=pl.CostEstimate(flops=flops, bytes_accessed=1, transcendentals=0),
        **more,
    )(*ins)


def shape_of(shape, dtype):
    return jax.ShapeDtypeStruct(shape, dtype)


def add_body(*refs):
    total = refs[0][...].astype(F32)
    for ref in refs[1:-1]:
        total = total + ref[...].astype(F32)
    refs[-1][...] = total.astype(BF)


def tick_body(clock, out):
    out[...] = clock[...] + 1.0


def pair_body(a, b, out):
    out[0] = a[...]
    out[1] = b[...]


def project_body(pad, first_block, *refs):
    refs = list(refs)
    n_tok = len(refs) - 13 - (1 if first_block else 0)
    toks, refs = refs[:n_tok], refs[n_tok:]
    g1, s1, wu, wv = refs[:4]
    refs = refs[4:]
    if first_block:
        st_in, refs = refs[0], refs[1:]
    normed, gu, dgu, v, dgv, st, xs, hid, tile = refs
    samples, rows, width = toks[0].shape
    half = wu.shape[1]
    size = samples * pad
    found = [jnp.zeros((CHUNK, 128), F32)] * (128 // CHUNK)
    low = rows // 8 * 8
    gain, shift = g1[...], s1[...]
    for b, tok in enumerate(toks):
        for i in range(samples):
            base = (b * samples + i) * pad
            xs[base + low : base + pad, :] = jnp.zeros((pad - low, width), F32)
            xs[base : base + rows, :] = tok[i].astype(F32)
            for c in range(base, base + pad, CHUNK):
                x = xs[c : c + CHUNK, :]
                center = x - jnp.mean(x, axis=-1, keepdims=True)
                inverse = lax.rsqrt(jnp.mean(center * center, axis=-1, keepdims=True) + EPSILON)
                normed[c : c + CHUNK, :] = (center * inverse * gain + shift).astype(BF)
        at = slice(b * size, (b + 1) * size)
        hid[at, 0:half] = dot(normed[at, :], wu[...], 1, 0)
        hid[at, half:] = dot(normed[at, :], wv[...], 1, 0)
    c0 = 0.7978845608028654
    c1 = 0.7978845608028654 * 0.044715

    def gelu_pair(h):
        a = (c1 * h) * h
        s = 0.5 + 0.5 * jnp.tanh(h * (c0 + a))
        g = h * s
        return g, s + (2.0 * g) * (1.0 - s) * (c0 + 3.0 * a)

    lane = iota((CHUNK, 128), 1)
    for b in range(len(toks)):
        for i in range(samples):
            base = (b * samples + i) * pad
            blk = 2 * (i * 4 + first_block + b)
            for c in range(pad // CHUNK):
                at = slice(base + c * CHUNK, base + (c + 1) * CHUNK)
                g, d = gelu_pair(hid[at, 0:half])
                gu[at, :] = g.astype(BF)
                dgu[at, :] = d.astype(BF)
                g, d = gelu_pair(hid[at, half:])
                v[at, :] = g
                dgv[at, :] = d.astype(BF)
                mean = jnp.mean(g, axis=-1, keepdims=True)
                center = g - mean
                square = jnp.sum(center * center, axis=-1, keepdims=True)
                found[c] = jnp.where(
                    lane == blk, mean, jnp.where(lane == blk + 1, square, found[c])
                )
    for c, part_found in enumerate(found):
        tile[c * CHUNK : (c + 1) * CHUNK, :] = part_found
    flipped = jnp.transpose(tile[...])[0 : st.shape[0], :]
    st[...] = flipped + st_in[...] if first_block else flipped


def project(pad, first_block, toks, g1, s1, wu, wv, st_in=None):
    samples, rows, width = toks[0].shape
    half = wu.shape[1]
    n_rows = len(toks) * samples * pad
    outs = [
        shape_of((n_rows, width), BF),
        shape_of((n_rows, half), BF),
        shape_of((n_rows, half), BF),
        shape_of((n_rows, half), F32),
        shape_of((n_rows, half), BF),
        shape_of((round_up(samples * 8, 8), 128), F32),
    ]
    scratch = [
        pltpu.VMEM((n_rows, width), F32),
        pltpu.VMEM((n_rows, 2 * half), F32),
        pltpu.VMEM((128, 128), F32),
    ]
    ins = [*toks, g1, s1, wu, wv] + ([st_in] if first_block else [])
    return call(
        functools.partial(project_body, pad, first_block),
        outs,
        ins,
        scratch,
        name="project",
    )


GROUPS = ((0, 1), (2,), (3,))


def part(r, i, samples, pad):
    for k, blocks in enumerate(GROUPS):
        if r in blocks:
            return k, ((r - blocks[0]) * samples + i) * pad


def group_rows(size):
    return [slice(blocks[0] * size, (blocks[-1] + 1) * size) for blocks in GROUPS]


def position_map(seq, rows, pad, n, columns):
    a = iota((columns, n * pad), 0)
    j = iota((columns, n * pad), 1)
    r = jnp.zeros_like(j)
    for k in range(1, n):
        r = r + (j >= k * pad).astype(jnp.int32)
    q = j - r * pad
    hit = (a == (r ^ seq) * rows + q) & (q < rows)
    hit = hit | ((a == n * rows) & (j == pad - 1)) | ((a == n * rows + 1) & (j == pad - 2))
    return jnp.where(hit, 1.0, 0.0).astype(BF)


def patch_count(meta, i):
    kind = meta[2 + i]
    return jnp.where(kind == 0, SMALL_P, jnp.where(kind == 1, MID_P, PATCHES))


def branch_scale(meta, i, samples, where):
    keep = jnp.where(where < patch_count(meta, i), meta[2 + samples + i], 0)
    return keep.astype(F32) / SURVIVAL


def valid_rows(meta, i, r, c, rows):
    p = c * CHUNK + iota((CHUNK, 1), 0)
    return (p < rows) & ((meta[0] ^ r) * rows + p < patch_count(meta, i))


def front_rows(pad, first_block, meta, cots, wo, gu, gb, gp, put):
    rows, width = cots[0].shape[1], cots[0].shape[2]
    samples = cots[0].shape[0] - 1
    low = rows // 16 * 16
    size = samples * pad
    for b, cot in enumerate(cots):
        where = (meta[0] ^ (first_block + b)) * rows + iota((rows, 1), 0)
        for i in range(samples):
            base = b * size + i * pad
            scale = branch_scale(meta, i, samples, where)
            gb[base + low : base + pad, :] = jnp.zeros((pad - low, width), BF)
            gb[base : base + rows, :] = (cot[i].astype(F32) * scale).astype(BF)
        at = slice(b * size, (b + 1) * size)
        gp[at, :] = dot(gb[at, :], wo[...], 1, 1)
        for i in range(samples):
            for c in range(0, pad, CHUNK):
                at = slice(b * size + i * pad + c, b * size + i * pad + c + CHUNK)
                put(b, i, c, (gp[at, :] * gu[at, :].astype(F32)).astype(BF))


def matrix_rows(pad, block, cot, pm, sp):
    samples, rows = cot.shape[0] - 1, cot.shape[1]
    low = rows // 16 * 16
    sp[block * pad + low : (block + 1) * pad, :] = jnp.zeros((pad - low, sp.shape[1]), BF)
    out = dot(cot[samples, :, 0 : pm.shape[0]], pm[...], 1, 0)
    sp[block * pad : block * pad + rows, :] = out.astype(BF)


def front_body(n, pad, first_block, count, meta, *refs):
    cots, refs = refs[:count], refs[count:]
    if first_block:
        wo, gu, pm, gb, gp, gs, sp = refs
    else:
        wo, gu, gb, gp, gs, sp, pm = refs
        pm[...] = position_map(meta[0], cots[0].shape[1], pad, n, pm.shape[0])
    samples = cots[0].shape[0] - 1

    def put(b, i, c, out):
        base = (b * samples + i) * pad + c
        gs[base : base + CHUNK, :] = out

    front_rows(pad, first_block, meta, cots, wo, gu, gb, gp, put)
    for b, cot in enumerate(cots):
        matrix_rows(pad, b, cot, pm, sp)


def prepare_body(n, pad, meta, c3, wo, gu2, pm, gs0, gs1, sp0, sp1, gb, gp, gs, gmix, sp, spt):
    samples, rows = c3.shape[0] - 1, c3.shape[1]
    most = (n - 1) * pad
    sp[0 : sp0.shape[0], :] = sp0[...]
    sp[sp0.shape[0] : most, :] = sp1[...]
    matrix_rows(pad, n - 1, c3, pm, sp)
    spt[...] = jnp.transpose(sp[...].astype(F32)).astype(BF)

    half = gp.shape[1]

    def put(b, i, c, out):
        gs[most + c : most + c + CHUNK, i * half : (i + 1) * half] = out

    front_rows(pad, n - 1, meta, (c3,), wo, gu2, gb, gp, put)
    for i in range(samples):
        for r in range(n - 1):
            k, base = part(r, i, samples, pad)
            here = slice(i * half, (i + 1) * half)
            gs[r * pad : (r + 1) * pad, here] = (gs0, gs1)[k][base : base + pad, :]
    full = dot(spt[...], gs[...], 1, 0)
    for i in range(samples):
        for r in range(n):
            base = (r * samples + i) * pad
            for c in range(pad // CHUNK):
                at = slice(r * pad + c * CHUNK, r * pad + (c + 1) * CHUNK)
                out = full[at, i * half : (i + 1) * half]
                out = jnp.where(valid_rows(meta, i, r, c, rows), out, 0.0)
                gmix[base + c * CHUNK : base + (c + 1) * CHUNK, :] = out


def own_lanes(rows, seq, half):
    count = half // 128
    return jnp.concatenate([rows[pl.ds(seq * count + k, 1), :] for k in range(count)], axis=1)


def lane_sum(x):
    total = x[:, 0:128]
    for k in range(1, x.shape[1] // 128):
        total = total + x[:, k * 128 : (k + 1) * 128]
    return total


def row_sum(x):
    ones = jnp.ones((8, x.shape[1]), BF)
    high = x.astype(BF)
    low = (x - high.astype(F32)).astype(BF)
    return dot(ones, high, 1, 1) + dot(ones, low, 1, 1)


def row_sums(parts, st, pad):
    blocks = parts.shape[0] // 2
    for b in range(blocks):
        for j in range(2):
            st[2 * b + j : 2 * b + j + 1, 0:pad] = row_sum(parts[j * blocks + b])[0:1, :]


def pack_sums(st):
    x = jnp.concatenate([st[8 * k : 8 * (k + 1), :] for k in range(3)], axis=1)
    terms = []
    for _ in range(3):
        terms.append(x.astype(BF).astype(F32))
        x = x - terms[-1]
    return jnp.concatenate(terms + [jnp.zeros_like(x)], axis=0).astype(BF)


def unpack_sums(packed):
    x = packed.astype(F32)
    x = (x[16:24] + x[8:16]) + x[0:8]
    return jnp.concatenate([x[:, 128 * k : 128 * (k + 1)] for k in range(3)], axis=0)


def spatial_body(
    n, pad, meta, v0, v1, v2, gu0, gu1, gu2, dgu0, dgu1, dgu2, sp, gp0, gp1, gp2, gs, pm, gmix, g2, s2, t0, t1, t2, t3,
    prod, ghu, cols, st, edge, m1, m2, m3,
    mixed, so, tile, parts,
):
    half, rows = gp0.shape[1], PATCHES // n
    samples = gs.shape[1] // half
    gps = (gp0, gp1, gp2)
    whole = half * n
    stats, vs, gus, dgus = (t0, t1, t2, t3), (v0, v1, v2), (gu0, gu1, gu2), (dgu0, dgu1, dgu2)
    tile[...] = jnp.zeros_like(tile)
    for i in range(samples):
        for r in range(n):
            at = [2 * (i * n + (r ^ k)) for k in range(n)]
            means = [stats[k][at[k] : at[k] + 1, :] for k in range(n)]
            squares = [stats[k][at[k] + 1 : at[k] + 2, :] for k in range(n)]
            mean = ((means[0] + means[1]) + (means[2] + means[3])) / n
            spread = (squares[0] + squares[1]) + (squares[2] + squares[3])
            for k in range(n):
                spread = spread + half * (means[k] - mean) * (means[k] - mean)
            blk = 2 * (i * n + r)
            tile[blk : blk + 1, :] = mean
            tile[blk + 1 : blk + 2, :] = lax.rsqrt(spread / whole + EPSILON)
    cols[...] = jnp.transpose(tile[...])
    gain, shift = own_lanes(g2, meta[0], half), own_lanes(s2, meta[0], half)
    for i in range(samples):
        for r in range(n):
            k, base = part(r, i, samples, pad)
            first = (r * samples + i) * pad
            blk = 2 * (i * n + r)
            for c in range(pad // CHUNK):
                here = slice(c * CHUNK, (c + 1) * CHUNK)
                mean, inverse = cols[here, blk : blk + 1], cols[here, blk + 1 : blk + 2]
                standard = (vs[k][base + c * CHUNK : base + (c + 1) * CHUNK, :] - mean) * inverse
                out = jnp.where(valid_rows(meta, i, r, c, rows), standard * gain + shift, 0.0)
                if r == 0 and (c + 1) * CHUNK == pad:
                    p = c * CHUNK + iota((CHUNK, 1), 0)
                    out = jnp.where(p >= pad - 2, 1.0, out)
                at = slice(r * pad + c * CHUNK, r * pad + (c + 1) * CHUNK)
                mixed[at, i * half : (i + 1) * half] = out.astype(BF)
                t = gmix[first + c * CHUNK : first + (c + 1) * CHUNK, :] * gain
                parts[i * n + r, here, :] = lane_sum(t)
                parts[samples * n + i * n + r, here, :] = lane_sum(t * standard)
    so[...] = dot(sp[...], mixed[...], 1, 0)
    row_sums(parts, st, pad)
    total = dot(gs[...], mixed[...], 1, 1)
    placed = dot(total.astype(BF), pm[...], 1, 1).astype(BF)
    packed = pack_sums(st)
    edge[...] = placed[0:pad, :]
    for r, message in enumerate((m1, m2, m3), 1):
        message[0:pad, :] = placed[r * pad : (r + 1) * pad, :]
        message[pad:, :] = packed
    for i in range(samples):
        for r in range(n):
            k, base = part(r, i, samples, pad)
            first = (r * samples + i) * pad
            for c in range(0, pad, CHUNK):
                src = slice(base + c, base + c + CHUNK)
                at = slice(first + c, first + c + CHUNK)
                s = so[r * pad + c : r * pad + c + CHUNK, i * half : (i + 1) * half]
                prod[at, :] = (gus[k][src, :].astype(F32) * s).astype(BF)
                ghu[at, :] = (gps[k][src, :] * s * dgus[k][src, :].astype(F32)).astype(BF)


def weight_sum(lefts, rights):
    total = None
    for left, right in zip(lefts, rights):
        term = dot(left, right, 0, 0)
        total = term if total is None else total + term
    return total


def store_shards(dp, whole, outs, base):
    shard = whole.shape[0] // 4
    for rho, out in enumerate(outs):
        here = whole[rows_at(((dp ^ rho) & 3) * shard, shard, 16), :]
        out[base : base + shard, :] = here.astype(BF)


def norm_sums(w, grad_w, grads):
    columns = None
    for c in range(0, grads.shape[0], CHUNK):
        g = grads[c : c + CHUNK, :].astype(F32)
        columns = g if columns is None else columns + g
    columns = jnp.sum(columns, axis=0, keepdims=True)
    first, second = [], []
    for c in range(w.shape[0] // CHUNK):
        at = slice(c * CHUNK, (c + 1) * CHUNK)
        x = w[at, :].astype(F32)
        first.append(lane_sum(x * grad_w[at, :]))
        second.append(lane_sum(x * columns))
    first = row_sum(jnp.concatenate(first, axis=0))
    second = row_sum(jnp.concatenate(second, axis=0))
    return jnp.where(iota(first.shape, 0) == 0, first, second)


def flip_body(n0, n1, n2, out, whole):
    base = 0
    for ref in (n0, n1, n2):
        whole[base : base + ref.shape[0], :] = ref[...]
        base += ref.shape[0]
    out[...] = jnp.transpose(whole[...])


def weights_body(meta, prod, gb0, gb1, gb2, ghu, flipped, s0, s1, s2, s3, uw, ow):
    groups = group_rows(prod.shape[0] // 4)
    outs = (s0, s1, s2, s3)
    ow[...] = weight_sum([g[...] for g in (gb0, gb1, gb2)], [prod[at, :] for at in groups])
    uw[...] = dot(flipped[...], ghu[...], 1, 0)
    store_shards(meta[1], ow, outs, 0)
    store_shards(meta[1], uw, outs, ow.shape[0] // 4)


def sums_body(w, grad_w, grads, out):
    out[...] = norm_sums(w, grad_w, grads)


EXTRA = 32


def back_body(
    n, pad, meta, gmix, v0, v1, v2, dgv0, dgv1, dgv2, cols, st, edge0, m1, m2, m3, g1, s1, g2, flipped,
    wv, first_sums,
    ghv, w0, w1, w2, w3,
    tile, col, vw, acc, extra,
):
    samples, half = gmix.shape[0] // (n * pad), gmix.shape[1]
    width = wv.shape[0]
    messages, vs, dgvs = (m1, m2, m3), (v0, v1, v2), (dgv0, dgv1, dgv2)
    stats = [st[...]] + [unpack_sums(m[pad:, :]) for m in messages]
    tile[...] = jnp.zeros_like(tile)
    for i in range(samples):
        for r in range(n):
            blk = 2 * (i * n + r)
            terms = [
                stats[k][2 * (i * n + (r ^ k)) : 2 * (i * n + (r ^ k)) + 2, :] for k in range(n)
            ]
            tile[blk : blk + 2, :] = ((terms[0] + terms[1]) + (terms[2] + terms[3])) / (half * n)
    col[...] = jnp.transpose(tile[...])
    gain = own_lanes(g2, meta[0], half)
    acc[...] = jnp.zeros_like(acc)
    for i in range(samples):
        for r in range(n):
            k, base = part(r, i, samples, pad)
            row = (r * samples + i) * pad
            blk = 2 * (i * n + r)
            for c in range(pad // CHUNK):
                here = slice(c * CHUNK, (c + 1) * CHUNK)
                at = slice(row + c * CHUNK, row + (c + 1) * CHUNK)
                src = slice(base + c * CHUNK, base + (c + 1) * CHUNK)
                mean, inverse = cols[here, blk : blk + 1], cols[here, blk + 1 : blk + 2]
                first, second = col[here, blk : blk + 1], col[here, blk + 1 : blk + 2]
                standard = (vs[k][src, :] - mean) * inverse
                g = gmix[at, :]
                out = inverse * (g * gain - first - standard * second)
                ghv[at, :] = (out * dgvs[k][src, :].astype(F32)).astype(BF)
                acc[0] += g * standard
                acc[1] += g
    vw[...] = dot(flipped[...], ghv[...], 1, 0)
    sums = first_sums[...] + norm_sums(wv, vw, ghv)
    shift_one = sums[1:2, :]
    gain_one = (sums[0:1, :] - s1[...] * shift_one) / g1[...]
    edge = edge0[...].astype(F32)
    for m in messages:
        edge = edge + m[0:pad, :].astype(F32)
    size = pad // 4
    extra[...] = jnp.zeros_like(extra)
    for k in range(4):
        extra[k, 0:size, :] = edge[k * size : (k + 1) * size, :]
    extra[0, size : size + 1, :] = jnp.sum(acc[0], axis=0, keepdims=True)
    extra[1, size : size + 1, :] = jnp.sum(acc[1], axis=0, keepdims=True)
    for k, row in ((2, gain_one), (3, shift_one)):
        extra[k, size : size + 1, :] = row[:, 0:half]
        extra[k, size + 1 : size + 2, 0 : width - half] = row[:, half:]
    outs = (w0, w1, w2, w3)
    store_shards(meta[1], vw, outs, 0)
    shard = vw.shape[0] // 4
    for rho, out in enumerate(outs):
        out[shard:, :] = extra[(meta[1] ^ rho) & 3].astype(BF)


def rows_body(n, pad, prod, wo, ghu, ghv, wu, wv, keep_a, keep_b, send):
    samples, rows = keep_a.shape[0] // 2, keep_a.shape[1]
    places = ((keep_a, 0), (send, 0), (keep_b, 0), (send, 2 * samples))
    for r, (out, first) in enumerate(places):
        at = slice(r * samples * pad, (r + 1) * samples * pad)
        branch = dot(prod[at, :], wo[...], 1, 0)
        grad = dot(ghu[at, :], wu[...], 1, 1) + dot(ghv[at, :], wv[...], 1, 1)
        for i in range(samples):
            out[first + i] = branch[i * pad : i * pad + rows, :].astype(BF)
            out[first + samples + i] = grad[i * pad : i * pad + rows, :].astype(BF)


def finish_rows_body(meta, tok, cot, keep, got_a, got_b, g1, output, grad_tokens):
    samples, rows = tok.shape[0], tok.shape[1]
    gain = g1[...]
    p = meta[0] * rows + iota((rows, 1), 0)
    for i in range(samples):
        x = tok[i].astype(F32)
        total = keep[i].astype(F32) + got_a[i].astype(F32) + got_b[i].astype(F32)
        output[i] = (x + branch_scale(meta, i, samples, p) * total).astype(BF)
        center = x - jnp.mean(x, axis=-1, keepdims=True)
        inverse = lax.rsqrt(jnp.mean(center * center, axis=-1, keepdims=True) + EPSILON)
        standard = center * inverse
        k = samples + i
        t = (keep[k].astype(F32) + got_a[k].astype(F32) + got_b[k].astype(F32)) * gain
        first = jnp.mean(t, axis=-1, keepdims=True)
        second = jnp.mean(t * standard, axis=-1, keepdims=True)
        grad = cot[i].astype(F32) + inverse * (t - first - standard * second)
        grad_tokens[i] = grad.astype(BF)


def sources(meta):
    seq, shard = meta[0], meta[1] & 3
    out = []
    for flip in (0, 1):
        s = seq ^ flip
        core = s & 1
        out += [
            (shard, s),
            (shard ^ (1 - core), s ^ (2 * core)),
            (shard ^ core, s ^ (2 * (1 - core))),
            (shard ^ 1, s ^ 2),
        ]
    return out


def place_wu(half, meta, pieces, which, w_in, w_out, wide, tall, sems):
    shard = wide.shape[1]
    copies = []
    origins = sources(meta)
    for piece, k in zip(pieces, which):
        group, seq = origins[k]
        for e in range(2):
            slot = len(copies) // 2
            row = (group ^ (2 * e)) * shard
            columns = rows_at(seq * half, half, 128)
            tall[slot] = jnp.transpose(piece[e, 0:shard, :].astype(F32))
            target = w_out.at[columns, rows_at(row, shard, 128)]
            copies.append(pltpu.make_async_copy(tall.at[slot], target, sems.at[2 * slot]))
            copies[-1].start()
            wide[slot] = piece[e, shard:, :].astype(F32)
            target = w_in.at[rows_at(row, shard, 16), columns]
            copies.append(pltpu.make_async_copy(wide.at[slot], target, sems.at[2 * slot + 1]))
            copies[-1].start()
    return copies


def place_v(half, gate, meta, pieces, which, w_in, wide, sems):
    shard = wide.shape[1]
    copies = []
    origins = sources(meta)
    for piece, k in zip(pieces, which):
        group, seq = origins[k]
        for e in range(2):
            slot = len(copies)
            wide[slot] = piece[e, 0:shard, :].astype(F32)
            columns = rows_at(gate + seq * half, half, 128)
            target = w_in.at[rows_at((group ^ (2 * e)) * shard, shard, 16), columns]
            copies.append(pltpu.make_async_copy(wide.at[slot], target, sems.at[slot]))
            copies[-1].start()
    return copies


def place_body(half, gate, fresh, which_wu, which_v, meta, *refs):
    *pieces, w_in, w_out, wide, tall, sems, more, more_sems = refs
    if not fresh:
        pieces = pieces[:-2]
    count = len(which_wu)
    copies = place_wu(half, meta, pieces[:count], which_wu, w_in, w_out, wide, tall, sems)
    copies += place_v(half, gate, meta, pieces[count:], which_v, w_in, more, more_sems)
    for copy in copies:
        copy.wait()


def place_last_body(half, gate, which, meta, *refs):
    pieces = refs[:8]
    w_in, *targets, wide, edge, norms = refs[10:20]
    spatial, bias, gain_one, shift_one, gain_two, shift_two, sems, small_sems = refs[20:]
    shard = wide.shape[1]
    rows, patches = spatial.shape
    size = edge.shape[0] // 4
    core = meta[0] & 1
    copies = place_v(half, gate, meta, [pieces[k] for k in which], which, w_in, wide, sems)
    small = []
    for k, (group, seq) in enumerate(sources(meta)):
        for e in range(2):
            at = group ^ (2 * e)
            rest = pieces[k][e, shard:, :].astype(F32)
            small.append((at, rest[0:size]))
            norms[at, seq] = rest[size:]
    for e in range(2):
        at, own = small[e]
        edge[rows_at(at * size, size, 8), :] = own
        at = (meta[1] & 3) ^ 1 ^ (2 * e)
        edge[rows_at(at * size, size, 8), :] = jnp.where(core == 0, small[2 + e][1], small[4 + e][1])
    spatial[...] = edge[0:rows, 0:patches]
    first = patches // 128 * 128
    tail = edge[0:rows, first:]
    column = jnp.sum(
        jnp.where(iota(tail.shape, 1) == patches - first, tail, 0.0), axis=1, keepdims=True
    )
    diagonal = iota((rows, rows), 0) == iota((rows, rows), 1)
    bias[...] = jnp.sum(jnp.where(diagonal, column, 0.0), axis=0)
    for at, out in ((2, gain_one), (3, shift_one)):
        total = (norms[at, 0] + norms[at, 1]) + (norms[at, 2] + norms[at, 3])
        out[0:half] = total[0, :]
        out[half:] = total[1, 0 : out.shape[0] - half]
    for at, out in ((0, gain_two), (1, shift_two)):
        for j in range(4):
            out[j * half : (j + 1) * half] = norms[at, j, 0, :]
    smalls = (spatial, bias, gain_one, shift_one, gain_two, shift_two)
    for k, (source, target) in enumerate(zip(smalls, targets)):
        copies.append(pltpu.make_async_copy(source, target, small_sems.at[k]))
        copies[-1].start()
    for copy in copies:
        copy.wait()


def solution(mesh):
    n, m = mesh.shape["seq"], mesh.shape["dp"]

    def over_seq(x, flip):
        return lax.ppermute(x, "seq", [(i, i ^ flip) for i in range(n)])

    def over_dp(x, flip):
        return lax.ppermute(x, "dp", [(i, i ^ flip) for i in range(m)])

    def mixed_axes(x, core_of_x):
        pairs = []
        for d in range(m):
            for s in range(n):
                other = (d ^ 1, s) if s & 1 == core_of_x else (d, s ^ 2)
                pairs.append((d * n + s, other[0] * n + other[1]))
        return lax.ppermute(x, ("dp", "seq"), pairs)

    def add(*terms):
        total = terms[0].astype(F32)
        for t in terms[1:]:
            total = total + t.astype(F32)
        return total.astype(BF)

    def pair_up(*terms):
        return jnp.stack(terms)

    def ordered():
        last = []

        def step(body, *ins):
            if last:
                ins, _ = lax.optimization_barrier((ins, last[0]))
            out = body(*ins) if body else ins[0]
            last[:] = [jax.tree.leaves(out)[0]]
            return out

        return step

    def shards(
        tokens,
        res_class,
        skip_mask,
        w_in,
        w_out,
        spatial,
        spatial_bias,
        gain_one,
        shift_one,
        gain_two,
        shift_two,
        cotangent,
    ):
        samples, rows, width = tokens.shape
        gate = w_out.shape[0]
        half = gate // n
        pad = round_up(rows + 2, 16)
        full = n * pad
        columns = round_up(n * rows + 2, 128)
        seq, dp = lax.axis_index("seq"), lax.axis_index("dp")
        meta = jnp.concatenate([seq[None], dp[None], res_class, skip_mask]).astype(jnp.int32)
        step = ordered()
        clock = jnp.zeros((8, 128), F32)

        def tick(clock):
            return call(tick_body, [shape_of(clock.shape, F32)], [clock], flops=4 * 10**9, name="tick")[0]

        big_bf, big_f32 = (shape_of((samples * full, half), d) for d in (BF, F32))
        images = shape_of((full, samples * half), BF)
        shard = width // 4
        square = shape_of((round_up(samples * 2 * n, 8), 128), F32)

        t0 = tokens
        t2 = over_seq(t0, 2)
        t1 = over_seq(t0, 1)
        high = lax.reduce_precision(spatial_bias, 8, 7)
        side = jnp.stack([high, spatial_bias - high], axis=1).astype(BF)
        packed = jnp.concatenate([spatial, side], axis=1)
        packed = jnp.pad(packed, ((0, 0), (0, width - packed.shape[1])))
        c0 = jnp.concatenate([cotangent, packed[None]])
        c2 = over_seq(c0, 2)
        wu = lax.dynamic_slice(w_in, (0, seq * half), (width, half))
        wv = lax.dynamic_slice(w_in, (0, gate + seq * half), (width, half))
        wo = lax.dynamic_slice(w_out, (seq * half, 0), (half, width))
        g1, s1 = gain_one[None], shift_one[None]
        g2, s2 = gain_two.reshape(-1, 128), shift_two.reshape(-1, 128)
        meta, wu, wv, wo, c0, t1 = lax.optimization_barrier((meta, wu, wv, wo, c0, t1))
        c1 = over_seq(c0, 1)

        n0, gu0, dgu0, v0, dgv0, st = step(
            lambda *a: project(pad, 0, a[:2], *a[2:]), t0, t1, g1, s1, wu, wv
        )
        t2 = step(None, t2)
        t3 = over_seq(t2, 1)
        n1, gu1, dgu1, v1, dgv1, st = step(
            lambda *a: project(pad, 2, a[:1], *a[1:]), t2, g1, s1, wu, wv, st
        )
        n2, gu2, dgu2, v2, dgv2, st = step(
            lambda *a: project(pad, 3, a[:1], *a[1:]), t3, g1, s1, wu, wv, st
        )
        normed = [n0, n1, n2]
        stats = [st] + [over_seq(st, k) for k in range(1, n)]

        def front(first_block, count, *ins):
            def shape(columns, dtype):
                return shape_of((count * samples * pad, columns), dtype)

            outs = [shape(width, BF), shape(half, F32), shape(half, BF)]
            outs.append(shape_of((count * pad, full), BF))
            return call(
                functools.partial(front_body, n, pad, first_block, count),
                outs + ([] if first_block else [shape_of((columns, full), BF)]),
                ins,
                specs=[SM] + [VM] * (len(ins) - 1),
                name="front",
            )

        gb0, gp0, gs0, sp0, pm = step(functools.partial(front, 0, 2), meta, c0, c1, wo, gu0)

        def flip(*ins):
            return call(
                flip_body,
                [shape_of((width, samples * full), BF)],
                ins,
                [pltpu.VMEM((samples * full, width), BF)],
                name="flip",
            )

        (flipped,) = step(flip, *normed)
        c2 = step(None, c2)
        c3 = over_seq(c2, 1)
        gb1, gp1, gs1, sp1 = step(functools.partial(front, 2, 1), meta, c2, wo, gu1, pm)

        def prepare(*ins):
            square_bf = shape_of((full, full), BF)
            last = [shape_of((samples * pad, c), d) for c, d in ((width, BF), (half, F32))]
            return call(
                functools.partial(prepare_body, n, pad),
                [*last, images, big_f32, square_bf],
                ins,
                [pltpu.VMEM((full, full), BF)],
                specs=[SM] + [VM] * (len(ins) - 1),
                name="prepare",
            )

        clock = step(tick, clock)
        gb2, gp2, gs, gmix, sp = step(prepare, meta, c3, wo, gu2, pm, gs0, gs1, sp0, sp1)

        def spatial_unit(*ins):
            message = shape_of((pad + 32, columns), BF)
            return call(
                functools.partial(spatial_body, n, pad),
                [big_bf, big_bf, shape_of((128, 128), F32), square, shape_of((pad, columns), BF)]
                + [message] * (n - 1),
                ins,
                [
                    pltpu.VMEM((full, samples * half), BF),
                    pltpu.VMEM((full, samples * half), F32),
                    pltpu.VMEM((128, 128), F32),
                    pltpu.VMEM((2 * samples * n, pad, 128), F32),
                ],
                specs=[SM] + [VM] * (len(ins) - 1),
                name="spatial",
            )

        prod, ghu, cols, st2, edge, *messages = step(
            spatial_unit, meta, v0, v1, v2, gu0, gu1, gu2, dgu0, dgu1, dgu2, sp, gp0, gp1, gp2, gs, pm,
            gmix, g2, s2, *stats,
        )
        messages = [over_seq(x, k) for k, x in enumerate(messages, 1)]

        def weights(*ins):
            return call(
                weights_body,
                [shape_of((2 * shard, half), BF)] * 4 + [shape_of((width, half), F32)],
                ins,
                [pltpu.VMEM((width, half), F32)],
                specs=[SM] + [VM] * (len(ins) - 1),
                name="weights",
            )

        def norm_shares(*ins):
            return call(sums_body, [shape_of((8, width), F32)], ins, name="norm_shares")

        def back(*ins):
            return call(
                functools.partial(back_body, n, pad),
                [big_bf] + [shape_of((shard + EXTRA, half), BF)] * 4,
                ins,
                [
                    pltpu.VMEM((128, 128), F32),
                    pltpu.VMEM((128, 128), F32),
                    pltpu.VMEM((width, half), F32),
                    pltpu.VMEM((2, CHUNK, half), F32),
                    pltpu.VMEM((4, EXTRA, half), F32),
                ],
                specs=[SM] + [VM] * (len(ins) - 1),
                name="back",
            )

        def rows_out(*ins):
            shape = (2 * samples, rows, width)
            outs = [shape_of(s, BF) for s in (shape, shape, (4 * samples, rows, width))]
            return call(functools.partial(rows_body, n, pad), outs, ins, name="rows_out")

        def finish_rows(*ins):
            shape = shape_of(tokens.shape, BF)
            return call(
                finish_rows_body, [shape, shape], ins, specs=[SM] + [VM] * 6, name="finish_rows"
            )

        wide_shapes = shape_of((width, 2 * gate), F32), shape_of((gate, width), F32)

        def place(fresh, which_wu, which_v, *ins):
            count = len(which_wu) + len(which_v)
            return call(
                functools.partial(place_body, half, gate, fresh, which_wu, which_v),
                wide_shapes,
                ins,
                [
                    pltpu.VMEM((2 * len(which_wu), shard, half), F32),
                    pltpu.VMEM((2 * len(which_wu), half, shard), F32),
                    pltpu.SemaphoreType.DMA((4 * len(which_wu),)),
                    pltpu.VMEM((max(2 * len(which_v), 1), shard, half), F32),
                    pltpu.SemaphoreType.DMA((max(2 * len(which_v), 1),)),
                ],
                specs=[SM] + [VM] * count + ([] if fresh else [HB] * 2),
                out_specs=[HB] * 2,
                input_output_aliases={} if fresh else {1 + count: 0, 2 + count: 1},
                name="place",
            )

        def place_last(which, *ins):
            one, two = shape_of((width,), F32), shape_of((gate,), F32)
            small = [shape_of((rows, n * rows), F32), shape_of((rows,), F32), one, one, two, two]
            return call(
                functools.partial(place_last_body, half, gate, which),
                [shape_of((width, 2 * gate), F32)] + small,
                ins,
                [
                    pltpu.VMEM((2 * len(which), shard, half), F32),
                    pltpu.VMEM((pad, columns), F32),
                    pltpu.VMEM((4, n, EXTRA - pad // 4, half), F32),
                    *(pltpu.VMEM(s.shape, F32) for s in small),
                    pltpu.SemaphoreType.DMA((2 * len(which),)),
                    pltpu.SemaphoreType.DMA((len(small),)),
                ],
                specs=[SM] + [VM] * 8 + [HB, VM],
                out_specs=[HB] * 7,
                input_output_aliases={9: 0},
                name="place_last",
            )

        def twin(x):
            return over_seq(x, 1)

        x = dict(messages=messages, clock=clock)

        def ev_tick():
            x["clock"] = step(tick, x["clock"])

        def reduce_start(key, shards):
            x[key] = shards[0]
            for rho in range(1, 4):
                x[f"{key}{rho}"] = over_dp(shards[rho], rho)

        def ev_weights():
            *x["a_shards"], x["uw"] = step(weights, meta, prod, gb0, gb1, gb2, ghu, flipped)

        def ev_a_send():
            reduce_start("a", step(None, x["a_shards"]))

        def ev_sums():
            (x["sums"],) = step(norm_shares, wu, x["uw"], ghu)

        def ev_stats():
            x["messages"] = step(None, x["messages"])

        def ev_back():
            x["ghv"], *x["v_shards"] = step(
                back, meta, gmix, v0, v1, v2, dgv0, dgv1, dgv2, cols, st2, edge, *x["messages"], g1, s1,
                g2, flipped, wv, x["sums"],
            )

        def ev_v_send():
            reduce_start("v", step(None, x["v_shards"]))

        def ev_rows():
            x["r_a"], x["r_b"], send = step(rows_out, prod, wo, ghu, x["ghv"], wu, wv)
            x["r_got"] = twin(send)

        def ev_rows_core():
            x["r_last"] = over_seq(step(lambda a, b: add(a, b[2 * samples :]), x["r_b"], x["r_got"]), 2)

        def ev_finish():
            x["output"], x["grad_tokens"] = step(
                finish_rows, meta, t0, c0, x["r_a"], x["r_got"], x["r_last"], g1
            )

        def ev_rs(k):
            x[k] = step(add, x[k], x[k + "1"], x[k + "2"], x[k + "3"])
            x[k + "z"] = over_dp(x[k], 4) if m > 4 else None

        def ev_z2(k):
            flip = 8
            while flip <= m:
                x[k] = step(add, x[k], x[k + "z"])
                if flip < m:
                    x[k + "z"] = over_dp(x[k], flip)
                flip *= 2
            x[k + "z"] = over_dp(x[k], 2)

        def ev_pair(k):
            x[k + "p0"] = step(pair_up, x[k], x[k + "z"])
            x[k + "p1"], x[k + "p2"] = mixed_axes(x[k + "p0"], 0), mixed_axes(x[k + "p0"], 1)

        def ev_mark(k):
            x[k + "p1"], x[k + "p2"] = step(None, (x[k + "p1"], x[k + "p2"]))
            x[k + "p3"] = mixed_axes(x[k + "p1"], 1)

        def ev_third(k):
            x[k + "p3"] = step(None, x[k + "p3"])

        def ev_twin(k, j):
            x[f"{k}q{j}"] = twin(x[f"{k}p{j}"])

        def ev_got(k, j):
            x[f"{k}q{j}"] = step(None, x[f"{k}q{j}"])

        def pieces(k, which):
            return [x[f"{k}{'pq'[j // 4]}{j % 4}"] for j in which]

        def ev_place(fresh, which_wu, which_v):
            ins = [*pieces("a", which_wu), *pieces("v", which_v)]
            ins += [] if fresh else [x["w_in"], x["w_out"]]
            x["w_in"], x["w_out"] = step(
                functools.partial(place, fresh, which_wu, which_v), meta, *ins
            )

        def ev_place_last():
            ins = [x[f"vp{j}"] for j in range(4)] + [x[f"vq{j}"] for j in range(4)]
            x["w_in"], x["spatial"], *x["small"] = step(
                functools.partial(place_last, (3, 7)), meta, *ins, x["w_in"], x["clock"]
            )

        events = dict(
            weights=ev_weights, sums=ev_sums, stats=ev_stats, back=ev_back,
            rows=ev_rows, rows_core=ev_rows_core, finish=ev_finish,
            place_last=ev_place_last,
            place_own=functools.partial(ev_place, True, (0, 4), (0, 4)),
            place_near=functools.partial(ev_place, False, (1, 2, 5, 6), ()),
            place_far=functools.partial(ev_place, False, (3, 7), (1, 2, 5, 6)),
            place_head=functools.partial(ev_place, True, (0, 1, 2, 4, 5, 6), ()),
            place_most=functools.partial(ev_place, False, (3, 7), (0, 1, 2, 4, 5, 6)),
            a_send=ev_a_send, v_send=ev_v_send, tick=ev_tick,
        )
        for k in ("a", "v"):
            for name, f in (("rs", ev_rs), ("z2", ev_z2), ("pair", ev_pair), ("mark", ev_mark), ("third", ev_third)):
                events[f"{k}_{name}"] = functools.partial(f, k)
            for j in range(4):
                events[f"{k}_twin{j}"] = functools.partial(ev_twin, k, j)
                events[f"{k}_got{j}"] = functools.partial(ev_got, k, j)
        for name in ORDER:
            events[name]()
        output, grad_tokens, grad_w_in, grad_w_out = (
            x[k] for k in ("output", "grad_tokens", "w_in", "w_out")
        )
        grad_spatial, sums = x["spatial"], x["small"]
        return (output, grad_tokens, grad_w_in, grad_w_out, grad_spatial, *sums)

    placed = (
        P("dp", "seq", None),
        P("dp"),
        P("dp"),
        P(),
        P(),
        P("seq", None),
        P("seq"),
        P(),
        P(),
        P(),
        P(),
        P("dp", "seq", None),
    )
    return jax.shard_map(
        shards,
        mesh=mesh,
        in_specs=placed,
        out_specs=(
            P("dp", "seq", None),
            P("dp", "seq", None),
            P(),
            P(),
            P("seq", None),
            P("seq"),
            P(),
            P(),
            P(),
            P(),
        ),
        check_vma=False,
    )
```

```python
import functools

import jax
import jax.numpy as jnp
from jax import lax
from jax.experimental import pallas as pl
from jax.experimental.pallas import tpu as pltpu
from jax.sharding import PartitionSpec as P

PATCHES = 324
SMALL_P = 100
MID_P = 196

EPSILON = 1e-05
SURVIVAL = 0.9

BF = jnp.bfloat16
F32 = jnp.float32
CHUNK = 16
VM = pl.BlockSpec(memory_space=pltpu.VMEM)
SM = pl.BlockSpec(memory_space=pltpu.SMEM)
HB = pl.BlockSpec(memory_space=pltpu.HBM)


ORDER = (
    "weights", "a_send", "sums", "tick", "stats", "back", "v_send", "rows", "a_rs", "tick", "tick", "tick",
    "rows_core", "v_rs", "a_z2", "v_z2", "a_pair", "tick", "v_pair", "finish", "a_mark", "tick", "v_mark", "tick",
    "a_twin0", "a_twin1", "a_twin2", "place_head", "a_third", "a_twin3", "v_third", "v_twin3", "v_twin0", "v_twin1",
    "v_twin2", "tick", "place_most", "place_last",
)


def round_up(size, multiple):
    return -(-size // multiple) * multiple


def dot(a, b, ca, cb):
    return lax.dot_general(a, b, (((ca,), (cb,)), ((), ())), preferred_element_type=F32)


def iota(shape, axis):
    return lax.broadcasted_iota(jnp.int32, shape, axis)


def rows_at(start, size, multiple):
    return pl.ds(pl.multiple_of(start, multiple), size)


def call(body, outs, ins, scratch=(), specs=None, out_specs=None, flops=1, **more):
    return pl.pallas_call(
        body,
        out_shape=outs,
        in_specs=specs if specs is not None else [VM] * len(ins),
        out_specs=out_specs if out_specs is not None else [VM] * len(outs),
        scratch_shapes=list(scratch),
        compiler_params=pltpu.CompilerParams(vmem_limit_bytes=20 * 2**20),
        cost_estimate=pl.CostEstimate(flops=flops, bytes_accessed=1, transcendentals=0),
        **more,
    )(*ins)


def shape_of(shape, dtype):
    return jax.ShapeDtypeStruct(shape, dtype)


def add_body(*refs):
    total = refs[0][...].astype(F32)
    for ref in refs[1:-1]:
        total = total + ref[...].astype(F32)
    refs[-1][...] = total.astype(BF)


def tick_body(clock, out):
    out[...] = clock[...] + 1.0


def pair_body(a, b, out):
    out[0] = a[...]
    out[1] = b[...]


def project_body(pad, first_block, *refs):
    refs = list(refs)
    n_tok = len(refs) - 13 - (1 if first_block else 0)
    toks, refs = refs[:n_tok], refs[n_tok:]
    g1, s1, wu, wv = refs[:4]
    refs = refs[4:]
    if first_block:
        st_in, refs = refs[0], refs[1:]
    normed, gu, dgu, v, dgv, st, xs, hid, tile = refs
    samples, rows, width = toks[0].shape
    half = wu.shape[1]
    size = samples * pad
    found = [jnp.zeros((CHUNK, 128), F32)] * (128 // CHUNK)
    low = rows // 8 * 8
    gain, shift = g1[...], s1[...]
    for b, tok in enumerate(toks):
        for i in range(samples):
            base = (b * samples + i) * pad
            xs[base + low : base + pad, :] = jnp.zeros((pad - low, width), F32)
            xs[base : base + rows, :] = tok[i].astype(F32)
            for c in range(base, base + pad, CHUNK):
                x = xs[c : c + CHUNK, :]
                center = x - jnp.mean(x, axis=-1, keepdims=True)
                inverse = lax.rsqrt(jnp.mean(center * center, axis=-1, keepdims=True) + EPSILON)
                normed[c : c + CHUNK, :] = (center * inverse * gain + shift).astype(BF)
        at = slice(b * size, (b + 1) * size)
        hid[at, 0:half] = dot(normed[at, :], wu[...], 1, 0)
        hid[at, half:] = dot(normed[at, :], wv[...], 1, 0)
    c0 = 0.7978845608028654
    c1 = 0.7978845608028654 * 0.044715

    def gelu_pair(h):
        a = (c1 * h) * h
        s = 0.5 + 0.5 * jnp.tanh(h * (c0 + a))
        g = h * s
        return g, s + (2.0 * g) * (1.0 - s) * (c0 + 3.0 * a)

    lane = iota((CHUNK, 128), 1)
    for b in range(len(toks)):
        for i in range(samples):
            base = (b * samples + i) * pad
            blk = 2 * (i * 4 + first_block + b)
            for c in range(pad // CHUNK):
                at = slice(base + c * CHUNK, base + (c + 1) * CHUNK)
                g, d = gelu_pair(hid[at, 0:half])
                gu[at, :] = g.astype(BF)
                dgu[at, :] = d.astype(BF)
                g, d = gelu_pair(hid[at, half:])
                v[at, :] = g
                dgv[at, :] = d.astype(BF)
                mean = jnp.mean(g, axis=-1, keepdims=True)
                center = g - mean
                square = jnp.sum(center * center, axis=-1, keepdims=True)
                found[c] = jnp.where(
                    lane == blk, mean, jnp.where(lane == blk + 1, square, found[c])
                )
    for c, part_found in enumerate(found):
        tile[c * CHUNK : (c + 1) * CHUNK, :] = part_found
    flipped = jnp.transpose(tile[...])[0 : st.shape[0], :]
    st[...] = flipped + st_in[...] if first_block else flipped


def project(pad, first_block, toks, g1, s1, wu, wv, st_in=None):
    samples, rows, width = toks[0].shape
    half = wu.shape[1]
    n_rows = len(toks) * samples * pad
    outs = [
        shape_of((n_rows, width), BF),
        shape_of((n_rows, half), BF),
        shape_of((n_rows, half), BF),
        shape_of((n_rows, half), F32),
        shape_of((n_rows, half), BF),
        shape_of((round_up(samples * 8, 8), 128), F32),
    ]
    scratch = [
        pltpu.VMEM((n_rows, width), F32),
        pltpu.VMEM((n_rows, 2 * half), F32),
        pltpu.VMEM((128, 128), F32),
    ]
    ins = [*toks, g1, s1, wu, wv] + ([st_in] if first_block else [])
    return call(
        functools.partial(project_body, pad, first_block),
        outs,
        ins,
        scratch,
        name="project",
    )


GROUPS = ((0, 1), (2,), (3,))


def part(r, i, samples, pad):
    for k, blocks in enumerate(GROUPS):
        if r in blocks:
            return k, ((r - blocks[0]) * samples + i) * pad


def group_rows(size):
    return [slice(blocks[0] * size, (blocks[-1] + 1) * size) for blocks in GROUPS]


def position_map(seq, rows, pad, n, columns):
    a = iota((columns, n * pad), 0)
    j = iota((columns, n * pad), 1)
    r = jnp.zeros_like(j)
    for k in range(1, n):
        r = r + (j >= k * pad).astype(jnp.int32)
    q = j - r * pad
    hit = (a == (r ^ seq) * rows + q) & (q < rows)
    hit = hit | ((a == n * rows) & (j == pad - 1)) | ((a == n * rows + 1) & (j == pad - 2))
    return jnp.where(hit, 1.0, 0.0).astype(BF)


def patch_count(meta, i):
    kind = meta[2 + i]
    return jnp.where(kind == 0, SMALL_P, jnp.where(kind == 1, MID_P, PATCHES))


def branch_scale(meta, i, samples, where):
    keep = jnp.where(where < patch_count(meta, i), meta[2 + samples + i], 0)
    return keep.astype(F32) / SURVIVAL


def valid_rows(meta, i, r, c, rows):
    p = c * CHUNK + iota((CHUNK, 1), 0)
    return (p < rows) & ((meta[0] ^ r) * rows + p < patch_count(meta, i))


def front_rows(pad, first_block, meta, cots, wo, gu, gb, gp, put):
    width = cots[0].shape[1]
    rows = PATCHES // 4
    samples = cots[0].shape[0] // rows - 1
    low = rows // 16 * 16
    size = samples * pad
    for b, cot in enumerate(cots):
        where = (meta[0] ^ (first_block + b)) * rows + iota((rows, 1), 0)
        for i in range(samples):
            base = b * size + i * pad
            scale = branch_scale(meta, i, samples, where)
            gb[base + low : base + pad, :] = jnp.zeros((pad - low, width), BF)
            gb[base : base + rows, :] = (cot[i * rows : (i + 1) * rows, :].astype(F32) * scale).astype(BF)
        at = slice(b * size, (b + 1) * size)
        gp[at, :] = dot(gb[at, :], wo[...], 1, 1)
        for i in range(samples):
            for c in range(0, pad, CHUNK):
                at = slice(b * size + i * pad + c, b * size + i * pad + c + CHUNK)
                put(b, i, c, (gp[at, :] * gu[at, :].astype(F32)).astype(BF))


def matrix_rows(pad, block, cot, pm, sp):
    rows = PATCHES // 4
    low = rows // 16 * 16
    sp[block * pad + low : (block + 1) * pad, :] = jnp.zeros((pad - low, sp.shape[1]), BF)
    out = dot(cot[cot.shape[0] - rows :, 0 : pm.shape[0]], pm[...], 1, 0)
    sp[block * pad : block * pad + rows, :] = out.astype(BF)


def front_body(n, pad, first_block, count, meta, *refs):
    cots, refs = refs[:count], refs[count:]
    if first_block:
        wo, gu, pm, gb, gp, gs, sp = refs
    else:
        wo, gu, gb, gp, gs, sp, pm = refs
        pm[...] = position_map(meta[0], PATCHES // n, pad, n, pm.shape[0])
    samples = cots[0].shape[0] // (PATCHES // n) - 1

    def put(b, i, c, out):
        base = (b * samples + i) * pad + c
        gs[base : base + CHUNK, :] = out

    front_rows(pad, first_block, meta, cots, wo, gu, gb, gp, put)
    for b, cot in enumerate(cots):
        matrix_rows(pad, b, cot, pm, sp)


def prepare_body(n, pad, meta, c3, wo, gu2, pm, gs0, gs1, sp0, sp1, gb, gp, gs, gmix, sp, spt):
    rows = PATCHES // n
    samples = c3.shape[0] // rows - 1
    most = (n - 1) * pad
    sp[0 : sp0.shape[0], :] = sp0[...]
    sp[sp0.shape[0] : most, :] = sp1[...]
    matrix_rows(pad, n - 1, c3, pm, sp)
    spt[...] = jnp.transpose(sp[...].astype(F32)).astype(BF)

    half = gp.shape[1]

    def put(b, i, c, out):
        gs[most + c : most + c + CHUNK, i * half : (i + 1) * half] = out

    front_rows(pad, n - 1, meta, (c3,), wo, gu2, gb, gp, put)
    for i in range(samples):
        for r in range(n - 1):
            k, base = part(r, i, samples, pad)
            here = slice(i * half, (i + 1) * half)
            gs[r * pad : (r + 1) * pad, here] = (gs0, gs1)[k][base : base + pad, :]
    full = dot(spt[...], gs[...], 1, 0)
    for i in range(samples):
        for r in range(n):
            base = (r * samples + i) * pad
            for c in range(pad // CHUNK):
                at = slice(r * pad + c * CHUNK, r * pad + (c + 1) * CHUNK)
                out = full[at, i * half : (i + 1) * half]
                out = jnp.where(valid_rows(meta, i, r, c, rows), out, 0.0)
                gmix[base + c * CHUNK : base + (c + 1) * CHUNK, :] = out


def own_lanes(rows, seq, half):
    count = half // 128
    return jnp.concatenate([rows[pl.ds(seq * count + k, 1), :] for k in range(count)], axis=1)


def lane_sum(x):
    total = x[:, 0:128]
    for k in range(1, x.shape[1] // 128):
        total = total + x[:, k * 128 : (k + 1) * 128]
    return total


def row_sum(x):
    ones = jnp.ones((8, x.shape[1]), BF)
    high = x.astype(BF)
    low = (x - high.astype(F32)).astype(BF)
    return dot(ones, high, 1, 1) + dot(ones, low, 1, 1)


def row_sums(parts, st, pad):
    blocks = parts.shape[0] // 2
    for b in range(blocks):
        for j in range(2):
            st[2 * b + j : 2 * b + j + 1, 0:pad] = row_sum(parts[j * blocks + b])[0:1, :]


def pack_sums(st):
    x = jnp.concatenate([st[8 * k : 8 * (k + 1), :] for k in range(3)], axis=1)
    terms = []
    for _ in range(3):
        terms.append(x.astype(BF).astype(F32))
        x = x - terms[-1]
    return jnp.concatenate(terms + [jnp.zeros_like(x)], axis=0).astype(BF)


def unpack_sums(packed):
    x = packed.astype(F32)
    x = (x[16:24] + x[8:16]) + x[0:8]
    return jnp.concatenate([x[:, 128 * k : 128 * (k + 1)] for k in range(3)], axis=0)


def spatial_body(
    n, pad, meta, v0, v1, v2, gu0, gu1, gu2, dgu0, dgu1, dgu2, sp, gp0, gp1, gp2, gs, pm, gmix, g2, s2, t0, t1, t2, t3,
    prod, ghu, cols, st, edge, m1, m2, m3,
    mixed, so, tile, parts,
):
    half, rows = gp0.shape[1], PATCHES // n
    samples = gs.shape[1] // half
    gps = (gp0, gp1, gp2)
    whole = half * n
    stats, vs, gus, dgus = (t0, t1, t2, t3), (v0, v1, v2), (gu0, gu1, gu2), (dgu0, dgu1, dgu2)
    tile[...] = jnp.zeros_like(tile)
    for i in range(samples):
        for r in range(n):
            at = [2 * (i * n + (r ^ k)) for k in range(n)]
            means = [stats[k][at[k] : at[k] + 1, :] for k in range(n)]
            squares = [stats[k][at[k] + 1 : at[k] + 2, :] for k in range(n)]
            mean = ((means[0] + means[1]) + (means[2] + means[3])) / n
            spread = (squares[0] + squares[1]) + (squares[2] + squares[3])
            for k in range(n):
                spread = spread + half * (means[k] - mean) * (means[k] - mean)
            blk = 2 * (i * n + r)
            tile[blk : blk + 1, :] = mean
            tile[blk + 1 : blk + 2, :] = lax.rsqrt(spread / whole + EPSILON)
    cols[...] = jnp.transpose(tile[...])
    gain, shift = own_lanes(g2, meta[0], half), own_lanes(s2, meta[0], half)
    for i in range(samples):
        for r in range(n):
            k, base = part(r, i, samples, pad)
            first = (r * samples + i) * pad
            blk = 2 * (i * n + r)
            for c in range(pad // CHUNK):
                here = slice(c * CHUNK, (c + 1) * CHUNK)
                mean, inverse = cols[here, blk : blk + 1], cols[here, blk + 1 : blk + 2]
                standard = (vs[k][base + c * CHUNK : base + (c + 1) * CHUNK, :] - mean) * inverse
                out = jnp.where(valid_rows(meta, i, r, c, rows), standard * gain + shift, 0.0)
                if r == 0 and (c + 1) * CHUNK == pad:
                    p = c * CHUNK + iota((CHUNK, 1), 0)
                    out = jnp.where(p >= pad - 2, 1.0, out)
                at = slice(r * pad + c * CHUNK, r * pad + (c + 1) * CHUNK)
                mixed[at, i * half : (i + 1) * half] = out.astype(BF)
                t = gmix[first + c * CHUNK : first + (c + 1) * CHUNK, :] * gain
                parts[i * n + r, here, :] = lane_sum(t)
                parts[samples * n + i * n + r, here, :] = lane_sum(t * standard)
    so[...] = dot(sp[...], mixed[...], 1, 0)
    row_sums(parts, st, pad)
    total = dot(gs[...], mixed[...], 1, 1)
    placed = dot(total.astype(BF), pm[...], 1, 1).astype(BF)
    packed = pack_sums(st)
    edge[...] = placed[0:pad, :]
    for r, message in enumerate((m1, m2, m3), 1):
        message[0:pad, :] = placed[r * pad : (r + 1) * pad, :]
        message[pad:, :] = packed
    for i in range(samples):
        for r in range(n):
            k, base = part(r, i, samples, pad)
            first = (r * samples + i) * pad
            for c in range(0, pad, CHUNK):
                src = slice(base + c, base + c + CHUNK)
                at = slice(first + c, first + c + CHUNK)
                s = so[r * pad + c : r * pad + c + CHUNK, i * half : (i + 1) * half]
                prod[at, :] = (gus[k][src, :].astype(F32) * s).astype(BF)
                ghu[at, :] = (gps[k][src, :] * s * dgus[k][src, :].astype(F32)).astype(BF)


def weight_sum(lefts, rights):
    total = None
    for left, right in zip(lefts, rights):
        term = dot(left, right, 0, 0)
        total = term if total is None else total + term
    return total


def store_shards(dp, whole, outs, base):
    shard = whole.shape[0] // 4
    for rho, out in enumerate(outs):
        here = whole[rows_at(((dp ^ rho) & 3) * shard, shard, 16), :]
        out[base : base + shard, :] = here.astype(BF)


def norm_sums(w, grad_w, grads):
    columns = None
    for c in range(0, grads.shape[0], CHUNK):
        g = grads[c : c + CHUNK, :].astype(F32)
        columns = g if columns is None else columns + g
    columns = jnp.sum(columns, axis=0, keepdims=True)
    first, second = [], []
    for c in range(w.shape[0] // CHUNK):
        at = slice(c * CHUNK, (c + 1) * CHUNK)
        x = w[at, :].astype(F32)
        first.append(lane_sum(x * grad_w[at, :]))
        second.append(lane_sum(x * columns))
    first = row_sum(jnp.concatenate(first, axis=0))
    second = row_sum(jnp.concatenate(second, axis=0))
    return jnp.where(iota(first.shape, 0) == 0, first, second)


def flip_body(n0, n1, n2, out, whole):
    base = 0
    for ref in (n0, n1, n2):
        whole[base : base + ref.shape[0], :] = ref[...]
        base += ref.shape[0]
    out[...] = jnp.transpose(whole[...])


def weights_body(meta, prod, gb0, gb1, gb2, ghu, flipped, s0, s1, s2, s3, uw, ow):
    groups = group_rows(prod.shape[0] // 4)
    outs = (s0, s1, s2, s3)
    ow[...] = weight_sum([g[...] for g in (gb0, gb1, gb2)], [prod[at, :] for at in groups])
    uw[...] = dot(flipped[...], ghu[...], 1, 0)
    store_shards(meta[1], ow, outs, 0)
    store_shards(meta[1], uw, outs, ow.shape[0] // 4)


def sums_body(w, grad_w, grads, out):
    out[...] = norm_sums(w, grad_w, grads)


EXTRA = 32


def back_body(
    n, pad, meta, gmix, v0, v1, v2, dgv0, dgv1, dgv2, cols, st, edge0, m1, m2, m3, g1, s1, g2, flipped,
    wv, first_sums,
    ghv, w0, w1, w2, w3,
    tile, col, vw, acc, extra,
):
    samples, half = gmix.shape[0] // (n * pad), gmix.shape[1]
    width = wv.shape[0]
    messages, vs, dgvs = (m1, m2, m3), (v0, v1, v2), (dgv0, dgv1, dgv2)
    stats = [st[...]] + [unpack_sums(m[pad:, :]) for m in messages]
    tile[...] = jnp.zeros_like(tile)
    for i in range(samples):
        for r in range(n):
            blk = 2 * (i * n + r)
            terms = [
                stats[k][2 * (i * n + (r ^ k)) : 2 * (i * n + (r ^ k)) + 2, :] for k in range(n)
            ]
            tile[blk : blk + 2, :] = ((terms[0] + terms[1]) + (terms[2] + terms[3])) / (half * n)
    col[...] = jnp.transpose(tile[...])
    gain = own_lanes(g2, meta[0], half)
    acc[...] = jnp.zeros_like(acc)
    for i in range(samples):
        for r in range(n):
            k, base = part(r, i, samples, pad)
            row = (r * samples + i) * pad
            blk = 2 * (i * n + r)
            for c in range(pad // CHUNK):
                here = slice(c * CHUNK, (c + 1) * CHUNK)
                at = slice(row + c * CHUNK, row + (c + 1) * CHUNK)
                src = slice(base + c * CHUNK, base + (c + 1) * CHUNK)
                mean, inverse = cols[here, blk : blk + 1], cols[here, blk + 1 : blk + 2]
                first, second = col[here, blk : blk + 1], col[here, blk + 1 : blk + 2]
                standard = (vs[k][src, :] - mean) * inverse
                g = gmix[at, :]
                out = inverse * (g * gain - first - standard * second)
                ghv[at, :] = (out * dgvs[k][src, :].astype(F32)).astype(BF)
                acc[0] += g * standard
                acc[1] += g
    vw[...] = dot(flipped[...], ghv[...], 1, 0)
    sums = first_sums[...] + norm_sums(wv, vw, ghv)
    shift_one = sums[1:2, :]
    gain_one = (sums[0:1, :] - s1[...] * shift_one) / g1[...]
    edge = edge0[...].astype(F32)
    for m in messages:
        edge = edge + m[0:pad, :].astype(F32)
    size = pad // 4
    extra[...] = jnp.zeros_like(extra)
    for k in range(4):
        extra[k, 0:size, :] = edge[k * size : (k + 1) * size, :]
    extra[0, size : size + 1, :] = jnp.sum(acc[0], axis=0, keepdims=True)
    extra[1, size : size + 1, :] = jnp.sum(acc[1], axis=0, keepdims=True)
    for k, row in ((2, gain_one), (3, shift_one)):
        extra[k, size : size + 1, :] = row[:, 0:half]
        extra[k, size + 1 : size + 2, 0 : width - half] = row[:, half:]
    outs = (w0, w1, w2, w3)
    store_shards(meta[1], vw, outs, 0)
    shard = vw.shape[0] // 4
    for rho, out in enumerate(outs):
        out[shard:, :] = extra[(meta[1] ^ rho) & 3].astype(BF)


def rows_body(n, pad, prod, wo, ghu, ghv, wu, wv, keep_a, keep_b, send):
    samples, rows = keep_a.shape[0] // 2, keep_a.shape[1]
    places = ((keep_a, 0), (send, 0), (keep_b, 0), (send, 2 * samples))
    for r, (out, first) in enumerate(places):
        at = slice(r * samples * pad, (r + 1) * samples * pad)
        branch = dot(prod[at, :], wo[...], 1, 0)
        grad = dot(ghu[at, :], wu[...], 1, 1) + dot(ghv[at, :], wv[...], 1, 1)
        for i in range(samples):
            out[first + i] = branch[i * pad : i * pad + rows, :].astype(BF)
            out[first + samples + i] = grad[i * pad : i * pad + rows, :].astype(BF)


def finish_rows_body(meta, tok, cot, keep, got_a, got_b, g1, output, grad_tokens):
    samples, rows = tok.shape[0], tok.shape[1]
    gain = g1[...]
    p = meta[0] * rows + iota((rows, 1), 0)
    for i in range(samples):
        x = tok[i].astype(F32)
        total = keep[i].astype(F32) + got_a[i].astype(F32) + got_b[i].astype(F32)
        output[i] = (x + branch_scale(meta, i, samples, p) * total).astype(BF)
        center = x - jnp.mean(x, axis=-1, keepdims=True)
        inverse = lax.rsqrt(jnp.mean(center * center, axis=-1, keepdims=True) + EPSILON)
        standard = center * inverse
        k = samples + i
        t = (keep[k].astype(F32) + got_a[k].astype(F32) + got_b[k].astype(F32)) * gain
        first = jnp.mean(t, axis=-1, keepdims=True)
        second = jnp.mean(t * standard, axis=-1, keepdims=True)
        grad = cot[i * rows : (i + 1) * rows, :].astype(F32) + inverse * (t - first - standard * second)
        grad_tokens[i] = grad.astype(BF)


def sources(meta):
    seq, shard = meta[0], meta[1] & 3
    out = []
    for flip in (0, 1):
        s = seq ^ flip
        core = s & 1
        out += [
            (shard, s),
            (shard ^ (1 - core), s ^ (2 * core)),
            (shard ^ core, s ^ (2 * (1 - core))),
            (shard ^ 1, s ^ 2),
        ]
    return out


def place_wu(half, meta, pieces, which, w_in, w_out, wide, tall, sems):
    shard = wide.shape[1]
    copies = []
    origins = sources(meta)
    for piece, k in zip(pieces, which):
        group, seq = origins[k]
        for e in range(2):
            slot = len(copies) // 2
            row = (group ^ (2 * e)) * shard
            columns = rows_at(seq * half, half, 128)
            tall[slot] = jnp.transpose(piece[e, 0:shard, :].astype(F32))
            target = w_out.at[columns, rows_at(row, shard, 128)]
            copies.append(pltpu.make_async_copy(tall.at[slot], target, sems.at[2 * slot]))
            copies[-1].start()
            wide[slot] = piece[e, shard:, :].astype(F32)
            target = w_in.at[rows_at(row, shard, 16), columns]
            copies.append(pltpu.make_async_copy(wide.at[slot], target, sems.at[2 * slot + 1]))
            copies[-1].start()
    return copies


def place_v(half, gate, meta, pieces, which, w_in, wide, sems):
    shard = wide.shape[1]
    copies = []
    origins = sources(meta)
    for piece, k in zip(pieces, which):
        group, seq = origins[k]
        for e in range(2):
            slot = len(copies)
            wide[slot] = piece[e, 0:shard, :].astype(F32)
            columns = rows_at(gate + seq * half, half, 128)
            target = w_in.at[rows_at((group ^ (2 * e)) * shard, shard, 16), columns]
            copies.append(pltpu.make_async_copy(wide.at[slot], target, sems.at[slot]))
            copies[-1].start()
    return copies


def place_body(half, gate, fresh, which_wu, which_v, meta, *refs):
    *pieces, w_in, w_out, wide, tall, sems, more, more_sems = refs
    if not fresh:
        pieces = pieces[:-2]
    count = len(which_wu)
    copies = place_wu(half, meta, pieces[:count], which_wu, w_in, w_out, wide, tall, sems)
    copies += place_v(half, gate, meta, pieces[count:], which_v, w_in, more, more_sems)
    for copy in copies:
        copy.wait()


def place_last_body(half, gate, which, meta, *refs):
    pieces = refs[:8]
    w_in, *targets, wide, edge, norms = refs[10:20]
    spatial, bias, gain_one, shift_one, gain_two, shift_two, sems, small_sems = refs[20:]
    shard = wide.shape[1]
    rows, patches = spatial.shape
    size = edge.shape[0] // 4
    core = meta[0] & 1
    copies = place_v(half, gate, meta, [pieces[k] for k in which], which, w_in, wide, sems)
    small = []
    for k, (group, seq) in enumerate(sources(meta)):
        for e in range(2):
            at = group ^ (2 * e)
            rest = pieces[k][e, shard:, :].astype(F32)
            small.append((at, rest[0:size]))
            norms[at, seq] = rest[size:]
    for e in range(2):
        at, own = small[e]
        edge[rows_at(at * size, size, 8), :] = own
        at = (meta[1] & 3) ^ 1 ^ (2 * e)
        edge[rows_at(at * size, size, 8), :] = jnp.where(core == 0, small[2 + e][1], small[4 + e][1])
    spatial[...] = edge[0:rows, 0:patches]
    first = patches // 128 * 128
    tail = edge[0:rows, first:]
    column = jnp.sum(
        jnp.where(iota(tail.shape, 1) == patches - first, tail, 0.0), axis=1, keepdims=True
    )
    diagonal = iota((rows, rows), 0) == iota((rows, rows), 1)
    bias[...] = jnp.sum(jnp.where(diagonal, column, 0.0), axis=0)
    for at, out in ((2, gain_one), (3, shift_one)):
        total = (norms[at, 0] + norms[at, 1]) + (norms[at, 2] + norms[at, 3])
        out[0:half] = total[0, :]
        out[half:] = total[1, 0 : out.shape[0] - half]
    for at, out in ((0, gain_two), (1, shift_two)):
        for j in range(4):
            out[j * half : (j + 1) * half] = norms[at, j, 0, :]
    smalls = (spatial, bias, gain_one, shift_one, gain_two, shift_two)
    for k, (source, target) in enumerate(zip(smalls, targets)):
        copies.append(pltpu.make_async_copy(source, target, small_sems.at[k]))
        copies[-1].start()
    for copy in copies:
        copy.wait()


def solution(mesh):
    n, m = mesh.shape["seq"], mesh.shape["dp"]

    def over_seq(x, flip):
        return lax.ppermute(x, "seq", [(i, i ^ flip) for i in range(n)])

    def over_dp(x, flip):
        return lax.ppermute(x, "dp", [(i, i ^ flip) for i in range(m)])

    def mixed_axes(x, core_of_x):
        pairs = []
        for d in range(m):
            for s in range(n):
                other = (d ^ 1, s) if s & 1 == core_of_x else (d, s ^ 2)
                pairs.append((d * n + s, other[0] * n + other[1]))
        return lax.ppermute(x, ("dp", "seq"), pairs)

    def add(*terms):
        total = terms[0].astype(F32)
        for t in terms[1:]:
            total = total + t.astype(F32)
        return total.astype(BF)

    def pair_up(*terms):
        return jnp.stack(terms)

    def ordered():
        last = []

        def step(body, *ins):
            if last:
                ins, _ = lax.optimization_barrier((ins, last[0]))
            out = body(*ins) if body else ins[0]
            last[:] = [jax.tree.leaves(out)[0]]
            return out

        return step

    def shards(
        tokens,
        res_class,
        skip_mask,
        w_in,
        w_out,
        spatial,
        spatial_bias,
        gain_one,
        shift_one,
        gain_two,
        shift_two,
        cotangent,
    ):
        samples, rows, width = tokens.shape
        gate = w_out.shape[0]
        half = gate // n
        pad = round_up(rows + 2, 16)
        full = n * pad
        columns = round_up(n * rows + 2, 128)
        seq, dp = lax.axis_index("seq"), lax.axis_index("dp")
        meta = jnp.concatenate([seq[None], dp[None], res_class, skip_mask]).astype(jnp.int32)
        step = ordered()
        clock = jnp.zeros((8, 128), F32)

        def tick(clock):
            return call(tick_body, [shape_of(clock.shape, F32)], [clock], flops=4 * 10**9, name="tick")[0]

        big_bf, big_f32 = (shape_of((samples * full, half), d) for d in (BF, F32))
        images = shape_of((full, samples * half), BF)
        shard = width // 4
        square = shape_of((round_up(samples * 2 * n, 8), 128), F32)

        t0 = tokens
        t2 = over_seq(t0, 2)
        t1 = over_seq(t0, 1)
        high = lax.reduce_precision(spatial_bias, 8, 7)
        side = jnp.stack([high, spatial_bias - high], axis=1).astype(BF)
        packed = jnp.concatenate([spatial, side], axis=1)
        packed = jnp.pad(packed, ((0, 0), (0, width - packed.shape[1])))
        c0 = jnp.concatenate([cotangent.reshape(-1, width), packed])
        c2 = over_seq(c0, 2)
        wu = lax.dynamic_slice(w_in, (0, seq * half), (width, half))
        wv = lax.dynamic_slice(w_in, (0, gate + seq * half), (width, half))
        wo = lax.dynamic_slice(w_out, (seq * half, 0), (half, width))
        g1, s1 = gain_one[None], shift_one[None]
        g2, s2 = gain_two.reshape(-1, 128), shift_two.reshape(-1, 128)
        meta, wu, wv, wo, c0, t1 = lax.optimization_barrier((meta, wu, wv, wo, c0, t1))
        c1 = over_seq(c0, 1)

        n0, gu0, dgu0, v0, dgv0, st = step(
            lambda *a: project(pad, 0, a[:2], *a[2:]), t0, t1, g1, s1, wu, wv
        )
        t2 = step(None, t2)
        t3 = over_seq(t2, 1)
        n1, gu1, dgu1, v1, dgv1, st = step(
            lambda *a: project(pad, 2, a[:1], *a[1:]), t2, g1, s1, wu, wv, st
        )
        n2, gu2, dgu2, v2, dgv2, st = step(
            lambda *a: project(pad, 3, a[:1], *a[1:]), t3, g1, s1, wu, wv, st
        )
        normed = [n0, n1, n2]
        stats = [st] + [over_seq(st, k) for k in range(1, n)]

        def front(first_block, count, *ins):
            def shape(columns, dtype):
                return shape_of((count * samples * pad, columns), dtype)

            outs = [shape(width, BF), shape(half, F32), shape(half, BF)]
            outs.append(shape_of((count * pad, full), BF))
            return call(
                functools.partial(front_body, n, pad, first_block, count),
                outs + ([] if first_block else [shape_of((columns, full), BF)]),
                ins,
                specs=[SM] + [VM] * (len(ins) - 1),
                name="front",
            )

        gb0, gp0, gs0, sp0, pm = step(functools.partial(front, 0, 2), meta, c0, c1, wo, gu0)

        def flip(*ins):
            return call(
                flip_body,
                [shape_of((width, samples * full), BF)],
                ins,
                [pltpu.VMEM((samples * full, width), BF)],
                name="flip",
            )

        (flipped,) = step(flip, *normed)
        c2 = step(None, c2)
        c3 = over_seq(c2, 1)
        gb1, gp1, gs1, sp1 = step(functools.partial(front, 2, 1), meta, c2, wo, gu1, pm)

        def prepare(*ins):
            square_bf = shape_of((full, full), BF)
            last = [shape_of((samples * pad, c), d) for c, d in ((width, BF), (half, F32))]
            return call(
                functools.partial(prepare_body, n, pad),
                [*last, images, big_f32, square_bf],
                ins,
                [pltpu.VMEM((full, full), BF)],
                specs=[SM] + [VM] * (len(ins) - 1),
                name="prepare",
            )

        clock = step(tick, clock)
        gb2, gp2, gs, gmix, sp = step(prepare, meta, c3, wo, gu2, pm, gs0, gs1, sp0, sp1)

        def spatial_unit(*ins):
            message = shape_of((pad + 32, columns), BF)
            return call(
                functools.partial(spatial_body, n, pad),
                [big_bf, big_bf, shape_of((128, 128), F32), square, shape_of((pad, columns), BF)]
                + [message] * (n - 1),
                ins,
                [
                    pltpu.VMEM((full, samples * half), BF),
                    pltpu.VMEM((full, samples * half), F32),
                    pltpu.VMEM((128, 128), F32),
                    pltpu.VMEM((2 * samples * n, pad, 128), F32),
                ],
                specs=[SM] + [VM] * (len(ins) - 1),
                name="spatial",
            )

        prod, ghu, cols, st2, edge, *messages = step(
            spatial_unit, meta, v0, v1, v2, gu0, gu1, gu2, dgu0, dgu1, dgu2, sp, gp0, gp1, gp2, gs, pm,
            gmix, g2, s2, *stats,
        )
        messages = [over_seq(x, k) for k, x in enumerate(messages, 1)]

        def weights(*ins):
            return call(
                weights_body,
                [shape_of((2 * shard, half), BF)] * 4 + [shape_of((width, half), F32)],
                ins,
                [pltpu.VMEM((width, half), F32)],
                specs=[SM] + [VM] * (len(ins) - 1),
                name="weights",
            )

        def norm_shares(*ins):
            return call(sums_body, [shape_of((8, width), F32)], ins, name="norm_shares")

        def back(*ins):
            return call(
                functools.partial(back_body, n, pad),
                [big_bf] + [shape_of((shard + EXTRA, half), BF)] * 4,
                ins,
                [
                    pltpu.VMEM((128, 128), F32),
                    pltpu.VMEM((128, 128), F32),
                    pltpu.VMEM((width, half), F32),
                    pltpu.VMEM((2, CHUNK, half), F32),
                    pltpu.VMEM((4, EXTRA, half), F32),
                ],
                specs=[SM] + [VM] * (len(ins) - 1),
                name="back",
            )

        def rows_out(*ins):
            shape = (2 * samples, rows, width)
            outs = [shape_of(s, BF) for s in (shape, shape, (4 * samples, rows, width))]
            return call(functools.partial(rows_body, n, pad), outs, ins, name="rows_out")

        def finish_rows(*ins):
            shape = shape_of(tokens.shape, BF)
            return call(
                finish_rows_body, [shape, shape], ins, specs=[SM] + [VM] * 6, name="finish_rows"
            )

        wide_shapes = shape_of((width, 2 * gate), F32), shape_of((gate, width), F32)

        def place(fresh, which_wu, which_v, *ins):
            count = len(which_wu) + len(which_v)
            return call(
                functools.partial(place_body, half, gate, fresh, which_wu, which_v),
                wide_shapes,
                ins,
                [
                    pltpu.VMEM((2 * len(which_wu), shard, half), F32),
                    pltpu.VMEM((2 * len(which_wu), half, shard), F32),
                    pltpu.SemaphoreType.DMA((4 * len(which_wu),)),
                    pltpu.VMEM((max(2 * len(which_v), 1), shard, half), F32),
                    pltpu.SemaphoreType.DMA((max(2 * len(which_v), 1),)),
                ],
                specs=[SM] + [VM] * count + ([] if fresh else [HB] * 2),
                out_specs=[HB] * 2,
                input_output_aliases={} if fresh else {1 + count: 0, 2 + count: 1},
                name="place",
            )

        def place_last(which, *ins):
            one, two = shape_of((width,), F32), shape_of((gate,), F32)
            small = [shape_of((rows, n * rows), F32), shape_of((rows,), F32), one, one, two, two]
            return call(
                functools.partial(place_last_body, half, gate, which),
                [shape_of((width, 2 * gate), F32)] + small,
                ins,
                [
                    pltpu.VMEM((2 * len(which), shard, half), F32),
                    pltpu.VMEM((pad, columns), F32),
                    pltpu.VMEM((4, n, EXTRA - pad // 4, half), F32),
                    *(pltpu.VMEM(s.shape, F32) for s in small),
                    pltpu.SemaphoreType.DMA((2 * len(which),)),
                    pltpu.SemaphoreType.DMA((len(small),)),
                ],
                specs=[SM] + [VM] * 8 + [HB, VM],
                out_specs=[HB] * 7,
                input_output_aliases={9: 0},
                name="place_last",
            )

        def twin(x):
            return over_seq(x, 1)

        x = dict(messages=messages, clock=clock)

        def ev_tick():
            x["clock"] = step(tick, x["clock"])

        def reduce_start(key, shards):
            x[key] = shards[0]
            for rho in range(1, 4):
                x[f"{key}{rho}"] = over_dp(shards[rho], rho)

        def ev_weights():
            *x["a_shards"], x["uw"] = step(weights, meta, prod, gb0, gb1, gb2, ghu, flipped)

        def ev_a_send():
            reduce_start("a", step(None, x["a_shards"]))

        def ev_sums():
            (x["sums"],) = step(norm_shares, wu, x["uw"], ghu)

        def ev_stats():
            x["messages"] = step(None, x["messages"])

        def ev_back():
            x["ghv"], *x["v_shards"] = step(
                back, meta, gmix, v0, v1, v2, dgv0, dgv1, dgv2, cols, st2, edge, *x["messages"], g1, s1,
                g2, flipped, wv, x["sums"],
            )

        def ev_v_send():
            reduce_start("v", step(None, x["v_shards"]))

        def ev_rows():
            x["r_a"], x["r_b"], send = step(rows_out, prod, wo, ghu, x["ghv"], wu, wv)
            x["r_got"] = twin(send)

        def ev_rows_core():
            x["r_last"] = over_seq(step(lambda a, b: add(a, b[2 * samples :]), x["r_b"], x["r_got"]), 2)

        def ev_finish():
            x["output"], x["grad_tokens"] = step(
                finish_rows, meta, t0, c0, x["r_a"], x["r_got"], x["r_last"], g1
            )

        def ev_rs(k):
            x[k] = step(add, x[k], x[k + "1"], x[k + "2"], x[k + "3"])
            x[k + "z"] = over_dp(x[k], 4) if m > 4 else None

        def ev_z2(k):
            flip = 8
            while flip <= m:
                x[k] = step(add, x[k], x[k + "z"])
                if flip < m:
                    x[k + "z"] = over_dp(x[k], flip)
                flip *= 2
            x[k + "z"] = over_dp(x[k], 2)

        def ev_pair(k):
            x[k + "p0"] = step(pair_up, x[k], x[k + "z"])
            x[k + "p1"], x[k + "p2"] = mixed_axes(x[k + "p0"], 0), mixed_axes(x[k + "p0"], 1)

        def ev_mark(k):
            x[k + "p1"], x[k + "p2"] = step(None, (x[k + "p1"], x[k + "p2"]))
            x[k + "p3"] = mixed_axes(x[k + "p1"], 1)

        def ev_third(k):
            x[k + "p3"] = step(None, x[k + "p3"])

        def ev_twin(k, j):
            x[f"{k}q{j}"] = twin(x[f"{k}p{j}"])

        def ev_got(k, j):
            x[f"{k}q{j}"] = step(None, x[f"{k}q{j}"])

        def pieces(k, which):
            return [x[f"{k}{'pq'[j // 4]}{j % 4}"] for j in which]

        def ev_place(fresh, which_wu, which_v):
            ins = [*pieces("a", which_wu), *pieces("v", which_v)]
            ins += [] if fresh else [x["w_in"], x["w_out"]]
            x["w_in"], x["w_out"] = step(
                functools.partial(place, fresh, which_wu, which_v), meta, *ins
            )

        def ev_place_last():
            ins = [x[f"vp{j}"] for j in range(4)] + [x[f"vq{j}"] for j in range(4)]
            x["w_in"], x["spatial"], *x["small"] = step(
                functools.partial(place_last, (3, 7)), meta, *ins, x["w_in"], x["clock"]
            )

        events = dict(
            weights=ev_weights, sums=ev_sums, stats=ev_stats, back=ev_back,
            rows=ev_rows, rows_core=ev_rows_core, finish=ev_finish,
            place_last=ev_place_last,
            place_own=functools.partial(ev_place, True, (0, 4), (0, 4)),
            place_near=functools.partial(ev_place, False, (1, 2, 5, 6), ()),
            place_far=functools.partial(ev_place, False, (3, 7), (1, 2, 5, 6)),
            place_head=functools.partial(ev_place, True, (0, 1, 2, 4, 5, 6), ()),
            place_most=functools.partial(ev_place, False, (3, 7), (0, 1, 2, 4, 5, 6)),
            a_send=ev_a_send, v_send=ev_v_send, tick=ev_tick,
        )
        for k in ("a", "v"):
            for name, f in (("rs", ev_rs), ("z2", ev_z2), ("pair", ev_pair), ("mark", ev_mark), ("third", ev_third)):
                events[f"{k}_{name}"] = functools.partial(f, k)
            for j in range(4):
                events[f"{k}_twin{j}"] = functools.partial(ev_twin, k, j)
                events[f"{k}_got{j}"] = functools.partial(ev_got, k, j)
        for name in ORDER:
            events[name]()
        output, grad_tokens, grad_w_in, grad_w_out = (
            x[k] for k in ("output", "grad_tokens", "w_in", "w_out")
        )
        grad_spatial, sums = x["spatial"], x["small"]
        return (output, grad_tokens, grad_w_in, grad_w_out, grad_spatial, *sums)

    placed = (
        P("dp", "seq", None),
        P("dp"),
        P("dp"),
        P(),
        P(),
        P("seq", None),
        P("seq"),
        P(),
        P(),
        P(),
        P(),
        P("dp", "seq", None),
    )
    return jax.shard_map(
        shards,
        mesh=mesh,
        in_specs=placed,
        out_specs=(
            P("dp", "seq", None),
            P("dp", "seq", None),
            P(),
            P(),
            P("seq", None),
            P("seq"),
            P(),
            P(),
            P(),
            P(),
        ),
        check_vma=False,
    )
```

```python
import functools

import jax
import jax.numpy as jnp
from jax import lax
from jax.experimental import pallas as pl
from jax.experimental.pallas import tpu as pltpu
from jax.sharding import PartitionSpec as P

PATCHES = 324
SMALL_P = 100
MID_P = 196

EPSILON = 1e-05
SURVIVAL = 0.9

BF = jnp.bfloat16
F32 = jnp.float32
CHUNK = 16
VM = pl.BlockSpec(memory_space=pltpu.VMEM)
SM = pl.BlockSpec(memory_space=pltpu.SMEM)
HB = pl.BlockSpec(memory_space=pltpu.HBM)


ORDER = (
    "weights", "a_send", "sums", "tick", "stats", "back", "v_send", "rows", "a_rs", "tick", "tick", "tick",
    "rows_core", "v_rs", "a_z2", "v_z2", "a_pair", "tick", "v_pair", "finish", "a_twin0", "a_mark", "tick", "v_mark",
    "tick", "a_twin1", "a_twin2", "place_head", "a_third", "v_third", "a_twin3", "v_twin3", "v_twin0", "v_twin1",
    "v_twin2", "tick", "place_most", "place_last",
)


def round_up(size, multiple):
    return -(-size // multiple) * multiple


def dot(a, b, ca, cb):
    return lax.dot_general(a, b, (((ca,), (cb,)), ((), ())), preferred_element_type=F32)


def iota(shape, axis):
    return lax.broadcasted_iota(jnp.int32, shape, axis)


def rows_at(start, size, multiple):
    return pl.ds(pl.multiple_of(start, multiple), size)


def call(body, outs, ins, scratch=(), specs=None, out_specs=None, flops=1, **more):
    return pl.pallas_call(
        body,
        out_shape=outs,
        in_specs=specs if specs is not None else [VM] * len(ins),
        out_specs=out_specs if out_specs is not None else [VM] * len(outs),
        scratch_shapes=list(scratch),
        compiler_params=pltpu.CompilerParams(vmem_limit_bytes=20 * 2**20),
        cost_estimate=pl.CostEstimate(flops=flops, bytes_accessed=1, transcendentals=0),
        **more,
    )(*ins)


def shape_of(shape, dtype):
    return jax.ShapeDtypeStruct(shape, dtype)


def add_body(*refs):
    total = refs[0][...].astype(F32)
    for ref in refs[1:-1]:
        total = total + ref[...].astype(F32)
    refs[-1][...] = total.astype(BF)


def tick_body(clock, out):
    out[...] = clock[...] + 1.0


def pair_body(a, b, out):
    out[0] = a[...]
    out[1] = b[...]


def project_body(pad, first_block, *refs):
    refs = list(refs)
    n_tok = len(refs) - 13 - (1 if first_block else 0)
    toks, refs = refs[:n_tok], refs[n_tok:]
    g1, s1, wu, wv = refs[:4]
    refs = refs[4:]
    if first_block:
        st_in, refs = refs[0], refs[1:]
    normed, gu, dgu, v, dgv, st, xs, hid, tile = refs
    samples, rows, width = toks[0].shape
    half = wu.shape[1]
    size = samples * pad
    found = [jnp.zeros((CHUNK, 128), F32)] * (128 // CHUNK)
    low = rows // 8 * 8
    gain, shift = g1[...], s1[...]
    for b, tok in enumerate(toks):
        for i in range(samples):
            base = (b * samples + i) * pad
            xs[base + low : base + pad, :] = jnp.zeros((pad - low, width), F32)
            xs[base : base + rows, :] = tok[i].astype(F32)
            for c in range(base, base + pad, CHUNK):
                x = xs[c : c + CHUNK, :]
                center = x - jnp.mean(x, axis=-1, keepdims=True)
                inverse = lax.rsqrt(jnp.mean(center * center, axis=-1, keepdims=True) + EPSILON)
                normed[c : c + CHUNK, :] = (center * inverse * gain + shift).astype(BF)
        at = slice(b * size, (b + 1) * size)
        hid[at, 0:half] = dot(normed[at, :], wu[...], 1, 0)
        hid[at, half:] = dot(normed[at, :], wv[...], 1, 0)
    c0 = 0.7978845608028654
    c1 = 0.7978845608028654 * 0.044715

    def gelu_pair(h):
        a = (c1 * h) * h
        s = 0.5 + 0.5 * jnp.tanh(h * (c0 + a))
        g = h * s
        return g, s + (2.0 * g) * (1.0 - s) * (c0 + 3.0 * a)

    lane = iota((CHUNK, 128), 1)
    for b in range(len(toks)):
        for i in range(samples):
            base = (b * samples + i) * pad
            blk = 2 * (i * 4 + first_block + b)
            for c in range(pad // CHUNK):
                at = slice(base + c * CHUNK, base + (c + 1) * CHUNK)
                g, d = gelu_pair(hid[at, 0:half])
                gu[at, :] = g.astype(BF)
                dgu[at, :] = d.astype(BF)
                g, d = gelu_pair(hid[at, half:])
                v[at, :] = g
                dgv[at, :] = d.astype(BF)
                mean = jnp.mean(g, axis=-1, keepdims=True)
                center = g - mean
                square = jnp.sum(center * center, axis=-1, keepdims=True)
                found[c] = jnp.where(
                    lane == blk, mean, jnp.where(lane == blk + 1, square, found[c])
                )
    for c, part_found in enumerate(found):
        tile[c * CHUNK : (c + 1) * CHUNK, :] = part_found
    flipped = jnp.transpose(tile[...])[0 : st.shape[0], :]
    st[...] = flipped + st_in[...] if first_block else flipped


def project(pad, first_block, toks, g1, s1, wu, wv, st_in=None):
    samples, rows, width = toks[0].shape
    half = wu.shape[1]
    n_rows = len(toks) * samples * pad
    outs = [
        shape_of((n_rows, width), BF),
        shape_of((n_rows, half), BF),
        shape_of((n_rows, half), BF),
        shape_of((n_rows, half), F32),
        shape_of((n_rows, half), BF),
        shape_of((round_up(samples * 8, 8), 128), F32),
    ]
    scratch = [
        pltpu.VMEM((n_rows, width), F32),
        pltpu.VMEM((n_rows, 2 * half), F32),
        pltpu.VMEM((128, 128), F32),
    ]
    ins = [*toks, g1, s1, wu, wv] + ([st_in] if first_block else [])
    return call(
        functools.partial(project_body, pad, first_block),
        outs,
        ins,
        scratch,
        name="project",
    )


GROUPS = ((0, 1), (2,), (3,))


def part(r, i, samples, pad):
    for k, blocks in enumerate(GROUPS):
        if r in blocks:
            return k, ((r - blocks[0]) * samples + i) * pad


def group_rows(size):
    return [slice(blocks[0] * size, (blocks[-1] + 1) * size) for blocks in GROUPS]


def position_map(seq, rows, pad, n, columns):
    a = iota((columns, n * pad), 0)
    j = iota((columns, n * pad), 1)
    r = jnp.zeros_like(j)
    for k in range(1, n):
        r = r + (j >= k * pad).astype(jnp.int32)
    q = j - r * pad
    hit = (a == (r ^ seq) * rows + q) & (q < rows)
    hit = hit | ((a == n * rows) & (j == pad - 1)) | ((a == n * rows + 1) & (j == pad - 2))
    return jnp.where(hit, 1.0, 0.0).astype(BF)


def patch_count(meta, i):
    kind = meta[2 + i]
    return jnp.where(kind == 0, SMALL_P, jnp.where(kind == 1, MID_P, PATCHES))


def branch_scale(meta, i, samples, where):
    keep = jnp.where(where < patch_count(meta, i), meta[2 + samples + i], 0)
    return keep.astype(F32) / SURVIVAL


def valid_rows(meta, i, r, c, rows):
    p = c * CHUNK + iota((CHUNK, 1), 0)
    return (p < rows) & ((meta[0] ^ r) * rows + p < patch_count(meta, i))


def front_rows(pad, first_block, meta, cots, wo, gu, gb, gp, put):
    width = cots[0].shape[1]
    rows = PATCHES // 4
    samples = cots[0].shape[0] // rows - 1
    low = rows // 16 * 16
    size = samples * pad
    for b, cot in enumerate(cots):
        where = (meta[0] ^ (first_block + b)) * rows + iota((rows, 1), 0)
        for i in range(samples):
            base = b * size + i * pad
            scale = branch_scale(meta, i, samples, where)
            gb[base + low : base + pad, :] = jnp.zeros((pad - low, width), BF)
            gb[base : base + rows, :] = (cot[i * rows : (i + 1) * rows, :].astype(F32) * scale).astype(BF)
        at = slice(b * size, (b + 1) * size)
        gp[at, :] = dot(gb[at, :], wo[...], 1, 1)
        for i in range(samples):
            for c in range(0, pad, CHUNK):
                at = slice(b * size + i * pad + c, b * size + i * pad + c + CHUNK)
                put(b, i, c, (gp[at, :] * gu[at, :].astype(F32)).astype(BF))


def matrix_rows(pad, block, cot, pm, sp):
    rows = PATCHES // 4
    low = rows // 16 * 16
    sp[block * pad + low : (block + 1) * pad, :] = jnp.zeros((pad - low, sp.shape[1]), BF)
    out = dot(cot[cot.shape[0] - rows :, 0 : pm.shape[0]], pm[...], 1, 0)
    sp[block * pad : block * pad + rows, :] = out.astype(BF)


def front_body(n, pad, first_block, count, meta, *refs):
    cots, refs = refs[:count], refs[count:]
    if first_block:
        wo, gu, pm, gb, gp, gs, sp = refs
    else:
        wo, gu, gb, gp, gs, sp, pm = refs
        pm[...] = position_map(meta[0], PATCHES // n, pad, n, pm.shape[0])
    samples = cots[0].shape[0] // (PATCHES // n) - 1

    def put(b, i, c, out):
        base = (b * samples + i) * pad + c
        gs[base : base + CHUNK, :] = out

    front_rows(pad, first_block, meta, cots, wo, gu, gb, gp, put)
    for b, cot in enumerate(cots):
        matrix_rows(pad, b, cot, pm, sp)


def prepare_body(n, pad, meta, c3, wo, gu2, pm, gs0, gs1, sp0, sp1, gb, gp, gs, gmix, sp, spt):
    rows = PATCHES // n
    samples = c3.shape[0] // rows - 1
    most = (n - 1) * pad
    sp[0 : sp0.shape[0], :] = sp0[...]
    sp[sp0.shape[0] : most, :] = sp1[...]
    matrix_rows(pad, n - 1, c3, pm, sp)
    spt[...] = jnp.transpose(sp[...].astype(F32)).astype(BF)

    half = gp.shape[1]

    def put(b, i, c, out):
        gs[most + c : most + c + CHUNK, i * half : (i + 1) * half] = out

    front_rows(pad, n - 1, meta, (c3,), wo, gu2, gb, gp, put)
    for i in range(samples):
        for r in range(n - 1):
            k, base = part(r, i, samples, pad)
            here = slice(i * half, (i + 1) * half)
            gs[r * pad : (r + 1) * pad, here] = (gs0, gs1)[k][base : base + pad, :]
    full = dot(spt[...], gs[...], 1, 0)
    for i in range(samples):
        for r in range(n):
            base = (r * samples + i) * pad
            for c in range(pad // CHUNK):
                at = slice(r * pad + c * CHUNK, r * pad + (c + 1) * CHUNK)
                out = full[at, i * half : (i + 1) * half]
                out = jnp.where(valid_rows(meta, i, r, c, rows), out, 0.0)
                gmix[base + c * CHUNK : base + (c + 1) * CHUNK, :] = out


def own_lanes(rows, seq, half):
    count = half // 128
    return jnp.concatenate([rows[pl.ds(seq * count + k, 1), :] for k in range(count)], axis=1)


def lane_sum(x):
    total = x[:, 0:128]
    for k in range(1, x.shape[1] // 128):
        total = total + x[:, k * 128 : (k + 1) * 128]
    return total


def row_sum(x):
    ones = jnp.ones((8, x.shape[1]), BF)
    high = x.astype(BF)
    low = (x - high.astype(F32)).astype(BF)
    return dot(ones, high, 1, 1) + dot(ones, low, 1, 1)


def row_sums(parts, st, pad):
    blocks = parts.shape[0] // 2
    for b in range(blocks):
        for j in range(2):
            st[2 * b + j : 2 * b + j + 1, 0:pad] = row_sum(parts[j * blocks + b])[0:1, :]


def pack_sums(st):
    x = jnp.concatenate([st[8 * k : 8 * (k + 1), :] for k in range(3)], axis=1)
    terms = []
    for _ in range(3):
        terms.append(x.astype(BF).astype(F32))
        x = x - terms[-1]
    return jnp.concatenate(terms + [jnp.zeros_like(x)], axis=0).astype(BF)


def unpack_sums(packed):
    x = packed.astype(F32)
    x = (x[16:24] + x[8:16]) + x[0:8]
    return jnp.concatenate([x[:, 128 * k : 128 * (k + 1)] for k in range(3)], axis=0)


def spatial_body(
    n, pad, meta, v0, v1, v2, gu0, gu1, gu2, dgu0, dgu1, dgu2, sp, gp0, gp1, gp2, gs, pm, gmix, g2, s2, t0, t1, t2, t3,
    prod, ghu, cols, st, edge, m1, m2, m3,
    mixed, so, tile, parts,
):
    half, rows = gp0.shape[1], PATCHES // n
    samples = gs.shape[1] // half
    gps = (gp0, gp1, gp2)
    whole = half * n
    stats, vs, gus, dgus = (t0, t1, t2, t3), (v0, v1, v2), (gu0, gu1, gu2), (dgu0, dgu1, dgu2)
    tile[...] = jnp.zeros_like(tile)
    for i in range(samples):
        for r in range(n):
            at = [2 * (i * n + (r ^ k)) for k in range(n)]
            means = [stats[k][at[k] : at[k] + 1, :] for k in range(n)]
            squares = [stats[k][at[k] + 1 : at[k] + 2, :] for k in range(n)]
            mean = ((means[0] + means[1]) + (means[2] + means[3])) / n
            spread = (squares[0] + squares[1]) + (squares[2] + squares[3])
            for k in range(n):
                spread = spread + half * (means[k] - mean) * (means[k] - mean)
            blk = 2 * (i * n + r)
            tile[blk : blk + 1, :] = mean
            tile[blk + 1 : blk + 2, :] = lax.rsqrt(spread / whole + EPSILON)
    cols[...] = jnp.transpose(tile[...])
    gain, shift = own_lanes(g2, meta[0], half), own_lanes(s2, meta[0], half)
    for i in range(samples):
        for r in range(n):
            k, base = part(r, i, samples, pad)
            first = (r * samples + i) * pad
            blk = 2 * (i * n + r)
            for c in range(pad // CHUNK):
                here = slice(c * CHUNK, (c + 1) * CHUNK)
                mean, inverse = cols[here, blk : blk + 1], cols[here, blk + 1 : blk + 2]
                standard = (vs[k][base + c * CHUNK : base + (c + 1) * CHUNK, :] - mean) * inverse
                out = jnp.where(valid_rows(meta, i, r, c, rows), standard * gain + shift, 0.0)
                if r == 0 and (c + 1) * CHUNK == pad:
                    p = c * CHUNK + iota((CHUNK, 1), 0)
                    out = jnp.where(p >= pad - 2, 1.0, out)
                at = slice(r * pad + c * CHUNK, r * pad + (c + 1) * CHUNK)
                mixed[at, i * half : (i + 1) * half] = out.astype(BF)
                t = gmix[first + c * CHUNK : first + (c + 1) * CHUNK, :] * gain
                parts[i * n + r, here, :] = lane_sum(t)
                parts[samples * n + i * n + r, here, :] = lane_sum(t * standard)
    so[...] = dot(sp[...], mixed[...], 1, 0)
    row_sums(parts, st, pad)
    total = dot(gs[...], mixed[...], 1, 1)
    placed = dot(total.astype(BF), pm[...], 1, 1).astype(BF)
    packed = pack_sums(st)
    edge[...] = placed[0:pad, :]
    for r, message in enumerate((m1, m2, m3), 1):
        message[0:pad, :] = placed[r * pad : (r + 1) * pad, :]
        message[pad:, :] = packed
    for i in range(samples):
        for r in range(n):
            k, base = part(r, i, samples, pad)
            first = (r * samples + i) * pad
            for c in range(0, pad, CHUNK):
                src = slice(base + c, base + c + CHUNK)
                at = slice(first + c, first + c + CHUNK)
                s = so[r * pad + c : r * pad + c + CHUNK, i * half : (i + 1) * half]
                prod[at, :] = (gus[k][src, :].astype(F32) * s).astype(BF)
                ghu[at, :] = (gps[k][src, :] * s * dgus[k][src, :].astype(F32)).astype(BF)


def weight_sum(lefts, rights):
    total = None
    for left, right in zip(lefts, rights):
        term = dot(left, right, 0, 0)
        total = term if total is None else total + term
    return total


def store_shards(dp, whole, outs, base):
    shard = whole.shape[0] // 4
    for rho, out in enumerate(outs):
        here = whole[rows_at(((dp ^ rho) & 3) * shard, shard, 16), :]
        out[base : base + shard, :] = here.astype(BF)


def norm_sums(w, grad_w, grads):
    columns = None
    for c in range(0, grads.shape[0], CHUNK):
        g = grads[c : c + CHUNK, :].astype(F32)
        columns = g if columns is None else columns + g
    columns = jnp.sum(columns, axis=0, keepdims=True)
    first, second = [], []
    for c in range(w.shape[0] // CHUNK):
        at = slice(c * CHUNK, (c + 1) * CHUNK)
        x = w[at, :].astype(F32)
        first.append(lane_sum(x * grad_w[at, :]))
        second.append(lane_sum(x * columns))
    first = row_sum(jnp.concatenate(first, axis=0))
    second = row_sum(jnp.concatenate(second, axis=0))
    return jnp.where(iota(first.shape, 0) == 0, first, second)


def flip_body(n0, n1, n2, out, whole):
    base = 0
    for ref in (n0, n1, n2):
        whole[base : base + ref.shape[0], :] = ref[...]
        base += ref.shape[0]
    out[...] = jnp.transpose(whole[...])


def weights_body(meta, prod, gb0, gb1, gb2, ghu, flipped, s0, s1, s2, s3, uw, ow):
    groups = group_rows(prod.shape[0] // 4)
    outs = (s0, s1, s2, s3)
    ow[...] = weight_sum([g[...] for g in (gb0, gb1, gb2)], [prod[at, :] for at in groups])
    uw[...] = dot(flipped[...], ghu[...], 1, 0)
    store_shards(meta[1], ow, outs, 0)
    store_shards(meta[1], uw, outs, ow.shape[0] // 4)


def sums_body(w, grad_w, grads, out):
    out[...] = norm_sums(w, grad_w, grads)


EXTRA = 32


def back_body(
    n, pad, meta, gmix, v0, v1, v2, dgv0, dgv1, dgv2, cols, st, edge0, m1, m2, m3, g1, s1, g2, flipped,
    wv, first_sums,
    ghv, w0, w1, w2, w3,
    tile, col, vw, acc, extra,
):
    samples, half = gmix.shape[0] // (n * pad), gmix.shape[1]
    width = wv.shape[0]
    messages, vs, dgvs = (m1, m2, m3), (v0, v1, v2), (dgv0, dgv1, dgv2)
    stats = [st[...]] + [unpack_sums(m[pad:, :]) for m in messages]
    tile[...] = jnp.zeros_like(tile)
    for i in range(samples):
        for r in range(n):
            blk = 2 * (i * n + r)
            terms = [
                stats[k][2 * (i * n + (r ^ k)) : 2 * (i * n + (r ^ k)) + 2, :] for k in range(n)
            ]
            tile[blk : blk + 2, :] = ((terms[0] + terms[1]) + (terms[2] + terms[3])) / (half * n)
    col[...] = jnp.transpose(tile[...])
    gain = own_lanes(g2, meta[0], half)
    acc[...] = jnp.zeros_like(acc)
    for i in range(samples):
        for r in range(n):
            k, base = part(r, i, samples, pad)
            row = (r * samples + i) * pad
            blk = 2 * (i * n + r)
            for c in range(pad // CHUNK):
                here = slice(c * CHUNK, (c + 1) * CHUNK)
                at = slice(row + c * CHUNK, row + (c + 1) * CHUNK)
                src = slice(base + c * CHUNK, base + (c + 1) * CHUNK)
                mean, inverse = cols[here, blk : blk + 1], cols[here, blk + 1 : blk + 2]
                first, second = col[here, blk : blk + 1], col[here, blk + 1 : blk + 2]
                standard = (vs[k][src, :] - mean) * inverse
                g = gmix[at, :]
                out = inverse * (g * gain - first - standard * second)
                ghv[at, :] = (out * dgvs[k][src, :].astype(F32)).astype(BF)
                acc[0] += g * standard
                acc[1] += g
    vw[...] = dot(flipped[...], ghv[...], 1, 0)
    sums = first_sums[...] + norm_sums(wv, vw, ghv)
    shift_one = sums[1:2, :]
    gain_one = (sums[0:1, :] - s1[...] * shift_one) / g1[...]
    edge = edge0[...].astype(F32)
    for m in messages:
        edge = edge + m[0:pad, :].astype(F32)
    size = pad // 4
    extra[...] = jnp.zeros_like(extra)
    for k in range(4):
        extra[k, 0:size, :] = edge[k * size : (k + 1) * size, :]
    extra[0, size : size + 1, :] = jnp.sum(acc[0], axis=0, keepdims=True)
    extra[1, size : size + 1, :] = jnp.sum(acc[1], axis=0, keepdims=True)
    for k, row in ((2, gain_one), (3, shift_one)):
        extra[k, size : size + 1, :] = row[:, 0:half]
        extra[k, size + 1 : size + 2, 0 : width - half] = row[:, half:]
    outs = (w0, w1, w2, w3)
    store_shards(meta[1], vw, outs, 0)
    shard = vw.shape[0] // 4
    for rho, out in enumerate(outs):
        out[shard:, :] = extra[(meta[1] ^ rho) & 3].astype(BF)


def rows_body(n, pad, prod, wo, ghu, ghv, wu, wv, keep_a, keep_b, send):
    samples, rows = keep_a.shape[0] // 2, keep_a.shape[1]
    places = ((keep_a, 0), (send, 0), (keep_b, 0), (send, 2 * samples))
    for r, (out, first) in enumerate(places):
        at = slice(r * samples * pad, (r + 1) * samples * pad)
        branch = dot(prod[at, :], wo[...], 1, 0)
        grad = dot(ghu[at, :], wu[...], 1, 1) + dot(ghv[at, :], wv[...], 1, 1)
        for i in range(samples):
            out[first + i] = branch[i * pad : i * pad + rows, :].astype(BF)
            out[first + samples + i] = grad[i * pad : i * pad + rows, :].astype(BF)


def finish_rows_body(meta, tok, cot, keep, got_a, got_b, g1, output, grad_tokens):
    samples, rows = tok.shape[0], tok.shape[1]
    gain = g1[...]
    p = meta[0] * rows + iota((rows, 1), 0)
    for i in range(samples):
        x = tok[i].astype(F32)
        total = keep[i].astype(F32) + got_a[i].astype(F32) + got_b[i].astype(F32)
        output[i] = (x + branch_scale(meta, i, samples, p) * total).astype(BF)
        center = x - jnp.mean(x, axis=-1, keepdims=True)
        inverse = lax.rsqrt(jnp.mean(center * center, axis=-1, keepdims=True) + EPSILON)
        standard = center * inverse
        k = samples + i
        t = (keep[k].astype(F32) + got_a[k].astype(F32) + got_b[k].astype(F32)) * gain
        first = jnp.mean(t, axis=-1, keepdims=True)
        second = jnp.mean(t * standard, axis=-1, keepdims=True)
        grad = cot[i * rows : (i + 1) * rows, :].astype(F32) + inverse * (t - first - standard * second)
        grad_tokens[i] = grad.astype(BF)


def sources(meta):
    seq, shard = meta[0], meta[1] & 3
    out = []
    for flip in (0, 1):
        s = seq ^ flip
        core = s & 1
        out += [
            (shard, s),
            (shard ^ (1 - core), s ^ (2 * core)),
            (shard ^ core, s ^ (2 * (1 - core))),
            (shard ^ 1, s ^ 2),
        ]
    return out


def place_wu(half, meta, pieces, which, w_in, w_out, wide, tall, sems):
    shard = wide.shape[1]
    copies = []
    origins = sources(meta)
    for piece, k in zip(pieces, which):
        group, seq = origins[k]
        for e in range(2):
            slot = len(copies) // 2
            row = (group ^ (2 * e)) * shard
            columns = rows_at(seq * half, half, 128)
            tall[slot] = jnp.transpose(piece[e, 0:shard, :].astype(F32))
            target = w_out.at[columns, rows_at(row, shard, 128)]
            copies.append(pltpu.make_async_copy(tall.at[slot], target, sems.at[2 * slot]))
            copies[-1].start()
            wide[slot] = piece[e, shard:, :].astype(F32)
            target = w_in.at[rows_at(row, shard, 16), columns]
            copies.append(pltpu.make_async_copy(wide.at[slot], target, sems.at[2 * slot + 1]))
            copies[-1].start()
    return copies


def place_v(half, gate, meta, pieces, which, w_in, wide, sems):
    shard = wide.shape[1]
    copies = []
    origins = sources(meta)
    for piece, k in zip(pieces, which):
        group, seq = origins[k]
        for e in range(2):
            slot = len(copies)
            wide[slot] = piece[e, 0:shard, :].astype(F32)
            columns = rows_at(gate + seq * half, half, 128)
            target = w_in.at[rows_at((group ^ (2 * e)) * shard, shard, 16), columns]
            copies.append(pltpu.make_async_copy(wide.at[slot], target, sems.at[slot]))
            copies[-1].start()
    return copies


def place_body(half, gate, fresh, which_wu, which_v, meta, *refs):
    *pieces, w_in, w_out, wide, tall, sems, more, more_sems = refs
    if not fresh:
        pieces = pieces[:-2]
    count = len(which_wu)
    copies = place_wu(half, meta, pieces[:count], which_wu, w_in, w_out, wide, tall, sems)
    copies += place_v(half, gate, meta, pieces[count:], which_v, w_in, more, more_sems)
    for copy in copies:
        copy.wait()


def place_last_body(half, gate, which, meta, *refs):
    pieces = refs[:8]
    w_in, *targets, wide, edge, norms = refs[10:20]
    spatial, bias, gain_one, shift_one, gain_two, shift_two, sems, small_sems = refs[20:]
    shard = wide.shape[1]
    rows, patches = spatial.shape
    size = edge.shape[0] // 4
    core = meta[0] & 1
    copies = place_v(half, gate, meta, [pieces[k] for k in which], which, w_in, wide, sems)
    small = []
    for k, (group, seq) in enumerate(sources(meta)):
        for e in range(2):
            at = group ^ (2 * e)
            rest = pieces[k][e, shard:, :].astype(F32)
            small.append((at, rest[0:size]))
            norms[at, seq] = rest[size:]
    for e in range(2):
        at, own = small[e]
        edge[rows_at(at * size, size, 8), :] = own
        at = (meta[1] & 3) ^ 1 ^ (2 * e)
        edge[rows_at(at * size, size, 8), :] = jnp.where(core == 0, small[2 + e][1], small[4 + e][1])
    spatial[...] = edge[0:rows, 0:patches]
    first = patches // 128 * 128
    tail = edge[0:rows, first:]
    column = jnp.sum(
        jnp.where(iota(tail.shape, 1) == patches - first, tail, 0.0), axis=1, keepdims=True
    )
    diagonal = iota((rows, rows), 0) == iota((rows, rows), 1)
    bias[...] = jnp.sum(jnp.where(diagonal, column, 0.0), axis=0)
    for at, out in ((2, gain_one), (3, shift_one)):
        total = (norms[at, 0] + norms[at, 1]) + (norms[at, 2] + norms[at, 3])
        out[0:half] = total[0, :]
        out[half:] = total[1, 0 : out.shape[0] - half]
    for at, out in ((0, gain_two), (1, shift_two)):
        for j in range(4):
            out[j * half : (j + 1) * half] = norms[at, j, 0, :]
    smalls = (spatial, bias, gain_one, shift_one, gain_two, shift_two)
    for k, (source, target) in enumerate(zip(smalls, targets)):
        copies.append(pltpu.make_async_copy(source, target, small_sems.at[k]))
        copies[-1].start()
    for copy in copies:
        copy.wait()


def solution(mesh):
    n, m = mesh.shape["seq"], mesh.shape["dp"]

    def over_seq(x, flip):
        return lax.ppermute(x, "seq", [(i, i ^ flip) for i in range(n)])

    def over_dp(x, flip):
        return lax.ppermute(x, "dp", [(i, i ^ flip) for i in range(m)])

    def mixed_axes(x, core_of_x):
        pairs = []
        for d in range(m):
            for s in range(n):
                other = (d ^ 1, s) if s & 1 == core_of_x else (d, s ^ 2)
                pairs.append((d * n + s, other[0] * n + other[1]))
        return lax.ppermute(x, ("dp", "seq"), pairs)

    def add(*terms):
        total = terms[0].astype(F32)
        for t in terms[1:]:
            total = total + t.astype(F32)
        return total.astype(BF)

    def pair_up(*terms):
        return jnp.stack(terms)

    def ordered():
        last = []

        def step(body, *ins):
            if last:
                ins, _ = lax.optimization_barrier((ins, last[0]))
            out = body(*ins) if body else ins[0]
            last[:] = [jax.tree.leaves(out)[0]]
            return out

        return step

    def shards(
        tokens,
        res_class,
        skip_mask,
        w_in,
        w_out,
        spatial,
        spatial_bias,
        gain_one,
        shift_one,
        gain_two,
        shift_two,
        cotangent,
    ):
        samples, rows, width = tokens.shape
        gate = w_out.shape[0]
        half = gate // n
        pad = round_up(rows + 2, 16)
        full = n * pad
        columns = round_up(n * rows + 2, 128)
        seq, dp = lax.axis_index("seq"), lax.axis_index("dp")
        meta = jnp.concatenate([seq[None], dp[None], res_class, skip_mask]).astype(jnp.int32)
        step = ordered()
        clock = jnp.zeros((8, 128), F32)

        def tick(clock):
            return call(tick_body, [shape_of(clock.shape, F32)], [clock], flops=4 * 10**9, name="tick")[0]

        big_bf, big_f32 = (shape_of((samples * full, half), d) for d in (BF, F32))
        images = shape_of((full, samples * half), BF)
        shard = width // 4
        square = shape_of((round_up(samples * 2 * n, 8), 128), F32)

        t0 = tokens
        t2 = over_seq(t0, 2)
        t1 = over_seq(t0, 1)
        high = lax.reduce_precision(spatial_bias, 8, 7)
        side = jnp.stack([high, spatial_bias - high], axis=1).astype(BF)
        packed = jnp.concatenate([spatial, side], axis=1)
        packed = jnp.pad(packed, ((0, 0), (0, width - packed.shape[1])))
        c0 = jnp.concatenate([cotangent.reshape(-1, width), packed])
        c2 = over_seq(c0, 2)
        wu = lax.dynamic_slice(w_in, (0, seq * half), (width, half))
        wv = lax.dynamic_slice(w_in, (0, gate + seq * half), (width, half))
        wo = lax.dynamic_slice(w_out, (seq * half, 0), (half, width))
        g1, s1 = gain_one[None], shift_one[None]
        g2, s2 = gain_two.reshape(-1, 128), shift_two.reshape(-1, 128)
        meta, wu, wv, wo, c0, t1 = lax.optimization_barrier((meta, wu, wv, wo, c0, t1))
        c1 = over_seq(c0, 1)

        n0, gu0, dgu0, v0, dgv0, st = step(
            lambda *a: project(pad, 0, a[:2], *a[2:]), t0, t1, g1, s1, wu, wv
        )
        t2 = step(None, t2)
        t3 = over_seq(t2, 1)
        n1, gu1, dgu1, v1, dgv1, st = step(
            lambda *a: project(pad, 2, a[:1], *a[1:]), t2, g1, s1, wu, wv, st
        )
        n2, gu2, dgu2, v2, dgv2, st = step(
            lambda *a: project(pad, 3, a[:1], *a[1:]), t3, g1, s1, wu, wv, st
        )
        normed = [n0, n1, n2]
        stats = [st] + [over_seq(st, k) for k in range(1, n)]

        def front(first_block, count, *ins):
            def shape(columns, dtype):
                return shape_of((count * samples * pad, columns), dtype)

            outs = [shape(width, BF), shape(half, F32), shape(half, BF)]
            outs.append(shape_of((count * pad, full), BF))
            return call(
                functools.partial(front_body, n, pad, first_block, count),
                outs + ([] if first_block else [shape_of((columns, full), BF)]),
                ins,
                specs=[SM] + [VM] * (len(ins) - 1),
                name="front",
            )

        gb0, gp0, gs0, sp0, pm = step(functools.partial(front, 0, 2), meta, c0, c1, wo, gu0)

        def flip(*ins):
            return call(
                flip_body,
                [shape_of((width, samples * full), BF)],
                ins,
                [pltpu.VMEM((samples * full, width), BF)],
                name="flip",
            )

        (flipped,) = step(flip, *normed)
        c2 = step(None, c2)
        c3 = over_seq(c2, 1)
        gb1, gp1, gs1, sp1 = step(functools.partial(front, 2, 1), meta, c2, wo, gu1, pm)

        def prepare(*ins):
            square_bf = shape_of((full, full), BF)
            last = [shape_of((samples * pad, c), d) for c, d in ((width, BF), (half, F32))]
            return call(
                functools.partial(prepare_body, n, pad),
                [*last, images, big_f32, square_bf],
                ins,
                [pltpu.VMEM((full, full), BF)],
                specs=[SM] + [VM] * (len(ins) - 1),
                name="prepare",
            )

        clock = step(tick, clock)
        gb2, gp2, gs, gmix, sp = step(prepare, meta, c3, wo, gu2, pm, gs0, gs1, sp0, sp1)

        def spatial_unit(*ins):
            message = shape_of((pad + 32, columns), BF)
            return call(
                functools.partial(spatial_body, n, pad),
                [big_bf, big_bf, shape_of((128, 128), F32), square, shape_of((pad, columns), BF)]
                + [message] * (n - 1),
                ins,
                [
                    pltpu.VMEM((full, samples * half), BF),
                    pltpu.VMEM((full, samples * half), F32),
                    pltpu.VMEM((128, 128), F32),
                    pltpu.VMEM((2 * samples * n, pad, 128), F32),
                ],
                specs=[SM] + [VM] * (len(ins) - 1),
                name="spatial",
            )

        prod, ghu, cols, st2, edge, *messages = step(
            spatial_unit, meta, v0, v1, v2, gu0, gu1, gu2, dgu0, dgu1, dgu2, sp, gp0, gp1, gp2, gs, pm,
            gmix, g2, s2, *stats,
        )
        messages = [over_seq(x, k) for k, x in enumerate(messages, 1)]

        def weights(*ins):
            return call(
                weights_body,
                [shape_of((2 * shard, half), BF)] * 4 + [shape_of((width, half), F32)],
                ins,
                [pltpu.VMEM((width, half), F32)],
                specs=[SM] + [VM] * (len(ins) - 1),
                name="weights",
            )

        def norm_shares(*ins):
            return call(sums_body, [shape_of((8, width), F32)], ins, name="norm_shares")

        def back(*ins):
            return call(
                functools.partial(back_body, n, pad),
                [big_bf] + [shape_of((shard + EXTRA, half), BF)] * 4,
                ins,
                [
                    pltpu.VMEM((128, 128), F32),
                    pltpu.VMEM((128, 128), F32),
                    pltpu.VMEM((width, half), F32),
                    pltpu.VMEM((2, CHUNK, half), F32),
                    pltpu.VMEM((4, EXTRA, half), F32),
                ],
                specs=[SM] + [VM] * (len(ins) - 1),
                name="back",
            )

        def rows_out(*ins):
            shape = (2 * samples, rows, width)
            outs = [shape_of(s, BF) for s in (shape, shape, (4 * samples, rows, width))]
            return call(functools.partial(rows_body, n, pad), outs, ins, name="rows_out")

        def finish_rows(*ins):
            shape = shape_of(tokens.shape, BF)
            return call(
                finish_rows_body, [shape, shape], ins, specs=[SM] + [VM] * 6, name="finish_rows"
            )

        wide_shapes = shape_of((width, 2 * gate), F32), shape_of((gate, width), F32)

        def place(fresh, which_wu, which_v, *ins):
            count = len(which_wu) + len(which_v)
            return call(
                functools.partial(place_body, half, gate, fresh, which_wu, which_v),
                wide_shapes,
                ins,
                [
                    pltpu.VMEM((2 * len(which_wu), shard, half), F32),
                    pltpu.VMEM((2 * len(which_wu), half, shard), F32),
                    pltpu.SemaphoreType.DMA((4 * len(which_wu),)),
                    pltpu.VMEM((max(2 * len(which_v), 1), shard, half), F32),
                    pltpu.SemaphoreType.DMA((max(2 * len(which_v), 1),)),
                ],
                specs=[SM] + [VM] * count + ([] if fresh else [HB] * 2),
                out_specs=[HB] * 2,
                input_output_aliases={} if fresh else {1 + count: 0, 2 + count: 1},
                name="place",
            )

        def place_last(which, *ins):
            one, two = shape_of((width,), F32), shape_of((gate,), F32)
            small = [shape_of((rows, n * rows), F32), shape_of((rows,), F32), one, one, two, two]
            return call(
                functools.partial(place_last_body, half, gate, which),
                [shape_of((width, 2 * gate), F32)] + small,
                ins,
                [
                    pltpu.VMEM((2 * len(which), shard, half), F32),
                    pltpu.VMEM((pad, columns), F32),
                    pltpu.VMEM((4, n, EXTRA - pad // 4, half), F32),
                    *(pltpu.VMEM(s.shape, F32) for s in small),
                    pltpu.SemaphoreType.DMA((2 * len(which),)),
                    pltpu.SemaphoreType.DMA((len(small),)),
                ],
                specs=[SM] + [VM] * 8 + [HB, VM],
                out_specs=[HB] * 7,
                input_output_aliases={9: 0},
                name="place_last",
            )

        def twin(x):
            return over_seq(x, 1)

        x = dict(messages=messages, clock=clock)

        def ev_tick():
            x["clock"] = step(tick, x["clock"])

        def reduce_start(key, shards):
            x[key] = shards[0]
            for rho in range(1, 4):
                x[f"{key}{rho}"] = over_dp(shards[rho], rho)

        def ev_weights():
            *x["a_shards"], x["uw"] = step(weights, meta, prod, gb0, gb1, gb2, ghu, flipped)

        def ev_a_send():
            reduce_start("a", step(None, x["a_shards"]))

        def ev_sums():
            (x["sums"],) = step(norm_shares, wu, x["uw"], ghu)

        def ev_stats():
            x["messages"] = step(None, x["messages"])

        def ev_back():
            x["ghv"], *x["v_shards"] = step(
                back, meta, gmix, v0, v1, v2, dgv0, dgv1, dgv2, cols, st2, edge, *x["messages"], g1, s1,
                g2, flipped, wv, x["sums"],
            )

        def ev_v_send():
            reduce_start("v", step(None, x["v_shards"]))

        def ev_rows():
            x["r_a"], x["r_b"], send = step(rows_out, prod, wo, ghu, x["ghv"], wu, wv)
            x["r_got"] = twin(send)

        def ev_rows_core():
            x["r_last"] = over_seq(step(lambda a, b: add(a, b[2 * samples :]), x["r_b"], x["r_got"]), 2)

        def ev_finish():
            x["output"], x["grad_tokens"] = step(
                finish_rows, meta, t0, c0, x["r_a"], x["r_got"], x["r_last"], g1
            )

        def ev_rs(k):
            x[k] = step(add, x[k], x[k + "1"], x[k + "2"], x[k + "3"])
            x[k + "z"] = over_dp(x[k], 4) if m > 4 else None

        def ev_z2(k):
            flip = 8
            while flip <= m:
                x[k] = step(add, x[k], x[k + "z"])
                if flip < m:
                    x[k + "z"] = over_dp(x[k], flip)
                flip *= 2
            x[k + "z"] = over_dp(x[k], 2)

        def ev_pair(k):
            x[k + "p0"] = step(pair_up, x[k], x[k + "z"])
            x[k + "p1"], x[k + "p2"] = mixed_axes(x[k + "p0"], 0), mixed_axes(x[k + "p0"], 1)

        def ev_mark(k):
            x[k + "p1"], x[k + "p2"] = step(None, (x[k + "p1"], x[k + "p2"]))
            x[k + "p3"] = mixed_axes(x[k + "p1"], 1)

        def ev_third(k):
            x[k + "p3"] = step(None, x[k + "p3"])

        def ev_twin(k, j):
            x[f"{k}q{j}"] = twin(x[f"{k}p{j}"])

        def ev_got(k, j):
            x[f"{k}q{j}"] = step(None, x[f"{k}q{j}"])

        def pieces(k, which):
            return [x[f"{k}{'pq'[j // 4]}{j % 4}"] for j in which]

        def ev_place(fresh, which_wu, which_v):
            ins = [*pieces("a", which_wu), *pieces("v", which_v)]
            ins += [] if fresh else [x["w_in"], x["w_out"]]
            x["w_in"], x["w_out"] = step(
                functools.partial(place, fresh, which_wu, which_v), meta, *ins
            )

        def ev_place_last():
            ins = [x[f"vp{j}"] for j in range(4)] + [x[f"vq{j}"] for j in range(4)]
            x["w_in"], x["spatial"], *x["small"] = step(
                functools.partial(place_last, (3, 7)), meta, *ins, x["w_in"], x["clock"]
            )

        events = dict(
            weights=ev_weights, sums=ev_sums, stats=ev_stats, back=ev_back,
            rows=ev_rows, rows_core=ev_rows_core, finish=ev_finish,
            place_last=ev_place_last,
            place_own=functools.partial(ev_place, True, (0, 4), (0, 4)),
            place_near=functools.partial(ev_place, False, (1, 2, 5, 6), ()),
            place_far=functools.partial(ev_place, False, (3, 7), (1, 2, 5, 6)),
            place_head=functools.partial(ev_place, True, (0, 1, 2, 4, 5, 6), ()),
            place_most=functools.partial(ev_place, False, (3, 7), (0, 1, 2, 4, 5, 6)),
            a_send=ev_a_send, v_send=ev_v_send, tick=ev_tick,
        )
        for k in ("a", "v"):
            for name, f in (("rs", ev_rs), ("z2", ev_z2), ("pair", ev_pair), ("mark", ev_mark), ("third", ev_third)):
                events[f"{k}_{name}"] = functools.partial(f, k)
            for j in range(4):
                events[f"{k}_twin{j}"] = functools.partial(ev_twin, k, j)
                events[f"{k}_got{j}"] = functools.partial(ev_got, k, j)
        for name in ORDER:
            events[name]()
        output, grad_tokens, grad_w_in, grad_w_out = (
            x[k] for k in ("output", "grad_tokens", "w_in", "w_out")
        )
        grad_spatial, sums = x["spatial"], x["small"]
        return (output, grad_tokens, grad_w_in, grad_w_out, grad_spatial, *sums)

    placed = (
        P("dp", "seq", None),
        P("dp"),
        P("dp"),
        P(),
        P(),
        P("seq", None),
        P("seq"),
        P(),
        P(),
        P(),
        P(),
        P("dp", "seq", None),
    )
    return jax.shard_map(
        shards,
        mesh=mesh,
        in_specs=placed,
        out_specs=(
            P("dp", "seq", None),
            P("dp", "seq", None),
            P(),
            P(),
            P("seq", None),
            P("seq"),
            P(),
            P(),
            P(),
            P(),
        ),
        check_vma=False,
    )
```
